32 devices in a mesh: section: 2 (over x), ctx: 8 (over z, y), tp: 2 (over core).
Axes of the slice: x: 2, y: 2, z: 4, core: 2. Of those that a mesh axis runs over, the one named last changes fastest.
Arguments:
- tokens: bfloat16 [4, 2048, 1024], P(None, 'ctx'), may hold values from -6 to 6
- cotangent: bfloat16 [4, 2048, 1024], P(None, 'ctx'), may hold values from -6 to 6
- block_order: int32 [16], replicated, may hold values from 0 to 15, each once
- first_gain: float32 [2, 1024], P('section'), may hold values from 0.25 to 1.75
- first_bias: float32 [2, 1024], P('section'), may hold values from -1.75 to 1.75
- second_gain: float32 [2, 1024], P('section'), may hold values from 0.25 to 1.75
- second_bias: float32 [2, 1024], P('section'), may hold values from -1.75 to 1.75
- joint_weight: bfloat16 [2, 3, 1024, 1024], P('section', None, None, 'tp'), may hold values from -0.25 to 0.25
- joint_bias: float32 [2, 3, 1024], P('section', None, 'tp'), may hold values from -1.75 to 1.75
- output_weight: bfloat16 [2, 1024, 1024], P('section', 'tp'), may hold values from -0.5 to 0.5
- output_bias: float32 [2, 1024], P('section'), may hold values from -1.75 to 1.75
- up_weight: bfloat16 [2, 1024, 4096], P('section', None, 'tp'), may hold values from -0.1875 to 0.1875
- up_bias: float32 [2, 4096], P('section', 'tp'), may hold values from -1.75 to 1.75
- down_weight: bfloat16 [2, 4096, 1024], P('section', 'tp'), may hold values from -0.125 to 0.125
- down_bias: float32 [2, 1024], P('section'), may hold values from -1.75 to 1.75
Outputs:
- section_out: bfloat16 [2, 4, 2048, 1024], P('section', None, 'ctx')
- section_in_grad: bfloat16 [2, 4, 2048, 1024], P('section', None, 'ctx')
- first_gain_gradient: float32 [2, 1024], P('section')
- first_bias_gradient: float32 [2, 1024], P('section')
- second_gain_gradient: float32 [2, 1024], P('section')
- second_bias_gradient: float32 [2, 1024], P('section')
- joint_weight_gradient: float32 [2, 3, 1024, 1024], P('section', None, 'ctx', 'tp')
- joint_bias_gradient: float32 [2, 3, 1024], P('section', None, 'tp')
- output_weight_gradient: float32 [2, 1024, 1024], P('section', 'tp', 'ctx')
- output_bias_gradient: float32 [2, 1024], P('section')
- up_weight_gradient: float32 [2, 1024, 4096], P('section', 'ctx', 'tp')
- up_bias_gradient: float32 [2, 4096], P('section', 'tp')
- down_weight_gradient: float32 [2, 4096, 1024], P('section', 'tp', 'ctx')
- down_bias_gradient: float32 [2, 1024], P('section')
- root_means: float32 [2, 3], P('section')
The draws below stay inside these ranges and needn't reach their ends.
Inputs may be any that keep to these rules, and one draw needn't show every extreme that they name: `block_order`: each stored block's place in its sequence, every place once; the same for all sequences.
All inputs are finite; a program needn't handle non-finite values.
Results may differ from the reference program's by a relative error of at most 0.028.
Values may be sent and summed in bfloat16 or wider, within the bound.
A program may use at most 256 MiB of HBM per device.

```python
import jax
import jax.numpy as jnp
from jax import lax

D = 1024
HEADS = 16
HEAD = 64
ROT = 16
FF = 4096
LEN = 2048
SEQS = 4
BLOCK = 128


def level_of(key, dims, split, low, high):
    def one(dim, shards_of):
        heights = jax.random.uniform(jax.random.fold_in(jax.random.fold_in(key, 6), dim), (shards_of,), jnp.float32, low / len(split), high / len(split))
        return jnp.repeat(jnp.exp(heights), dims[dim] // shards_of).reshape((-1,) + (1,) * (len(dims) - dim - 1))

    level = one(*split[0])
    for cut in split[1:]:
        level = level * one(*cut)
    return level


def gaussian(own_key, extent, width, limit, shards=(), kind=jnp.bfloat16):
    entries = width * jax.random.normal(own_key, extent, jnp.float32)
    if shards:
        entries = entries * level_of(own_key, extent, shards, -0.22, 0.18)
    return jnp.clip(entries, -limit, limit).astype(kind)


def setup_inputs(seed: int = 0) -> dict:
    splits = jax.random.split(jax.random.key(seed), 16)
    tokens = gaussian(splits[0], (SEQS, LEN, D), 1.0, 6.0, ((1, 8),))
    cotangent = gaussian(splits[1], (SEQS, LEN, D), 1.0, 6.0, ((1, 8),))
    block_order = jax.random.permutation(splits[2], LEN // BLOCK).astype(jnp.int32)
    first_gain = jnp.clip(1.0 + 0.15 * jax.random.normal(splits[3], (2, D), jnp.float32), 0.25, 1.75)
    first_bias = gaussian(splits[4], (2, D), 0.3, 1.75, ((0, 2),), jnp.float32)
    second_gain = jnp.clip(1.0 + 0.15 * jax.random.normal(splits[5], (2, D), jnp.float32), 0.25, 1.75)
    second_bias = gaussian(splits[6], (2, D), 0.3, 1.75, ((0, 2),), jnp.float32)
    joint_weight = gaussian(splits[7], (2, 3, D, D), (D // 2) ** -0.5, 0.25, ((0, 2), (3, 2)))
    joint_bias = gaussian(splits[8], (2, 3, D), 0.3, 1.75, ((0, 2), (2, 2)), jnp.float32)
    output_weight = gaussian(splits[9], (2, D, D), (D // 8) ** -0.5, 0.5, ((0, 2), (1, 2)))
    output_bias = gaussian(splits[10], (2, D), 0.3, 1.75, ((0, 2),), jnp.float32)
    up_weight = gaussian(splits[11], (2, D, FF), D ** -0.5, 0.1875, ((0, 2), (2, 2)))
    up_bias = gaussian(splits[12], (2, FF), 0.3, 1.75, ((0, 2), (1, 2)), jnp.float32)
    down_weight = gaussian(splits[13], (2, FF, D), (FF // 2) ** -0.5, 0.125, ((0, 2), (1, 2)))
    down_bias = gaussian(splits[14], (2, D), 0.3, 1.75, ((0, 2),), jnp.float32)
    return dict(tokens=tokens, cotangent=cotangent, block_order=block_order, first_gain=first_gain, first_bias=first_bias, second_gain=second_gain, second_bias=second_bias, joint_weight=joint_weight, joint_bias=joint_bias, output_weight=output_weight, output_bias=output_bias, up_weight=up_weight, up_bias=up_bias, down_weight=down_weight, down_bias=down_bias)


@jax.custom_vjp
def low(v):
    return lax.optimization_barrier(v.astype(jnp.bfloat16)).astype(jnp.float32)

@jax.custom_vjp
def low_back(v):
    return v

def low_keep(v):
    return (low(v), None)

def low_pass(kept, grad):
    return (grad,)

def back_keep(v):
    return (v, None)

def back_low(kept, grad):
    return (low(grad),)
low.defvjp(low_keep, low_pass)
low_back.defvjp(back_keep, back_low)
HIGHEST = lax.Precision.HIGHEST
EPS = 1e-05
ROTARY_BASE = 10000.0
NEGATIVE = -1e+30

def layer_norm(values, gain, shift):
    middle = lax.optimization_barrier(jnp.mean(values, axis=-1, keepdims=True))
    centered = values - middle
    spread = lax.optimization_barrier(jnp.mean(centered * centered, axis=-1, keepdims=True))
    return centered * lax.rsqrt(spread + EPS) * gain + shift

def rotate(values, cosine, sine):
    half = cosine.shape[-1]
    first = values[..., :half]
    second = values[..., half:2 * half]
    return jnp.concatenate([first * cosine - second * sine, second * cosine + first * sine, values[..., 2 * half:]], axis=-1)

def angle_table(block_order):
    offsets = jnp.arange(BLOCK, dtype=jnp.int32)
    places = (block_order.astype(jnp.int32)[:, None] * BLOCK + offsets[None, :]).reshape(-1)
    exponent = jnp.arange(ROT // 2, dtype=jnp.float32) * (2.0 / ROT)
    inverse = jnp.power(jnp.float32(ROTARY_BASE), -exponent)
    turns = places.astype(jnp.float32)[:, None] * inverse[None, :]
    return (places, jnp.cos(turns)[:, None, :], jnp.sin(turns)[:, None, :])

def attend_core(queries, key_rows, value_rows, allowed):
    scores = low_back(jnp.einsum('qhc,khc->hqk', queries, key_rows, precision=HIGHEST) * HEAD ** (-0.5))
    scores = jnp.where(allowed[None], scores, NEGATIVE)
    row_top = lax.optimization_barrier(jnp.max(scores, axis=-1, keepdims=True))
    raised = jnp.exp(scores - row_top)
    soft = low(raised / lax.optimization_barrier(jnp.sum(raised, axis=-1, keepdims=True)))
    return low_back(low(jnp.einsum('hqk,khc->qhc', soft, value_rows, precision=HIGHEST)))

def residual_layer(state, weights, cosine, sine, allowed):
    gain_one, bias_one, gain_two, bias_two, w_joint, b_joint, w_output, b_output, w_up, b_up, w_down, b_down = weights
    first_in = low(layer_norm(state, gain_one, bias_one))
    second_in = low(layer_norm(state, gain_two, bias_two))
    joined = low_back(jnp.einsum('ld,tde->tle', first_in, w_joint, precision=HIGHEST) + b_joint[:, None, :])
    joined = joined.reshape(3, LEN, HEADS, HEAD)
    queries = low(rotate(joined[0], cosine, sine))
    key_rows = low(rotate(joined[1], cosine, sine))
    value_rows = low(joined[2])
    mixture = jax.checkpoint(attend_core)(queries, key_rows, value_rows, allowed)
    attention = jnp.dot(mixture.reshape(LEN, D), w_output, precision=HIGHEST) + b_output
    hidden = low_back(jnp.dot(second_in, w_up, precision=HIGHEST) + b_up)
    active = low(jax.nn.gelu(hidden, approximate=False))
    feedforward = jnp.dot(active, w_down, precision=HIGHEST) + b_down
    return (state + attention + feedforward, (attention, feedforward))

def reference(tokens, cotangent, block_order, first_gain, first_bias, second_gain, second_bias, joint_weight, joint_bias, output_weight, output_bias, up_weight, up_bias, down_weight, down_bias):
    places, cosine, sine = angle_table(block_order)
    allowed = places[None, :] <= places[:, None]
    params = tuple((p.astype(jnp.float32) for p in (first_gain, first_bias, second_gain, second_bias, joint_weight, joint_bias, output_weight, output_bias, up_weight, up_bias, down_weight, down_bias)))
    section_zero = tuple((p[0] for p in params))
    section_one = tuple((p[1] for p in params))

    def section_fn(state, weights):
        return residual_layer(state, weights, cosine, sine, allowed)

    def squares(values):
        return jnp.sum(values * values)

    def run(carry, item):
        totals, moments = carry
        source, upstream = item
        state_zero = source.astype(jnp.float32)
        out_zero, pull_zero, aux_zero = jax.vjp(section_fn, state_zero, section_zero, has_aux=True)
        state_one = low(out_zero)
        out_one, pull_one, aux_one = jax.vjp(section_fn, state_one, section_one, has_aux=True)
        back_one, weights_one = pull_one(upstream.astype(jnp.float32))
        sent = low(back_one)
        back_zero, weights_zero = pull_zero(sent)
        totals = jax.tree.map(jnp.add, totals, (weights_zero, weights_one))
        fresh = jnp.stack([squares(state_zero), squares(aux_zero[0]), squares(aux_zero[1]), squares(state_one), squares(aux_one[0]), squares(aux_one[1])])
        outputs = (out_zero.astype(jnp.bfloat16), out_one.astype(jnp.bfloat16), back_zero.astype(jnp.bfloat16), sent.astype(jnp.bfloat16))
        return ((totals, moments + fresh), outputs)
    start = (jax.tree.map(jnp.zeros_like, (section_zero, section_one)), jnp.zeros((6,), jnp.float32))
    (totals, moments), outputs = lax.scan(run, start, (tokens, cotangent))
    section_out = jnp.stack([outputs[0], outputs[1]])
    section_in_grad = jnp.stack([outputs[2], outputs[3]])
    gradients = tuple((jnp.stack([totals[0][i], totals[1][i]]) for i in range(12)))
    root_means = jnp.sqrt(moments.reshape(2, 3) / (SEQS * LEN * D))
    return (section_out, section_in_grad) + gradients + (root_means,)
```

```python
import functools

import jax
import jax.numpy as jnp
from jax import lax
from jax.experimental import pallas as pl
from jax.experimental.pallas import tpu as pltpu
from jax.sharding import PartitionSpec as P

HEAD = 64
ROT = 16
EPS = 1e-05
ROTARY_BASE = 10000.0
NEGATIVE = -1e30
STACK = 4
GROUP = STACK * HEAD
KEY_TILE = 512
VMEM_LIMIT = 56 * 1024 * 1024
BF16 = jnp.bfloat16
F32 = jnp.float32


def dot(a, b):
    return jnp.dot(a, b, preferred_element_type=F32)


def dot_nt(a, b):
    return lax.dot_general(a, b, (((1,), (1,)), ((), ())), preferred_element_type=F32)


def params_of(**more):
    return pltpu.CompilerParams(vmem_limit_bytes=VMEM_LIMIT, **more)


def whole(shape):
    return pl.BlockSpec(shape, lambda *_: (0,) * len(shape))


def rows_of(tile, *rest):
    return pl.BlockSpec((tile, *rest), lambda r, *_: (r,) + (0,) * len(rest))


def cost(flops, size):
    return pl.CostEstimate(flops=int(flops), bytes_accessed=int(size), transcendentals=0)


def normalize(values):
    middle = jnp.mean(values, axis=-1, keepdims=True)
    centered = values - middle
    spread = jnp.mean(centered * centered, axis=-1, keepdims=True)
    inverse = lax.rsqrt(spread + EPS)
    return centered * inverse, inverse


def turn(values, cosine, sine_up, sine_down):
    pieces = []
    for start in range(0, values.shape[1], 128):
        part = values[:, start : start + 128]
        ahead = pltpu.roll(part, 128 - ROT // 2, 1)
        behind = pltpu.roll(part, ROT // 2, 1)
        pieces.append(part * cosine + ahead * sine_up + behind * sine_down)
    return jnp.concatenate(pieces, axis=1)


def joint_kernel(with_queries, h_ref, gain_ref, shift_ref, w_ref, b_ref, cos_ref, up_ref, down_ref, n_ref, k_ref, v_ref, *maybe_q):
    scaled, _ = normalize(h_ref[...].astype(F32))
    low = (scaled * gain_ref[...] + shift_ref[...]).astype(BF16)
    n_ref[...] = low
    cosine, sine_up, sine_down = cos_ref[...], up_ref[...], down_ref[...]
    keys = dot(low, w_ref[1]) + b_ref[1:2]
    k_ref[...] = turn(keys, cosine, sine_up, sine_down).astype(BF16)
    v_ref[...] = (dot(low, w_ref[2]) + b_ref[2:3]).astype(BF16)
    if with_queries:
        queries = dot(low, w_ref[0]) + b_ref[0:1]
        queries = turn(queries, cosine, sine_up, sine_down)
        maybe_q[0][...] = queries.astype(BF16) * jnp.asarray(HEAD ** (-0.5), BF16)


def joint_call(h, gain, shift, w_joint, b_joint, table, with_queries):
    rows, width = h.shape
    local = w_joint.shape[2]
    tile = min(256, rows)
    count = 3 if with_queries else 2
    out = [jax.ShapeDtypeStruct((rows, width), BF16)] + [jax.ShapeDtypeStruct((rows, local), BF16)] * count
    return pl.pallas_call(
        functools.partial(joint_kernel, with_queries),
        grid=(rows // tile,),
        in_specs=[
            rows_of(tile, width),
            whole((1, width)),
            whole((1, width)),
            whole(w_joint.shape),
            whole(b_joint.shape),
            rows_of(tile, 128),
            rows_of(tile, 128),
            rows_of(tile, 128),
        ],
        out_specs=[rows_of(tile, width)] + [rows_of(tile, local)] * count,
        out_shape=out,
        compiler_params=params_of(),
        cost_estimate=cost(2 * rows * width * local * count, 4 * rows * width + 2 * w_joint.size),
        name="joint_projection",
    )(h, gain, shift, w_joint, b_joint, *table)


def gelu_parts(x):
    size = jnp.abs(x)
    t = 1.0 / (1.0 + (0.3275911 * 0.5**0.5) * size)
    bell = jnp.exp(-0.5 * x * x)
    poly = t * (0.5 * 0.254829592 + t * (-0.5 * 0.284496736 + t * (0.5 * 1.421413741 + t * (-0.5 * 1.453152027 + t * (0.5 * 1.061405429)))))
    tail = poly * bell
    return jnp.where(x < 0, tail, 1.0 - tail), bell


def ffn_kernel(save, h_ref, gain_ref, shift_ref, up_ref, b_ref, down_ref, part_ref, *saved):
    scaled, _ = normalize(h_ref[...].astype(F32))
    low = (scaled * gain_ref[...] + shift_ref[...]).astype(BF16)
    if save:
        saved[0][...] = low
    units = up_ref.shape[1]
    total = None
    for start in range(0, units, 512):
        cut = pl.ds(start, 512)
        hidden = dot(low, up_ref[:, cut]) + b_ref[:, cut]
        share, bell = gelu_parts(hidden)
        active = (hidden * share).astype(BF16)
        if save:
            saved[1][:, cut] = active
            saved[2][:, cut] = (share + hidden * bell * 0.3989422804014327).astype(BF16)
        term = dot(active, down_ref[cut, :])
        total = term if total is None else total + term
    part_ref[...] = total.astype(BF16)


def ffn_call(h, gain, shift, w_up, b_up, w_down, save):
    rows, width = h.shape
    units = w_up.shape[1]
    tile = min(256, rows)
    out = [jax.ShapeDtypeStruct((rows, width), BF16)]
    out_specs = [rows_of(tile, width)]
    if save:
        out += [jax.ShapeDtypeStruct((rows, width), BF16)] + [jax.ShapeDtypeStruct((rows, units), BF16)] * 2
        out_specs += [rows_of(tile, width), rows_of(tile, units), rows_of(tile, units)]
    return pl.pallas_call(
        functools.partial(ffn_kernel, save),
        grid=(rows // tile,),
        in_specs=[
            rows_of(tile, width),
            whole((1, width)),
            whole((1, width)),
            whole(w_up.shape),
            whole((1, units)),
            whole(w_down.shape),
        ],
        out_specs=out_specs,
        out_shape=out,
        compiler_params=params_of(),
        cost_estimate=cost(4 * rows * width * units, 4 * w_up.size + 4 * rows * width),
        name="feed_forward",
    )(h, gain, shift, w_up, b_up, w_down)


def ffn_back_kernel(g_ref, slope_ref, up_ref, down_ref, part_ref, hidden_ref, sums_ref):
    upstream = g_ref[...]
    units = up_ref.shape[1]

    @pl.when(pl.program_id(0) == 0)
    def _():
        sums_ref[...] = jnp.zeros_like(sums_ref)

    total = None
    for start in range(0, units, 512):
        cut = pl.ds(start, 512)
        d_active = dot_nt(upstream, down_ref[cut, :])
        d_hidden = (d_active * slope_ref[:, cut].astype(F32)).astype(BF16)
        hidden_ref[:, cut] = d_hidden
        sums_ref[:, cut] += jnp.sum(d_hidden.astype(F32), axis=0, keepdims=True)
        term = dot_nt(d_hidden, up_ref[:, cut])
        total = term if total is None else total + term
    part_ref[...] = total.astype(BF16)


def ffn_back_call(g, slope, w_up, w_down):
    rows, width = g.shape
    units = w_up.shape[1]
    tile = min(256, rows)
    return pl.pallas_call(
        ffn_back_kernel,
        grid=(rows // tile,),
        in_specs=[rows_of(tile, width), rows_of(tile, units), whole(w_up.shape), whole(w_down.shape)],
        out_specs=[rows_of(tile, width), rows_of(tile, units), whole((1, units))],
        out_shape=[
            jax.ShapeDtypeStruct((rows, width), BF16),
            jax.ShapeDtypeStruct((rows, units), BF16),
            jax.ShapeDtypeStruct((1, units), F32),
        ],
        compiler_params=params_of(),
        cost_estimate=cost(4 * rows * width * units, 4 * w_up.size + 4 * rows * (width + units)),
        name="feed_forward_back",
    )(g, slope, w_up, w_down)


def load_sorted(places_ref, parts, targets, sem, block):
    copies = []
    for refs, target in zip(parts, targets):
        index = 0
        for ref in refs:
            for local in range(ref.shape[0] // block):
                place = places_ref[index]
                copies.append(
                    pltpu.make_async_copy(
                        ref.at[pl.ds(local * block, block)],
                        target.at[pl.ds(pl.multiple_of(place * block, block), block)],
                        sem,
                    )
                )
                index += 1
    for copy in copies:
        copy.start()
    for copy in copies:
        copy.wait()


def transpose_into(source, target):
    rows, columns = source.shape

    def step(index, _):
        start = pl.multiple_of(index * 256, 256)
        for column in range(0, columns, 256):
            target[column : column + 256, pl.ds(start, 256)] = source[pl.ds(start, 256), column : column + 256].T
        return 0

    lax.fori_loop(0, rows // 256, step, 0)


def stacked(values):
    owner = lax.broadcasted_iota(jnp.int32, values.shape, 1) // HEAD
    zero = jnp.zeros_like(values)
    return jnp.concatenate([jnp.where(owner == a, values, zero) for a in range(STACK)], axis=0)


def unstacked(total, tile):
    picked = [total[a * HEAD : (a + 1) * HEAD, a * tile : (a + 1) * tile] for a in range(STACK)]
    return jnp.concatenate(picked, axis=0).T


def attend_kernel(
    block, remote, places_ref, limits_ref, q_ref, spots_ref, wo_ref, *refs
):
    key_refs, value_refs = refs[: 1 + remote], refs[1 + remote : 2 + 2 * remote]
    part_ref, mix_ref, lse_ref, keys, values, values_t, total, sem = refs[2 + 2 * remote :]
    step = pl.program_id(0)
    tile = q_ref.shape[0]
    groups = q_ref.shape[1] // GROUP

    @pl.when(step == 0)
    def _():
        load_sorted(places_ref, (key_refs, value_refs), (keys, values), sem, block)
        transpose_into(values, values_t)

    spots = spots_ref[0]
    lanes = [slice(g * GROUP, (g + 1) * GROUP) for g in range(groups)]
    heads = [stacked(q_ref[:, lane]) for lane in lanes]
    total[...] = jnp.zeros_like(total)

    def tile_step(masked, index, carry):
        start = pl.multiple_of(index * KEY_TILE, KEY_TILE)
        fresh = []
        for g, lane in enumerate(lanes):
            top, mass = carry[g]
            scores = dot_nt(keys[pl.ds(start, KEY_TILE), lane], heads[g])
            if masked:
                spot = start + lax.broadcasted_iota(jnp.int32, scores.shape, 0)
                scores = jnp.where(spot <= spots, scores, NEGATIVE)
            later = jnp.maximum(top, jnp.max(scores, axis=0, keepdims=True))
            shrink = jnp.exp(top - later)
            raised = jnp.exp(scores - later)
            mass = mass * shrink + jnp.sum(raised, axis=0, keepdims=True)
            total[lane, :] = total[lane, :] * shrink + dot(
                values_t[lane, pl.ds(start, KEY_TILE)], raised.astype(BF16)
            )
            fresh.append((later, mass))
        return tuple(fresh)

    first = jnp.full((1, STACK * tile), NEGATIVE, F32)
    carry = tuple((first, jnp.zeros_like(first)) for _ in lanes)
    carry = lax.fori_loop(0, limits_ref[step, 0], functools.partial(tile_step, False), carry)
    carry = lax.fori_loop(limits_ref[step, 0], limits_ref[step, 1], functools.partial(tile_step, True), carry)
    pieces = []
    for g, lane in enumerate(lanes):
        top, mass = carry[g]
        lse_ref[0, g : g + 1, :] = top + jnp.log(mass)
        pieces.append(unstacked(total[lane, :] * (1.0 / mass), tile))
    mixture = jnp.concatenate(pieces, axis=1).astype(BF16)
    mix_ref[...] = mixture
    part_ref[...] = dot(mixture, wo_ref[...]).astype(BF16)


def attend_call(queries, key_parts, value_parts, spots, places, limits, w_output, block):
    rows, local = queries.shape
    width = w_output.shape[1]
    tile = rows // limits.shape[0]
    length = sum(part.shape[0] for part in key_parts)
    groups = local // GROUP
    anywhere = pl.BlockSpec(memory_space=pl.ANY)
    return pl.pallas_call(
        functools.partial(attend_kernel, block, len(key_parts) - 1),
        grid_spec=pltpu.PrefetchScalarGridSpec(
            num_scalar_prefetch=2,
            grid=(rows // tile,),
            in_specs=[
                rows_of(tile, local),
                rows_of(1, 1, STACK * tile),
                whole(w_output.shape),
            ]
            + [anywhere] * (2 * len(key_parts)),
            out_specs=[rows_of(tile, width), rows_of(tile, local), rows_of(1, groups, STACK * tile)],
            scratch_shapes=[
                pltpu.VMEM((length, local), BF16),
                pltpu.VMEM((length, local), BF16),
                pltpu.VMEM((local, length), BF16),
                pltpu.VMEM((local, STACK * tile), F32),
                pltpu.SemaphoreType.DMA,
            ],
        ),
        out_shape=[
            jax.ShapeDtypeStruct((rows, width), BF16),
            jax.ShapeDtypeStruct((rows, local), BF16),
            jax.ShapeDtypeStruct((rows // tile, groups, STACK * tile), F32),
        ],
        compiler_params=params_of(),
        cost_estimate=cost(12 * rows * length * local, 2 * length * local * 4),
        name="attend",
    )(places, limits, queries, spots, w_output, *key_parts, *value_parts)


def attend_back_kernel(
    block, remote, places_ref, limits_ref, q_ref, g_ref, mix_ref, lse_ref, spots_ref, wo_ref,
    cos_ref, up_ref, down_ref, cos_all, up_all, down_all, *refs
):
    key_refs, value_refs = refs[: 1 + remote], refs[1 + remote : 2 + 2 * remote]
    dq_ref, dk_ref, dv_ref, sums_ref, keys, values, keys_t, d_keys, d_values, total, sem = refs[2 + 2 * remote :]
    step = pl.program_id(0)
    tile = q_ref.shape[0]
    groups = q_ref.shape[1] // GROUP

    @pl.when(step == 0)
    def _():
        load_sorted(places_ref, (key_refs, value_refs), (keys, values), sem, block)
        transpose_into(keys, keys_t)
        d_keys[...] = jnp.zeros_like(d_keys)
        d_values[...] = jnp.zeros_like(d_values)
        sums_ref[...] = jnp.zeros_like(sums_ref)

    spots = spots_ref[0]
    lanes = [slice(g * GROUP, (g + 1) * GROUP) for g in range(groups)]
    d_mixture = dot_nt(g_ref[...], wo_ref[...]).astype(BF16)
    product = d_mixture.astype(F32) * mix_ref[...].astype(F32)
    high = product.astype(BF16)
    rest = (product - high.astype(F32)).astype(BF16)
    picker = jnp.where(
        lax.broadcasted_iota(jnp.int32, (8, GROUP), 0) == lax.broadcasted_iota(jnp.int32, (8, GROUP), 1) // HEAD, 1.0, 0.0
    ).astype(BF16)
    heads, sides, inner, lse = [], [], [], []
    for g, lane in enumerate(lanes):
        heads.append(stacked(q_ref[:, lane]))
        sides.append(stacked(d_mixture[:, lane]))
        sums = dot_nt(picker, high[:, lane]) + dot_nt(picker, rest[:, lane])
        inner.append(jnp.concatenate([sums[a : a + 1] for a in range(STACK)], axis=1))
        lse.append(lse_ref[0, g : g + 1, :])
    total[...] = jnp.zeros_like(total)

    def tile_step(masked, index, carry):
        start = pl.multiple_of(index * KEY_TILE, KEY_TILE)
        cut = pl.ds(start, KEY_TILE)
        for g, lane in enumerate(lanes):
            scores = dot_nt(keys[cut, lane], heads[g])
            if masked:
                spot = start + lax.broadcasted_iota(jnp.int32, scores.shape, 0)
                scores = jnp.where(spot <= spots, scores, NEGATIVE)
            weights = jnp.exp(scores - lse[g])
            d_weights = dot_nt(values[cut, lane], sides[g])
            d_scores = (weights * (d_weights - inner[g])).astype(BF16)
            d_values[cut, lane] += dot(weights.astype(BF16), sides[g])
            d_keys[cut, lane] += dot(d_scores, heads[g])
            total[lane, :] += dot(keys_t[lane, cut], d_scores)
        return carry

    lax.fori_loop(0, limits_ref[step, 0], functools.partial(tile_step, False), 0)
    lax.fori_loop(limits_ref[step, 0], limits_ref[step, 1], functools.partial(tile_step, True), 0)
    pieces = [unstacked(total[lane, :], tile) for lane in lanes]
    d_queries = jnp.concatenate(pieces, axis=1) * HEAD ** (-0.5)
    d_queries = turn(d_queries, cos_ref[...], -up_ref[...], -down_ref[...]).astype(BF16)
    dq_ref[...] = d_queries
    sums_ref[0:1, :] += jnp.sum(d_queries.astype(F32), axis=0, keepdims=True)

    @pl.when(step == pl.num_programs(0) - 1)
    def _():
        for index in range(dk_ref.shape[0] // block):
            place = pl.ds(pl.multiple_of(places_ref[index] * block, block), block)
            rows = pl.ds(index * block, block)
            turned = turn(d_keys[place, :], cos_all[rows, :], -up_all[rows, :], -down_all[rows, :]).astype(BF16)
            dk_ref[rows, :] = turned
            low = d_values[place, :].astype(BF16)
            dv_ref[rows, :] = low
            sums_ref[1:2, :] += jnp.sum(turned.astype(F32), axis=0, keepdims=True)
            sums_ref[2:3, :] += jnp.sum(low.astype(F32), axis=0, keepdims=True)


def attend_back_call(queries, g, mixture, lse, key_parts, value_parts, spots, places, limits, w_output, table, block):
    rows, local = queries.shape
    width = w_output.shape[1]
    tile = rows // limits.shape[0]
    length = sum(part.shape[0] for part in key_parts)
    groups = local // GROUP
    anywhere = pl.BlockSpec(memory_space=pl.ANY)
    return pl.pallas_call(
        functools.partial(attend_back_kernel, block, len(key_parts) - 1),
        grid_spec=pltpu.PrefetchScalarGridSpec(
            num_scalar_prefetch=2,
            grid=(rows // tile,),
            in_specs=[
                rows_of(tile, local),
                rows_of(tile, width),
                rows_of(tile, local),
                rows_of(1, groups, STACK * tile),
                rows_of(1, 1, STACK * tile),
                whole(w_output.shape),
            ]
            + [rows_of(tile, 128)] * 3
            + [whole((length, 128))] * 3
            + [anywhere] * (2 * len(key_parts)),
            out_specs=[rows_of(tile, local), whole((length, local)), whole((length, local)), whole((8, local))],
            scratch_shapes=[
                pltpu.VMEM((length, local), BF16),
                pltpu.VMEM((length, local), BF16),
                pltpu.VMEM((local, length), BF16),
                pltpu.VMEM((length, local), F32),
                pltpu.VMEM((length, local), F32),
                pltpu.VMEM((local, STACK * tile), F32),
                pltpu.SemaphoreType.DMA,
            ],
        ),
        out_shape=[
            jax.ShapeDtypeStruct((rows, local), BF16),
            jax.ShapeDtypeStruct((length, local), BF16),
            jax.ShapeDtypeStruct((length, local), BF16),
            jax.ShapeDtypeStruct((8, local), F32),
        ],
        compiler_params=params_of(),
        cost_estimate=cost(24 * rows * length * local, 2 * length * local * 8),
        name="attend_back",
    )(
        places, limits, queries, g, mixture, lse, spots, w_output,
        *(part[:rows] for part in table), *table, *key_parts, *value_parts,
    )


def joint_back_kernel(count, *refs):
    w_ref, part_ref = refs[count], refs[count + 1]
    total = None
    for index in range(count):
        term = dot_nt(refs[index][...], w_ref[3 - count + index])
        total = term if total is None else total + term
    part_ref[...] = total.astype(BF16)


def joint_back_call(grads, offset, rows, w_joint):
    width, local = w_joint.shape[1:]
    tile = min(256, rows)
    first = offset // tile
    return pl.pallas_call(
        functools.partial(joint_back_kernel, len(grads)),
        grid=(rows // tile,),
        in_specs=[pl.BlockSpec((tile, local), lambda r: (first + r, 0))] * len(grads) + [whole(w_joint.shape)],
        out_specs=rows_of(tile, width),
        out_shape=jax.ShapeDtypeStruct((rows, width), BF16),
        compiler_params=params_of(),
        cost_estimate=cost(2 * rows * width * local * len(grads), 2 * rows * (width + 3 * local) + 2 * w_joint.size),
        name="joint_projection_back",
    )(*grads, w_joint)


def norm_back_kernel(h_ref, g_ref, first_ref, second_ref, gains_ref, out_ref, sums_ref):
    @pl.when(pl.program_id(0) == 0)
    def _():
        sums_ref[...] = jnp.zeros_like(sums_ref)

    scaled, inverse = normalize(h_ref[...].astype(F32))
    upstream = g_ref[...].astype(F32)
    d_first = first_ref[0].astype(F32)
    for index in range(1, first_ref.shape[0]):
        d_first += first_ref[index].astype(F32)
    d_second = second_ref[0].astype(F32) + second_ref[1].astype(F32)
    for row, term in enumerate((d_first * scaled, d_first, d_second * scaled, d_second, upstream)):
        sums_ref[row : row + 1, :] += jnp.sum(term, axis=0, keepdims=True)
    d_scaled = d_first * gains_ref[0:1] + d_second * gains_ref[1:2]
    middle = jnp.mean(d_scaled, axis=-1, keepdims=True)
    along = jnp.mean(d_scaled * scaled, axis=-1, keepdims=True)
    out_ref[...] = (upstream + inverse * (d_scaled - middle - scaled * along)).astype(BF16)


def norm_back_call(h, g, firsts, seconds, gains):
    rows, width = h.shape
    tile = min(128, rows)

    def piled(count):
        return pl.BlockSpec((count, tile, width), lambda r: (0, r, 0))

    return pl.pallas_call(
        norm_back_kernel,
        grid=(rows // tile,),
        in_specs=[rows_of(tile, width), rows_of(tile, width), piled(firsts.shape[0]), piled(2), whole(gains.shape)],
        out_specs=[rows_of(tile, width), whole((8, width))],
        out_shape=[jax.ShapeDtypeStruct((rows, width), BF16), jax.ShapeDtypeStruct((8, width), F32)],
        compiler_params=params_of(),
        cost_estimate=cost(20 * rows * width, 2 * rows * width * 8),
        name="norm_back",
    )(h, g, firsts, seconds, gains)


def swap_core(shard):
    return lax.ppermute(shard, "tp", [(0, 1), (1, 0)])


def swap_ctx(shard, mask):
    return lax.ppermute(shard, "ctx", [(c, c ^ mask) for c in range(lax.axis_size("ctx"))])


def next_section(shard, by):
    size = lax.axis_size("section")
    return lax.ppermute(shard, "section", [(s, s + by) for s in range(size) if 0 <= s + by < size])


def reduce_ctx(pieces, masks):
    for mask in masks:
        half = pieces.shape[0] // 2
        arrived = swap_ctx(pieces[half:], mask)
        total = pieces[:half].astype(F32) + arrived.astype(F32)
        pieces = total.astype(BF16)
    return total[0]


def mask_order(masks):
    order = [0]
    for mask in reversed(masks):
        order = order + [value ^ mask for value in order]
    return order


def by_owner(values, masks, rank):
    share = values.shape[1] // (1 << len(masks))
    parts = [lax.dynamic_slice_in_dim(values, (rank ^ m) * share, share, 1) for m in mask_order(masks)]
    return jnp.concatenate(parts, axis=1)


def tn(a, b):
    return lax.dot_general(a, b, (((0,), (0,)), ((), ())), preferred_element_type=F32)


def on_device(
    tokens,
    cotangent,
    block_order,
    first_gain,
    first_bias,
    second_gain,
    second_bias,
    joint_weight,
    joint_bias,
    output_weight,
    output_bias,
    up_weight,
    up_bias,
    down_weight,
    down_bias,
):
    section = lax.axis_index("section")
    sections = lax.axis_size("section")
    ctx = lax.axis_index("ctx")
    ctx_size = lax.axis_size("ctx")
    core = lax.axis_index("tp")
    seqs, local_len, width = tokens.shape
    block = local_len // 2
    chips = ctx_size // seqs
    seq, member = ctx // chips, ctx % chips
    rows = seqs * block
    chip_rows = 2 * rows
    length = chips * chip_rows
    seq_masks = [chips << b for b in range((seqs - 1).bit_length())]
    member_masks = [1 << b for b in range((chips - 1).bit_length())]

    k, u, a = jnp.meshgrid(jnp.arange(chips), jnp.arange(2), jnp.arange(seqs), indexing="ij")
    stored = (2 * ((seq ^ a) * chips + (member ^ k)) + (core ^ u)).reshape(-1)
    places = block_order[stored]
    spots = (places[:, None] * block + jnp.arange(block, dtype=jnp.int32)).reshape(-1)
    exponent = jnp.arange(ROT // 2, dtype=F32) * (2.0 / ROT)
    inverse = jnp.power(jnp.float32(ROTARY_BASE), -exponent)
    turns = spots.astype(F32)[:, None] * inverse[None, :]
    cosine, sine = jnp.cos(turns), jnp.sin(turns)
    half = ROT // 2
    blank = jnp.zeros((length, HEAD - ROT), F32)
    none = jnp.zeros((length, half), F32)
    table = (
        jnp.tile(jnp.concatenate([cosine, cosine, blank + 1.0], 1), (1, 128 // HEAD)),
        jnp.tile(jnp.concatenate([-sine, none, blank], 1), (1, 128 // HEAD)),
        jnp.tile(jnp.concatenate([none, sine, blank], 1), (1, 128 // HEAD)),
    )
    near = tuple(part[:chip_rows] for part in table)
    far = tuple(part[chip_rows:] for part in table)

    tile = max(block, 128)
    per_tile = tile // block
    tile_places = places[: chip_rows // block].reshape(-1, per_tile)
    lowest, highest = jnp.min(tile_places, 1), jnp.max(tile_places, 1)
    limits = jnp.stack([(lowest * block + 1) // KEY_TILE, (highest * block + block - 1) // KEY_TILE + 1], 1)
    spot_rows = jnp.tile(spots[:chip_rows].reshape(-1, 1, tile), (1, 1, STACK))

    gain_one, shift_one, gain_two, shift_two = first_gain, first_bias, second_gain, second_bias
    w_joint, b_joint = joint_weight[0], joint_bias[0]
    w_output, b_output = output_weight[0], output_bias
    w_up, b_up = up_weight[0], up_bias
    w_down, b_down = down_weight[0], down_bias
    gains = jnp.concatenate([gain_one, gain_two], 0)

    def to_planes(values):
        mine = lax.dynamic_slice_in_dim(values, core * block, block, 1)
        parts = []
        for shift in range(seqs):
            part = lax.dynamic_index_in_dim(mine, seq ^ shift, 0, keepdims=False)
            parts.append(part if shift == 0 else swap_ctx(part, shift * chips))
        return jnp.concatenate(parts, axis=0)

    def from_planes(values):
        parts = values.reshape(seqs, block, width)
        parts = jnp.stack([parts[s] if s == 0 else swap_ctx(parts[s], s * chips) for s in range(seqs)])
        both = jnp.stack([parts, swap_core(parts)], 1)
        ordered = [
            lax.dynamic_index_in_dim(lax.dynamic_index_in_dim(both, s ^ seq, 0, False), v ^ core, 0, False)
            for s in range(seqs)
            for v in range(2)
        ]
        return jnp.stack(ordered).reshape(1, seqs, local_len, width)

    def forward(own, save):
        others = [swap_ctx(own, k) for k in range(1, chips)]
        chip = jnp.concatenate([own, swap_core(own)], 0)
        outs = joint_call(chip, gain_one, shift_one, w_joint, b_joint, near, True)
        normal, keys, values, queries = outs
        ffn_part, *kept_ffn = ffn_call(chip, gain_two, shift_two, w_up, b_up, w_down, save)
        key_parts, value_parts, normal_parts = [keys], [values], [normal]
        if chips > 1:
            rest = jnp.concatenate([x for other in others for x in (other, swap_core(other))], 0)
            far_normal, far_keys, far_values = joint_call(rest, gain_one, shift_one, w_joint, b_joint, far, False)
            key_parts.append(far_keys)
            value_parts.append(far_values)
            normal_parts.append(far_normal)
        attn_part, mixture, lse = attend_call(
            queries, key_parts, value_parts, spot_rows, places, limits, w_output, block
        )
        attention = attn_part[:rows].astype(F32) + swap_core(attn_part[rows:]).astype(F32) + b_output
        feedforward = ffn_part[:rows].astype(F32) + swap_core(ffn_part[rows:]).astype(F32) + b_down
        state = own.astype(F32)
        result = (state + attention + feedforward).astype(BF16)
        if not save:
            return result
        moments = jnp.stack(
            [jnp.sum(state * state), jnp.sum(attention * attention), jnp.sum(feedforward * feedforward)]
        )
        return result, moments, (normal_parts, queries, key_parts, value_parts, mixture, lse, *kept_ffn)

    def backward(own, g_own, kept):
        normal_parts, queries, key_parts, value_parts, mixture, lse, second_in, active, slope = kept
        g = jnp.concatenate([g_own, swap_core(g_own)], 0)
        d_queries, d_keys, d_values, joint_sums = attend_back_call(
            queries, g, mixture, lse, key_parts, value_parts, spot_rows, places, limits, w_output, table, block
        )
        near_part = joint_back_call([d_queries, d_keys, d_values], 0, chip_rows, w_joint)
        firsts = [near_part[:rows], swap_core(near_part[rows:])]
        if chips > 1:
            far_part = joint_back_call([d_keys, d_values], chip_rows, length - chip_rows, w_joint)
            far_part = far_part.reshape(chips - 1, 2, rows, width)
            far_sum = (far_part[:, 0].astype(F32) + swap_core(far_part[:, 1]).astype(F32)).astype(BF16)
            firsts += [swap_ctx(far_sum[k - 1], k) for k in range(1, chips)]
        second_part, d_hidden, up_sums = ffn_back_call(g, slope, w_up, w_down)
        seconds = [second_part[:rows], swap_core(second_part[rows:])]
        d_own, norm_sums = norm_back_call(own, g_own, jnp.stack(firsts), jnp.stack(seconds), gains)
        return d_own, norm_sums, (g, d_queries, d_keys, d_values, joint_sums, d_hidden, up_sums)

    token_rows = to_planes(tokens)
    g_rows = to_planes(cotangent)
    own = token_rows
    for tick in range(sections):
        last = tick == sections - 1
        if not last:
            result = forward(own, False)
            own = jnp.where(section == 0, token_rows, next_section(result, 1))
        else:
            result, moments, kept = forward(own, True)
    section_out = from_planes(result)
    g_own = g_rows
    for tick in range(sections):
        d_own, norm_sums, grads = backward(own, g_own, kept)
        if tick < sections - 1:
            g_own = jnp.where(section == sections - 1, g_rows, next_section(d_own, -1))
    section_in_grad = from_planes(d_own)

    normal_parts, queries, key_parts, value_parts, mixture, lse, second_in, active, slope = kept
    g, d_queries, d_keys, d_values, joint_sums, d_hidden, up_sums = grads
    late = member_masks + seq_masks
    early = seq_masks + member_masks
    local = w_output.shape[0]
    units = w_up.shape[1]

    g_late = by_owner(g, late, ctx)
    down_pieces = tn(g_late, active).astype(BF16).reshape(ctx_size, -1, units)
    down_total = reduce_ctx(down_pieces, late).T
    output_pieces = tn(g_late, mixture).astype(BF16).reshape(ctx_size, -1, local)
    output_total = reduce_ctx(output_pieces, late).T
    up_pieces = tn(by_owner(second_in, early, ctx), d_hidden).astype(BF16).reshape(ctx_size, -1, units)
    up_total = reduce_ctx(up_pieces, early)
    near_normal = by_owner(normal_parts[0], late, ctx)
    query_pieces = tn(near_normal, d_queries)
    key_pieces = tn(near_normal, d_keys[:chip_rows])
    value_pieces = tn(near_normal, d_values[:chip_rows])
    if chips > 1:
        far_normal = by_owner(normal_parts[1], late, ctx)
        key_pieces += tn(far_normal, d_keys[chip_rows:])
        value_pieces += tn(far_normal, d_values[chip_rows:])
    joint_pieces = jnp.stack([query_pieces, key_pieces, value_pieces]).astype(BF16)
    joint_pieces = joint_pieces.reshape(3, ctx_size, -1, local).transpose(1, 0, 2, 3)
    joint_total = reduce_ctx(joint_pieces, late)

    both = jnp.concatenate([norm_sums[:5].reshape(-1), moments])
    both = both + swap_core(both)
    small = jnp.concatenate([both, joint_sums[:3].reshape(-1), up_sums.reshape(-1)])
    for mask in late:
        small = small + swap_ctx(small, mask)
    norm_total = small[: 5 * width].reshape(5, 1, width)
    moment_total = small[5 * width : 5 * width + 3]
    joint_shift = small[5 * width + 3 : 5 * width + 3 + 3 * local].reshape(1, 3, local)
    up_shift = small[5 * width + 3 + 3 * local :].reshape(1, units)
    root_means = jnp.sqrt(moment_total / (length * seqs * width))
    return (
        section_out,
        section_in_grad,
        norm_total[0],
        norm_total[1],
        norm_total[2],
        norm_total[3],
        joint_total[None],
        joint_shift,
        output_total[None],
        norm_total[4],
        up_total[None],
        up_shift,
        down_total[None],
        norm_total[4],
        root_means[None],
    )


def solution(mesh):
    in_specs = (
        P(None, "ctx", None),
        P(None, "ctx", None),
        P(),
        P("section", None),
        P("section", None),
        P("section", None),
        P("section", None),
        P("section", None, None, "tp"),
        P("section", None, "tp"),
        P("section", "tp", None),
        P("section", None),
        P("section", None, "tp"),
        P("section", "tp"),
        P("section", "tp", None),
        P("section", None),
    )
    out_specs = (
        P("section", None, "ctx", None),
        P("section", None, "ctx", None),
        P("section", None),
        P("section", None),
        P("section", None),
        P("section", None),
        P("section", None, "ctx", "tp"),
        P("section", None, "tp"),
        P("section", "tp", "ctx"),
        P("section", None),
        P("section", "ctx", "tp"),
        P("section", "tp"),
        P("section", "tp", "ctx"),
        P("section", None),
        P("section", None),
    )
    return jax.shard_map(
        on_device, mesh=mesh, in_specs=in_specs, out_specs=out_specs, check_vma=False
    )
```

```python
import functools

import jax
import jax.numpy as jnp
from jax import lax
from jax.experimental import pallas as pl
from jax.experimental.pallas import tpu as pltpu
from jax.sharding import PartitionSpec as P

HEAD = 64
ROT = 16
EPS = 1e-05
ROTARY_BASE = 10000.0
NEGATIVE = -1e30
STACK = 4
GROUP = STACK * HEAD
KEY_TILE = 512
VMEM_LIMIT = 56 * 1024 * 1024
BF16 = jnp.bfloat16
F32 = jnp.float32


def dot(a, b):
    return jnp.dot(a, b, preferred_element_type=F32)


def dot_nt(a, b):
    return lax.dot_general(a, b, (((1,), (1,)), ((), ())), preferred_element_type=F32)


def params_of(**more):
    return pltpu.CompilerParams(vmem_limit_bytes=VMEM_LIMIT, **more)


def whole(shape):
    return pl.BlockSpec(shape, lambda *_: (0,) * len(shape))


def rows_of(tile, *rest):
    return pl.BlockSpec((tile, *rest), lambda r, *_: (r,) + (0,) * len(rest))


def halves_of(tile, count, *rest):
    return [
        pl.BlockSpec((tile, *rest), lambda r, *_: (jnp.minimum(r, count - 1),) + (0,) * len(rest)),
        pl.BlockSpec((tile, *rest), lambda r, *_: (jnp.maximum(r - count, 0),) + (0,) * len(rest)),
    ]


def pick(refs):
    return jnp.where(pl.program_id(0) < pl.num_programs(0) // 2, refs[0][...], refs[1][...])


def put(refs, value):
    first = pl.program_id(0) < pl.num_programs(0) // 2
    for ref, here in zip(refs, (first, jnp.logical_not(first))):

        @pl.when(here)
        def _():
            ref[...] = value


def waiting(kernel, inputs, deps):
    return lambda *refs: kernel(*refs[:inputs], *refs[inputs + len(deps) :])


def exchanged(position, mask):
    for bit in range(mask.bit_length()):
        if mask >> bit & 1:
            position = position + (1 << bit) - (2 << bit) * (position // (1 << bit) % 2)
    return position


def carrying(kernel, inputs, outputs, moves):
    count = len(moves)

    def body(*refs):
        sources = refs[inputs : inputs + count]
        outs = refs[inputs + count : inputs + count + outputs]
        targets = refs[inputs + count + outputs : inputs + 2 * count + outputs]
        *scratch, send, receive = refs[inputs + 2 * count + outputs :]
        partners = [{axis: exchanged(lax.axis_index(axis), mask)} for axis, mask in moves]
        copies = [
            pltpu.make_async_remote_copy(
                source, target, send.at[n], receive.at[n], device_id=partner, device_id_type=pl.DeviceIdType.MESH
            )
            for n, (source, target, partner) in enumerate(zip(sources, targets, partners))
        ]

        @pl.when(pl.program_id(0) == 0)
        def _():
            barrier = pltpu.get_barrier_semaphore()
            for partner in partners:
                pl.semaphore_signal(barrier, inc=1, device_id=partner, device_id_type=pl.DeviceIdType.MESH)
            pl.semaphore_wait(barrier, count)
            for copy in copies:
                copy.start()

        kernel(*refs[:inputs], *outs, *scratch)

        @pl.when(pl.program_id(0) == pl.num_programs(0) - 1)
        def _():
            for copy in copies:
                copy.wait()

    return body


def carrier_semaphores(count):
    return [pltpu.SemaphoreType.DMA((count,)), pltpu.SemaphoreType.DMA((count,))]


def anywhere(count):
    return [pl.BlockSpec(memory_space=pl.ANY)] * count


def cost(flops, size):
    return pl.CostEstimate(flops=int(flops), bytes_accessed=int(size), transcendentals=0)


def shape_of(*shape, dtype=BF16):
    return jax.ShapeDtypeStruct(shape, dtype)


def normalize(values):
    middle = jnp.mean(values, axis=-1, keepdims=True)
    centered = values - middle
    spread = jnp.mean(centered * centered, axis=-1, keepdims=True)
    inverse = lax.rsqrt(spread + EPS)
    return centered * inverse, inverse


def turn(values, cosine, sine):
    pieces = []
    for start in range(0, values.shape[1], 128):
        part = values[:, start : start + 128]
        ahead = pltpu.roll(part, 128 - ROT // 2, 1)
        behind = pltpu.roll(part, ROT // 2, 1)
        entry = lax.broadcasted_iota(jnp.int32, part.shape, 1) % HEAD
        pieces.append(part * cosine + jnp.where(entry < ROT // 2, -ahead, behind) * sine)
    return jnp.concatenate(pieces, axis=1)


def joint_kernel(h0_ref, h1_ref, gain_ref, shift_ref, w_ref, b_ref, cos_ref, sin_ref, n_ref, k_ref, v_ref):
    scaled, _ = normalize(pick((h0_ref, h1_ref)).astype(F32))
    low = (scaled * gain_ref[...] + shift_ref[...]).astype(BF16)
    n_ref[...] = low
    cosine, sine = cos_ref[...], sin_ref[...]
    keys = dot(low, w_ref[1]) + b_ref[1:2]
    values = dot(low, w_ref[2]) + b_ref[2:3]
    k_ref[...] = turn(keys, cosine, sine).astype(BF16)
    v_ref[...] = values.astype(BF16)


def joint_call(pair, gain, shift, w_joint, b_joint, table, offset, deps=()):
    rows, width = pair[0].shape
    local = w_joint.shape[2]
    tile = min(512, rows)
    first = offset // tile
    count = 2
    turns = pl.BlockSpec((tile, 128), lambda r: (first + r, 0))
    return pl.pallas_call(
        waiting(joint_kernel, 8, deps),
        grid=(2 * rows // tile,),
        in_specs=halves_of(tile, rows // tile, width)
        + [whole((1, width)), whole((1, width)), whole(w_joint.shape), whole(b_joint.shape), turns, turns]
        + anywhere(len(deps)),
        out_specs=[rows_of(tile, width)] + [rows_of(tile, local)] * count,
        out_shape=[shape_of(2 * rows, width)] + [shape_of(2 * rows, local)] * count,
        compiler_params=params_of(),
        cost_estimate=cost(4 * rows * width * local * count, 8 * rows * width + 2 * w_joint.size),
        name="joint_projection",
    )(*pair, gain, shift, w_joint, b_joint, *table, *deps)


def gelu_parts(x):
    return 0.5 + 0.5 * lax.erf(x * 0.5**0.5), jnp.exp(-0.5 * x * x)


def front_kernel(
    save, h0_ref, h1_ref, norms_ref, w_ref, b_ref, cos_ref, sin_ref, up_ref, up_b_ref, down_ref,
    n_ref, k_ref, v_ref, q_ref, part0_ref, part1_ref, *saved
):
    scaled, _ = normalize(pick((h0_ref, h1_ref)).astype(F32))
    low = (scaled * norms_ref[0:1] + norms_ref[1:2]).astype(BF16)
    n_ref[...] = low
    cosine, sine = cos_ref[...], sin_ref[...]
    keys = dot(low, w_ref[1]) + b_ref[1:2]
    values = dot(low, w_ref[2]) + b_ref[2:3]
    queries = dot(low, w_ref[0]) + b_ref[0:1]
    q_ref[...] = (turn(queries, cosine, sine) * HEAD ** (-0.5)).astype(BF16)
    k_ref[...] = turn(keys, cosine, sine).astype(BF16)
    v_ref[...] = values.astype(BF16)
    low = (scaled * norms_ref[2:3] + norms_ref[3:4]).astype(BF16)
    if save:
        saved[0][...] = low
    total = None
    for start in range(0, up_ref.shape[1], 512):
        cut = pl.ds(start, 512)
        hidden = dot(low, up_ref[:, cut]) + up_b_ref[:, cut]
        share, bell = gelu_parts(hidden)
        active = (hidden * share).astype(BF16)
        if save:
            saved[1][:, cut] = active
            saved[2][:, cut] = (share + hidden * bell * 0.3989422804014327).astype(BF16)
        term = dot(active, down_ref[cut, :])
        total = term if total is None else total + term
    put((part0_ref, part1_ref), total.astype(BF16))


def front_call(pair, norms, w_joint, b_joint, table, w_up, b_up, w_down, save, moves, moved, name, number):
    rows, width = pair[0].shape
    local = w_joint.shape[2]
    units = w_up.shape[1]
    tile = min(512, rows)
    out = [shape_of(2 * rows, width)] + [shape_of(2 * rows, local)] * 3 + [shape_of(rows, width)] * 2
    out_specs = [rows_of(tile, width)] + [rows_of(tile, local)] * 3 + halves_of(tile, rows // tile, width)
    if save:
        out += [shape_of(2 * rows, width)] + [shape_of(2 * rows, units)] * 2
        out_specs += [rows_of(tile, width), rows_of(tile, units), rows_of(tile, units)]
    ins = (norms, w_joint, b_joint, *table, w_up, b_up, w_down)
    turns = rows_of(tile, 128)
    specs = [turns if x is table[0] or x is table[1] else whole(x.shape) for x in ins]
    outs = pl.pallas_call(
        carrying(functools.partial(front_kernel, save), 2 + len(ins), len(out), moves),
        grid=(2 * rows // tile,),
        in_specs=halves_of(tile, rows // tile, width) + specs + anywhere(len(moves)),
        out_specs=out_specs + anywhere(len(moves)),
        out_shape=out + [shape_of(*x.shape) for x in moved],
        scratch_shapes=carrier_semaphores(len(moves)),
        compiler_params=params_of(collective_id=number, has_side_effects=True),
        cost_estimate=cost(4 * rows * width * (3 * local + 2 * units), 4 * w_up.size + 16 * rows * width),
        name=name,
    )(*pair, *ins, *moved)
    return outs[: len(out)], outs[len(out) :]


def ffn_back_kernel(g0_ref, g1_ref, slope_ref, up_ref, down_ref, part0_ref, part1_ref, hidden_ref, sums_ref):
    upstream = pick((g0_ref, g1_ref))
    units = up_ref.shape[1]

    @pl.when(pl.program_id(0) == 0)
    def _():
        sums_ref[...] = jnp.zeros_like(sums_ref)

    total = None
    for start in range(0, units, 512):
        cut = pl.ds(start, 512)
        d_active = dot_nt(upstream, down_ref[cut, :])
        d_hidden = (d_active * slope_ref[:, cut].astype(F32)).astype(BF16)
        hidden_ref[:, cut] = d_hidden
        sums_ref[:, cut] += jnp.sum(d_hidden.astype(F32), axis=0, keepdims=True)
        term = dot_nt(d_hidden, up_ref[:, cut])
        total = term if total is None else total + term
    put((part0_ref, part1_ref), total.astype(BF16))


def ffn_back_call(pair, slope, w_up, w_down, deps=()):
    rows, width = pair[0].shape
    units = w_up.shape[1]
    tile = min(512, rows)
    return pl.pallas_call(
        waiting(ffn_back_kernel, 5, deps),
        grid=(2 * rows // tile,),
        in_specs=halves_of(tile, rows // tile, width) + [rows_of(tile, units), whole(w_up.shape), whole(w_down.shape)]
        + anywhere(len(deps)),
        out_specs=halves_of(tile, rows // tile, width) + [rows_of(tile, units), whole((1, units))],
        out_shape=[shape_of(rows, width)] * 2 + [shape_of(2 * rows, units), shape_of(1, units, dtype=F32)],
        compiler_params=params_of(),
        cost_estimate=cost(8 * rows * width * units, 4 * w_up.size + 8 * rows * (width + units)),
        name="feed_forward_back",
    )(*pair, slope, w_up, w_down, *deps)


def start_sorted(places_ref, parts, targets, sem, block):
    copies = []
    for refs, target in zip(parts, targets):
        index = 0
        for ref in refs:
            for local in range(ref.shape[0] // block):
                place = pl.ds(pl.multiple_of(places_ref[index] * block, block), block)
                copies.append(pltpu.make_async_copy(ref.at[pl.ds(local * block, block)], target.at[place], sem))
                index += 1
    for copy in copies:
        copy.start()
    return copies


def transpose_into(source, target):
    rows, columns = source.shape

    def step(index, _):
        start = pl.multiple_of(index * 256, 256)
        for column in range(0, columns, 256):
            target[column : column + 256, pl.ds(start, 256)] = source[pl.ds(start, 256), column : column + 256].T
        return 0

    lax.fori_loop(0, rows // 256, step, 0)


def stacked(values):
    owner = lax.broadcasted_iota(jnp.int32, values.shape, 1) // HEAD
    zero = jnp.zeros_like(values)
    return jnp.concatenate([jnp.where(owner == a, values, zero) for a in range(STACK)], axis=0)


def spots_of(places_ref, step, tile, block, shape, axis):
    at = lax.broadcasted_iota(jnp.int32, shape, axis) % tile
    count = tile // block
    spot = at + places_ref[step * count] * block
    for s in range(1, count):
        spot = jnp.where(at >= s * block, at - s * block + places_ref[step * count + s] * block, spot)
    return spot


def attend_kernel(block, tile, remote, places_ref, limits_ref, q_ref, wo_ref, *refs):
    key_refs, value_refs = refs[: 1 + remote], refs[1 + remote : 2 + 2 * remote]
    part0_ref, part1_ref, mix_ref, lse_ref, keys, values, scores_ref, sem = refs[2 + 2 * remote :]
    groups = q_ref.shape[1] // GROUP
    half = part0_ref.shape[0]
    rows = STACK * tile
    lanes = [slice(g * GROUP, (g + 1) * GROUP) for g in range(groups)]
    for copy in start_sorted(places_ref, (key_refs, value_refs), (keys, values), sem, block):
        copy.wait()

    def tile_step(step, _):
        mine = pl.ds(pl.multiple_of(step * tile, tile), tile)
        heads = [stacked(q_ref[mine, lane]) for lane in lanes]
        spots = spots_of(places_ref, step, tile, block, (rows, 128), 0)

        def attend_to(count):
            open_end = (count - 1) * KEY_TILE if tile == block else 0
            tops = []
            for g, lane in enumerate(lanes):
                top = None
                for start in range(0, count * KEY_TILE, KEY_TILE):
                    scores = dot_nt(heads[g], keys[start : start + KEY_TILE, lane])
                    for column in range(0, KEY_TILE, 128):
                        piece = scores[:, column : column + 128]
                        if start + column >= open_end:
                            spot = start + column + lax.broadcasted_iota(jnp.int32, piece.shape, 1)
                            piece = jnp.where(spot <= spots, piece, NEGATIVE)
                        scores_ref[g, :, start + column : start + column + 128] = piece
                        top = piece if top is None else jnp.maximum(top, piece)
                tops.append(jnp.broadcast_to(jnp.max(top, axis=1, keepdims=True), (rows, 128)))
            for g, lane in enumerate(lanes):
                mass, total = None, None
                for start in range(0, count * KEY_TILE, KEY_TILE):
                    raised = []
                    for column in range(start, start + KEY_TILE, 128):
                        piece = jnp.exp(scores_ref[g, :, column : column + 128] - tops[g])
                        mass = piece if mass is None else mass + piece
                        raised.append(piece.astype(BF16))
                    term = dot(jnp.concatenate(raised, axis=1), values[start : start + KEY_TILE, lane])
                    total = term if total is None else total + term
                mass = jnp.broadcast_to(jnp.sum(mass, axis=1, keepdims=True), (rows, 128))
                total = total * jnp.concatenate([1.0 / mass] * (GROUP // 128), axis=1)
                owner = lax.broadcasted_iota(jnp.int32, (tile, GROUP), 1) // HEAD
                mixture = total[:tile]
                for a in range(1, STACK):
                    mixture = jnp.where(owner == a, total[a * tile : (a + 1) * tile], mixture)
                mix_ref[mine, lane] = mixture.astype(BF16)
                lse = tops[g] + jnp.log(mass)
                for a in range(STACK):
                    lse_ref[step, g : g + 1, a * tile : (a + 1) * tile] = lse[a * tile : (a + 1) * tile].T[0:1]

        for count in range(1, keys.shape[0] // KEY_TILE + 1):
            pl.when(limits_ref[step, 1] == count)(functools.partial(attend_to, count))
        return 0

    lax.fori_loop(0, q_ref.shape[0] // tile, tile_step, 0)
    part0_ref[...] = dot(mix_ref[:half], wo_ref[...]).astype(BF16)
    part1_ref[...] = dot(mix_ref[half:], wo_ref[...]).astype(BF16)


def attend_call(queries, key_parts, value_parts, places, limits, w_output, block, deps=()):
    rows, local = queries.shape
    width = w_output.shape[1]
    tile = rows // limits.shape[0]
    length = sum(part.shape[0] for part in key_parts)
    groups = local // GROUP
    outs = [(rows // 2, width), (rows // 2, width), (rows, local), (rows // tile, groups, STACK * tile)]
    return pl.pallas_call(
        waiting(functools.partial(attend_kernel, block, tile, len(key_parts) - 1), 4 + 2 * len(key_parts), deps),
        grid_spec=pltpu.PrefetchScalarGridSpec(
            num_scalar_prefetch=2,
            grid=(1,),
            in_specs=[whole((rows, local)), whole(w_output.shape)] + anywhere(2 * len(key_parts) + len(deps)),
            out_specs=[whole(shape) for shape in outs],
            scratch_shapes=[
                pltpu.VMEM((length, local), BF16),
                pltpu.VMEM((length, local), BF16),
                pltpu.VMEM((groups, STACK * tile, length), F32),
                pltpu.SemaphoreType.DMA,
            ],
        ),
        out_shape=[shape_of(*shape) for shape in outs[:3]] + [shape_of(*outs[3], dtype=F32)],
        compiler_params=params_of(),
        cost_estimate=cost(12 * rows * length * local, 2 * length * local * 4),
        name="attend",
    )(places, limits, queries, w_output, *key_parts, *value_parts, *deps)


def attend_back_kernel(
    block, tile, remote, places_ref, limits_ref, q_ref, g0_ref, g1_ref, mix_ref, lse_ref, wo_ref, cos_ref, sin_ref, *refs
):
    key_refs, value_refs = refs[: 1 + remote], refs[1 + remote : 2 + 2 * remote]
    (dq_ref, dk_ref, dv_ref, sums_ref, keys, values, keys_t, d_keys, d_values, d_mixture, inner, total, d_queries, sem) = refs[
        2 + 2 * remote :
    ]
    groups = q_ref.shape[1] // GROUP
    rows = q_ref.shape[0]
    half = g0_ref.shape[0]
    lanes = [slice(g * GROUP, (g + 1) * GROUP) for g in range(groups)]
    copies = start_sorted(places_ref, (key_refs, value_refs), (keys, values), sem, block)
    d_keys[...] = jnp.zeros_like(d_keys)
    d_values[...] = jnp.zeros_like(d_values)
    head_of = lax.broadcasted_iota(jnp.int32, (8, GROUP), 1) // HEAD
    picker = jnp.where(lax.broadcasted_iota(jnp.int32, (8, GROUP), 0) == head_of, 1.0, 0.0).astype(BF16)
    for index, ref in enumerate((g0_ref, g1_ref)):
        cut = pl.ds(index * half, half)
        low = dot_nt(ref[...], wo_ref[...]).astype(BF16)
        d_mixture[cut, :] = low
        product = low.astype(F32) * mix_ref[cut, :].astype(F32)
        high = product.astype(BF16)
        rest = (product - high.astype(F32)).astype(BF16)
        for g, lane in enumerate(lanes):
            inner[g * 8 : (g + 1) * 8, cut] = dot_nt(picker, high[:, lane]) + dot_nt(picker, rest[:, lane])
    for copy in copies:
        copy.wait()
    transpose_into(keys, keys_t)

    def query_step(step, _):
        mine = pl.ds(pl.multiple_of(step * tile, tile), tile)
        spots = spots_of(places_ref, step, tile, block, (1, STACK * tile), 1)
        heads = [stacked(q_ref[mine, lane]) for lane in lanes]
        sides = [stacked(d_mixture[mine, lane]) for lane in lanes]
        sums = [
            jnp.concatenate([inner[g * 8 + a : g * 8 + a + 1, mine] for a in range(STACK)], axis=1) for g in range(groups)
        ]
        lse = [lse_ref[step, g : g + 1, :] for g in range(groups)]
        total[...] = jnp.zeros_like(total)

        def key_step(masked, index, carry):
            start = pl.multiple_of(index * KEY_TILE, KEY_TILE)
            cut = pl.ds(start, KEY_TILE)
            for g, lane in enumerate(lanes):
                scores = dot_nt(keys[cut, lane], heads[g])
                if masked:
                    spot = start + lax.broadcasted_iota(jnp.int32, scores.shape, 0)
                    scores = jnp.where(spot <= spots, scores, NEGATIVE)
                weights = jnp.exp(scores - lse[g])
                d_weights = dot_nt(values[cut, lane], sides[g])
                d_scores = (weights * (d_weights - sums[g])).astype(BF16)
                d_values[cut, lane] += dot(weights.astype(BF16), sides[g])
                d_keys[cut, lane] += dot(d_scores, heads[g])
                total[lane, :] += dot(keys_t[lane, cut], d_scores)
            return carry

        lax.fori_loop(0, limits_ref[step, 0], functools.partial(key_step, False), 0)
        lax.fori_loop(limits_ref[step, 0], limits_ref[step, 1], functools.partial(key_step, True), 0)
        for lane in lanes:
            picked = [total[lane, :][a * HEAD : (a + 1) * HEAD, a * tile : (a + 1) * tile] for a in range(STACK)]
            d_queries[mine, lane] = jnp.concatenate(picked, axis=0).T
        return 0

    lax.fori_loop(0, rows // tile, query_step, 0)
    turned = turn(d_queries[...] * HEAD ** (-0.5), cos_ref[:rows], -sin_ref[:rows]).astype(BF16)
    dq_ref[...] = turned
    sums_ref[...] = jnp.zeros_like(sums_ref)
    sums_ref[0:1, :] = jnp.sum(turned.astype(F32), axis=0, keepdims=True)

    def block_step(index, _):
        place = pl.ds(pl.multiple_of(places_ref[index] * block, block), block)
        mine = pl.ds(pl.multiple_of(index * block, block), block)
        turned = turn(d_keys[place, :], cos_ref[mine, :], -sin_ref[mine, :]).astype(BF16)
        dk_ref[mine, :] = turned
        low = d_values[place, :].astype(BF16)
        dv_ref[mine, :] = low
        sums_ref[1:2, :] += jnp.sum(turned.astype(F32), axis=0, keepdims=True)
        sums_ref[2:3, :] += jnp.sum(low.astype(F32), axis=0, keepdims=True)
        return 0

    lax.fori_loop(0, dk_ref.shape[0] // block, block_step, 0)


def attend_back_call(
    queries, g_pair, mixture, lse, key_parts, value_parts, places, limits, w_output, table, block, deps=()
):
    rows, local = queries.shape
    width = w_output.shape[1]
    tile = rows // limits.shape[0]
    length = sum(part.shape[0] for part in key_parts)
    groups = local // GROUP
    ins = (queries, *g_pair, mixture, lse, w_output, *table)
    return pl.pallas_call(
        waiting(
            functools.partial(attend_back_kernel, block, tile, len(key_parts) - 1), 2 + len(ins) + 2 * len(key_parts), deps
        ),
        grid_spec=pltpu.PrefetchScalarGridSpec(
            num_scalar_prefetch=2,
            grid=(1,),
            in_specs=[whole(x.shape) for x in ins] + anywhere(2 * len(key_parts) + len(deps)),
            out_specs=[whole((rows, local)), whole((length, local)), whole((length, local)), whole((8, local))],
            scratch_shapes=[
                pltpu.VMEM((length, local), BF16),
                pltpu.VMEM((length, local), BF16),
                pltpu.VMEM((local, length), BF16),
                pltpu.VMEM((length, local), F32),
                pltpu.VMEM((length, local), F32),
                pltpu.VMEM((rows, local), BF16),
                pltpu.VMEM((8 * groups, rows), F32),
                pltpu.VMEM((local, STACK * tile), F32),
                pltpu.VMEM((rows, local), F32),
                pltpu.SemaphoreType.DMA,
            ],
        ),
        out_shape=[shape_of(rows, local), shape_of(length, local), shape_of(length, local), shape_of(8, local, dtype=F32)],
        compiler_params=params_of(),
        cost_estimate=cost(24 * rows * length * local, 2 * length * local * 8),
        name="attend_back",
    )(places, limits, *ins, *key_parts, *value_parts, *deps)


def joint_back_kernel(count, *refs):
    w_ref = refs[count]
    total = None
    for index in range(count):
        term = dot_nt(refs[index][...], w_ref[3 - count + index])
        total = term if total is None else total + term
    put(refs[count + 1 :], total.astype(BF16))


def joint_back_call(grads, offset, rows, w_joint, deps=()):
    width, local = w_joint.shape[1:]
    half = rows // 2
    tile = min(512, half)
    first = offset // tile
    return pl.pallas_call(
        waiting(functools.partial(joint_back_kernel, len(grads)), len(grads) + 1, deps),
        grid=(rows // tile,),
        in_specs=[pl.BlockSpec((tile, local), lambda r: (first + r, 0))] * len(grads)
        + [whole(w_joint.shape)]
        + anywhere(len(deps)),
        out_specs=halves_of(tile, half // tile, width),
        out_shape=[shape_of(half, width)] * 2,
        compiler_params=params_of(),
        cost_estimate=cost(2 * rows * width * local * len(grads), 2 * rows * (width + 3 * local) + 2 * w_joint.size),
        name="joint_projection_back",
    )(*grads, w_joint, *deps)


def rear_kernel(q_ref, k_ref, v_ref, w_ref, g0_ref, g1_ref, slope_ref, up_ref, down_ref, first0_ref, first1_ref, part0_ref, part1_ref):
    total = dot_nt(q_ref[...], w_ref[0]) + dot_nt(k_ref[...], w_ref[1]) + dot_nt(v_ref[...], w_ref[2])
    put((first0_ref, first1_ref), total.astype(BF16))
    upstream = pick((g0_ref, g1_ref))
    total = None
    for start in range(0, up_ref.shape[1], 512):
        cut = pl.ds(start, 512)
        d_active = dot_nt(upstream, down_ref[cut, :])
        d_hidden = (d_active * slope_ref[:, cut].astype(F32)).astype(BF16)
        term = dot_nt(d_hidden, up_ref[:, cut])
        total = term if total is None else total + term
    put((part0_ref, part1_ref), total.astype(BF16))


def rear_call(grads, w_joint, pair, slope, w_up, w_down, moves, moved, name, number):
    rows, width = pair[0].shape
    local = w_joint.shape[2]
    units = w_up.shape[1]
    tile = min(512, rows)
    halves = halves_of(tile, rows // tile, width)
    outs = pl.pallas_call(
        carrying(rear_kernel, 9, 4, moves),
        grid=(2 * rows // tile,),
        in_specs=[rows_of(tile, local)] * 3
        + [whole(w_joint.shape)]
        + halves
        + [rows_of(tile, units), whole(w_up.shape), whole(w_down.shape)]
        + anywhere(len(moves)),
        out_specs=halves + halves + anywhere(len(moves)),
        out_shape=[shape_of(rows, width)] * 4 + [shape_of(*x.shape) for x in moved],
        scratch_shapes=carrier_semaphores(len(moves)),
        compiler_params=params_of(collective_id=number, has_side_effects=True),
        cost_estimate=cost(4 * rows * width * (3 * local + 2 * units), 4 * w_up.size + 16 * rows * width),
        name=name,
    )(*grads, w_joint, *pair, slope, w_up, w_down, *moved)
    return outs[:2], outs[2:4], outs[4:]


def norm_back_kernel(firsts, h_ref, g_ref, gains_ref, *refs):
    first_refs, second_refs, (out_ref, sums_ref) = refs[:firsts], refs[firsts:-2], refs[-2:]

    @pl.when(pl.program_id(0) == 0)
    def _():
        sums_ref[...] = jnp.zeros_like(sums_ref)

    scaled, inverse = normalize(h_ref[...].astype(F32))
    upstream = g_ref[...].astype(F32)
    d_first = sum(ref[...].astype(F32) for ref in first_refs)
    d_second = sum(ref[...].astype(F32) for ref in second_refs)
    for row, term in enumerate((d_first * scaled, d_first, d_second * scaled, d_second, upstream)):
        sums_ref[row : row + 1, :] += jnp.sum(term, axis=0, keepdims=True)
    d_scaled = d_first * gains_ref[0:1] + d_second * gains_ref[1:2]
    middle = jnp.mean(d_scaled, axis=-1, keepdims=True)
    along = jnp.mean(d_scaled * scaled, axis=-1, keepdims=True)
    out_ref[...] = (upstream + inverse * (d_scaled - middle - scaled * along)).astype(BF16)


def norm_back_call(h, g, firsts, seconds, gains, deps=()):
    rows, width = h.shape
    tile = min(128, rows)
    one = rows_of(tile, width)
    return pl.pallas_call(
        waiting(functools.partial(norm_back_kernel, len(firsts)), 3 + len(firsts) + len(seconds), deps),
        grid=(rows // tile,),
        in_specs=[one, one, whole(gains.shape)] + [one] * (len(firsts) + len(seconds)) + anywhere(len(deps)),
        out_specs=[one, whole((8, width))],
        out_shape=[shape_of(rows, width), shape_of(8, width, dtype=F32)],
        compiler_params=params_of(),
        cost_estimate=cost(20 * rows * width, 2 * rows * width * 8),
        name="norm_back",
    )(h, g, gains, *firsts, *seconds, *deps)


def merge_kernel(h_ref, a0_ref, a1_ref, f0_ref, f1_ref, shifts_ref, out_ref, sums_ref):
    @pl.when(pl.program_id(0) == 0)
    def _():
        sums_ref[...] = jnp.zeros_like(sums_ref)

    state = h_ref[...].astype(F32)
    attention = a0_ref[...].astype(F32) + a1_ref[...].astype(F32) + shifts_ref[0:1]
    feedforward = f0_ref[...].astype(F32) + f1_ref[...].astype(F32) + shifts_ref[1:2]
    out_ref[...] = (state + attention + feedforward).astype(BF16)
    for row, term in enumerate((state, attention, feedforward)):
        sums_ref[row : row + 1, :] += jnp.sum(term * term, axis=0, keepdims=True)


def merge_call(h, attn_pair, ffn_pair, shifts, deps=()):
    rows, width = h.shape
    tile = min(128, rows)
    one = rows_of(tile, width)
    return pl.pallas_call(
        waiting(merge_kernel, 6, deps),
        grid=(rows // tile,),
        in_specs=[one] * 5 + [whole(shifts.shape)] + anywhere(len(deps)),
        out_specs=[one, whole((8, width))],
        out_shape=[shape_of(rows, width), shape_of(8, width, dtype=F32)],
        compiler_params=params_of(),
        cost_estimate=cost(10 * rows * width, 2 * rows * width * 6),
        name="merge",
    )(h, *attn_pair, *ffn_pair, shifts, *deps)


def tn(a, b):
    return lax.dot_general(a, b, (((0,), (0,)), ((), ())), preferred_element_type=F32)


def slope_kernel(count, terms, *refs):
    lefts = [jnp.concatenate([ref[...] for ref in refs[t * count : (t + 1) * count]], axis=1) for t in range(terms)]
    rights = refs[terms * count : terms * (count + 1)]
    out_ref = refs[-1]
    share = lefts[0].shape[1] // count
    total = sum(tn(left, right[...]) for left, right in zip(lefts, rights)).astype(BF16)
    for index in range(count):
        out_ref[index] = total[index * share : (index + 1) * share]


def slope_call(owners, terms, width, place, name, buffer=None, deps=()):
    share = terms[0][0].shape[1] // owners
    columns = terms[0][1].shape[1]
    count = 4
    steps = owners // count
    ins, specs = [], []
    for left, _, _ in terms:
        for index in range(count):
            ins.append(left)
            specs.append(pl.BlockSpec((left.shape[0], share), functools.partial(lambda i, r: (0, count * r + i), index)))
    for left, right, row in terms:
        ins.append(right)
        specs.append(pl.BlockSpec((left.shape[0], columns), functools.partial(lambda i, r: (i, 0), row)))
    behind = ((buffer,) if buffer is not None else ()) + tuple(deps)
    return pl.pallas_call(
        waiting(functools.partial(slope_kernel, count, len(terms)), len(ins), behind),
        grid=(steps,),
        in_specs=specs + anywhere(len(behind)),
        out_specs=pl.BlockSpec((count, share, columns), lambda r: (r, 0, place // columns)),
        out_shape=shape_of(owners, share, width),
        input_output_aliases={len(ins): 0} if buffer is not None else {},
        compiler_params=params_of(),
        cost_estimate=cost(
            sum(2 * a.size * columns for a, _, _ in terms),
            sum(2 * (a.size + a.shape[0] * columns) for a, _, _ in terms) + 2 * owners * share * columns,
        ),
        name=name,
    )(*ins, *behind)


def joint_slope_kernel(count, owners_ref, *refs):
    near = jnp.concatenate([ref[...] for ref in refs[:count]], axis=1)
    far = jnp.concatenate([ref[...] for ref in refs[count : 2 * count]], axis=1)
    q_ref, k0_ref, k1_ref, v0_ref, v1_ref = refs[2 * count : 2 * count + 5]
    outs = refs[2 * count + 5 :]
    share = near.shape[1] // count
    totals = (
        tn(near, q_ref[...]),
        tn(near, k0_ref[...]) + tn(far, k1_ref[...]),
        tn(near, v0_ref[...]) + tn(far, v1_ref[...]),
    )
    for out0_ref, out1_ref, total in zip(outs[0::2], outs[1::2], totals):
        low = total.astype(BF16)
        first = pl.program_id(0) < pl.num_programs(0) // 2
        for ref, here in ((out0_ref, first), (out1_ref, jnp.logical_not(first))):

            @pl.when(here)
            def _():
                for index in range(count):
                    ref[index] = low[index * share : (index + 1) * share]


def joint_slope_call(owners, normals, grads, deps):
    total = owners.shape[0]
    rows, width = normals[0].shape
    share = width // total
    local = grads[0].shape[1]
    count = 2
    ins, specs = [], []
    for normal in normals:
        for index in range(count):
            ins.append(normal)
            specs.append(pl.BlockSpec((rows, share), functools.partial(lambda i, r, o: (0, o[count * r + i]), index)))
    for grad, row in ((grads[0], 0), (grads[1], 0), (grads[1], 1), (grads[2], 0), (grads[2], 1)):
        ins.append(grad)
        specs.append(pl.BlockSpec((rows, local), functools.partial(lambda i, r, o: (i, 0), row)))
    outs = pl.pallas_call(
        waiting(functools.partial(joint_slope_kernel, count), 1 + len(ins), deps),
        grid_spec=pltpu.PrefetchScalarGridSpec(
            num_scalar_prefetch=1,
            grid=(total // count,),
            in_specs=specs + anywhere(len(deps)),
            out_specs=halves_of(count, total // count // 2, share, local) * 3,
        ),
        out_shape=[shape_of(total // 2, share, local)] * 6,
        compiler_params=params_of(),
        cost_estimate=cost(10 * rows * width * local, 16 * rows * width),
        name="joint_slope",
    )(owners, *ins, *deps)
    return [(outs[2 * t], outs[2 * t + 1]) for t in range(3)]


def swap_core(shard):
    return lax.ppermute(shard, "tp", [(0, 1), (1, 0)])


def swap_ctx(shard, mask):
    return lax.ppermute(shard, "ctx", [(c, c ^ mask) for c in range(lax.axis_size("ctx"))])


def next_section(shard, by):
    size = lax.axis_size("section")
    return lax.ppermute(shard, "section", [(s, s + by) for s in range(size) if 0 <= s + by < size])


def mask_order(masks):
    order = [0]
    for mask in reversed(masks):
        order = order + [value ^ mask for value in order]
    return order


class Reduction:
    def __init__(self, kept, sent, masks):
        self.kept, self.masks = kept, list(masks)
        self.total = None
        self.sent = sent
        self.arrived = swap_ctx(sent, self.masks[0])

    def go_on(self):
        if self.total is not None:
            return self
        total = self.kept.astype(F32) + self.arrived.astype(F32)
        self.masks = self.masks[1:]
        if not self.masks:
            self.total = total[0]
            self.sent = self.arrived = self.total
            return self
        half = total.shape[0] // 2
        self.kept = total[:half].astype(BF16)
        self.sent = total[half:].astype(BF16)
        self.arrived = swap_ctx(self.sent, self.masks[0])
        return self


def on_device(
    tokens,
    cotangent,
    block_order,
    first_gain,
    first_bias,
    second_gain,
    second_bias,
    joint_weight,
    joint_bias,
    output_weight,
    output_bias,
    up_weight,
    up_bias,
    down_weight,
    down_bias,
):
    section = lax.axis_index("section")
    sections = lax.axis_size("section")
    ctx = lax.axis_index("ctx")
    ctx_size = lax.axis_size("ctx")
    core = lax.axis_index("tp")
    seqs, local_len, width = tokens.shape
    block = local_len // 2
    chips = ctx_size // seqs
    seq, member = ctx // chips, ctx % chips
    rows = seqs * block
    chip_rows = 2 * rows
    length = chips * chip_rows
    seq_masks = [chips << b for b in range((seqs - 1).bit_length())]
    member_masks = [1 << b for b in range((chips - 1).bit_length())]

    k, u, a = jnp.meshgrid(jnp.arange(chips), jnp.arange(2), jnp.arange(seqs), indexing="ij")
    stored = (2 * ((seq ^ a) * chips + (member ^ k)) + (core ^ u)).reshape(-1)
    places = block_order[stored]
    spots = (places[:, None] * block + jnp.arange(block, dtype=jnp.int32)).reshape(-1)
    exponent = jnp.arange(ROT // 2, dtype=F32) * (2.0 / ROT)
    inverse = jnp.power(jnp.float32(ROTARY_BASE), -exponent)
    turns = spots.astype(F32)[:, None] * inverse[None, :]
    cosine, sine = jnp.cos(turns), jnp.sin(turns)
    rest = jnp.zeros((length, HEAD - ROT), F32)
    table = (
        jnp.tile(jnp.concatenate([cosine, cosine, rest + 1.0], 1), (1, 128 // HEAD)),
        jnp.tile(jnp.concatenate([sine, sine, rest], 1), (1, 128 // HEAD)),
    )

    tile = max(block, 128)
    tile_places = places[: chip_rows // block].reshape(-1, tile // block)
    lowest, highest = jnp.min(tile_places, 1), jnp.max(tile_places, 1)
    limits = jnp.stack([(lowest * block + 1) // KEY_TILE, (highest * block + block - 1) // KEY_TILE + 1], 1)

    gain_one, shift_one, gain_two, shift_two = first_gain, first_bias, second_gain, second_bias
    w_joint, b_joint = joint_weight[0], joint_bias[0]
    w_output, b_output = output_weight[0], output_bias
    w_up, b_up = up_weight[0], up_bias
    w_down, b_down = down_weight[0], down_bias
    gains = jnp.concatenate([gain_one, gain_two], 0)
    norms = jnp.concatenate([gain_one, shift_one, gain_two, shift_two], 0)
    shifts = jnp.concatenate([b_output, b_down], 0)

    def plane_parts(values):
        mine = lax.dynamic_slice_in_dim(values, core * block, block, 1)
        return [lax.dynamic_index_in_dim(mine, seq ^ shift, 0, keepdims=False) for shift in range(seqs)]

    def from_planes(values):
        parts = values.reshape(seqs, block, width)
        return [parts[s] if s == 0 else swap_ctx(parts[s], s * chips) for s in range(seqs)]

    def in_order(parts):
        parts = jnp.stack(parts)
        both = jnp.stack([parts, swap_core(parts)], 1)
        ordered = [
            lax.dynamic_index_in_dim(lax.dynamic_index_in_dim(both, s ^ seq, 0, False), v ^ core, 0, False)
            for s in range(seqs)
            for v in range(2)
        ]
        return jnp.stack(ordered).reshape(1, seqs, local_len, width)

    def paired(parts):
        count = len(parts) // 2
        return tuple(x[0] if count == 1 else jnp.concatenate(x, 0) for x in (parts[:count], parts[count:]))

    def forward(own, save, moves, moved, name, number):
        chip = (own, swap_core(own))
        moves = [("ctx", k) for k in range(1, chips)] + moves
        outs, arrived = front_call(
            chip, norms, w_joint, b_joint, table, w_up, b_up, w_down, save, moves, [own] * (chips - 1) + moved, name, number
        )
        normal, keys, values, queries, ffn0, ffn1, *kept_ffn = outs
        others, arrived = arrived[: chips - 1], arrived[chips - 1 :]
        key_parts, value_parts, normal_parts = [keys], [values], [normal]
        if chips > 1:
            rest = paired([x for other in others for x in (other, swap_core(other))])
            far_normal, far_keys, far_values = joint_call(
                rest, gain_one, shift_one, w_joint, b_joint, table, chip_rows
            )
            key_parts.append(far_keys)
            value_parts.append(far_values)
            normal_parts.append(far_normal)
        attn0, attn1, mixture, lse = attend_call(queries, key_parts, value_parts, places, limits, w_output, block)
        result, moments = merge_call(own, (attn0, swap_core(attn1)), (ffn0, swap_core(ffn1)), shifts)
        return result, moments, (normal_parts, queries, key_parts, value_parts, mixture, lse, *kept_ffn), arrived

    def attention_back(g_pair, kept, deps=()):
        normal_parts, queries, key_parts, value_parts, mixture, lse, second_in, active, slope = kept
        return attend_back_call(
            queries, g_pair, mixture, lse, key_parts, value_parts, places, limits, w_output, table, block, deps
        )

    def far_back(d_keys, d_values, deps=()):
        if chips == 1:
            return []
        far = joint_back_call([d_keys, d_values], chip_rows, length - chip_rows, w_joint, deps)
        if chips > 2:
            far = jnp.concatenate(far, 0).reshape(chips - 1, 2, rows, width)
            far = far[:, 0], far[:, 1]
        sums = (far[0].astype(F32) + swap_core(far[1]).astype(F32)).astype(BF16).reshape(chips - 1, rows, width)
        return [sums[k - 1] for k in range(1, chips)]

    others = [("ctx", k) for k in range(1, chips)]
    planes = [("ctx", s * chips) for s in range(1, seqs)]
    token_parts = plane_parts(tokens)
    token_rows = jnp.concatenate([token_parts[0]] + [swap_ctx(token_parts[s], s * chips) for s in range(1, seqs)], 0)
    g_parts = plane_parts(cotangent)
    own = token_rows
    for tick in range(sections):
        first = tick == 0
        result, moments, kept, arrived = forward(
            own, tick == sections - 1, planes if first else [], g_parts[1:] if first else [], "front" + str(tick), tick
        )
        if first:
            g_rows = jnp.concatenate([g_parts[0], *arrived], 0)
        if tick < sections - 1:
            own = jnp.where(section == 0, token_rows, next_section(result, 1))
    out_parts = from_planes(result)
    moments = jnp.sum(moments[:3], axis=1)
    normal_parts, queries, key_parts, value_parts, mixture, lse, second_in, active, slope = kept
    g_own = g_rows
    for tick in range(sections - 1):
        g_pair = (g_own, swap_core(g_own))
        d_queries, d_keys, d_values, _ = attention_back(g_pair, kept)
        sums = far_back(d_keys, d_values, tuple(out_parts) if tick == 0 else ())
        near, second, arrivals = rear_call(
            (d_queries, d_keys, d_values), w_joint, g_pair, slope, w_up, w_down, others, sums, "rear" + str(tick), sections + tick
        )
        firsts = [near[0], swap_core(near[1]), *arrivals]
        d_own, _ = norm_back_call(own, g_own, firsts, [second[0], swap_core(second[1])], gains)
        g_own = jnp.where(section == sections - 1, g_rows, next_section(d_own, -1))
    section_out = in_order(out_parts)

    masks = member_masks + seq_masks
    owners = jnp.stack([ctx ^ m for m in mask_order(masks)]).astype(jnp.int32)
    local = w_output.shape[0]
    units = w_up.shape[1]
    share = width // ctx_size
    g_pair = (g_own, swap_core(g_own))
    by_blocks = share % 128 == 0 and chips == 2
    g_chip = g_pair if by_blocks else jnp.concatenate(g_pair, 0)
    if by_blocks:
        terms = [(g_pair[0], active, 0), (g_pair[1], active, 1)]
        slopes = slope_call(ctx_size, terms, 2 * units + local, 0, "down_slope")
        terms = [(g_pair[0], mixture, 0), (g_pair[1], mixture, 1)]
        slopes = slope_call(ctx_size, terms, 2 * units + local, 2 * units, "output_slope", slopes)
    second0, second1, d_hidden, up_sums = ffn_back_call(g_pair, slope, w_up, w_down, (slopes,) if by_blocks else ())
    if by_blocks:
        slopes = slope_call(ctx_size, [(second_in, d_hidden, 0)], 2 * units + local, units, "up_slope", slopes)
    else:
        pairs = ((g_chip, active), (second_in, d_hidden), (g_chip, mixture))
        slopes = jnp.concatenate([tn(a, b).astype(BF16).reshape(ctx_size, share, -1) for a, b in pairs], 2)
    slope_total = lax.psum_scatter(slopes, "ctx", scatter_dimension=0, tiled=False).astype(F32)
    d_queries, d_keys, d_values, joint_sums = attention_back(g_pair, kept, (slopes,))
    sums = far_back(d_keys, d_values)
    near = joint_back_call([d_queries, d_keys, d_values], 0, chip_rows, w_joint, tuple(sums))
    arrivals = [swap_ctx(part, k + 1) for k, part in enumerate(sums)]
    if by_blocks:
        halves = joint_slope_call(owners, normal_parts, (d_queries, d_keys, d_values), (near[0],))
    else:
        halves = []
        for grad in (d_queries, d_keys, d_values):
            piece = tn(normal_parts[0], grad[:chip_rows])
            if chips > 1 and grad is not d_queries:
                piece = piece + tn(normal_parts[1], grad[chip_rows:])
            piece = jnp.take(piece.astype(BF16).reshape(ctx_size, share, local), owners, axis=0)
            halves.append((piece[: ctx_size // 2], piece[ctx_size // 2 :]))
    joints = [Reduction(*pair, masks) for pair in halves]
    firsts = [near[0], swap_core(near[1]), *arrivals]
    seconds = [second0, swap_core(second1)]
    d_own, norm_sums = norm_back_call(own, g_own, firsts, seconds, gains, (joints[0].sent,))
    section_in_grad = in_order(from_planes(d_own))
    for _ in masks:
        for reduction in joints:
            reduction.go_on()
    down_total = slope_total[:, :units].T
    up_total = slope_total[:, units : 2 * units]
    output_total = slope_total[:, 2 * units :].T
    joint_total = jnp.stack([r.total for r in joints])

    both = jnp.concatenate([norm_sums[:5].reshape(-1), moments])
    both = both + swap_core(both)
    small = jnp.concatenate([both, joint_sums[:3].reshape(-1), up_sums.reshape(-1)])
    for mask in masks:
        small = small + swap_ctx(small, mask)
    norm_total = small[: 5 * width].reshape(5, 1, width)
    moment_total = small[5 * width : 5 * width + 3]
    joint_shift = small[5 * width + 3 : 5 * width + 3 + 3 * local].reshape(1, 3, local)
    up_shift = small[5 * width + 3 + 3 * local :].reshape(1, units)
    root_means = jnp.sqrt(moment_total / (length * seqs * width))
    return (
        section_out,
        section_in_grad,
        norm_total[0],
        norm_total[1],
        norm_total[2],
        norm_total[3],
        joint_total[None],
        joint_shift,
        output_total[None],
        norm_total[4],
        up_total[None],
        up_shift,
        down_total[None],
        norm_total[4],
        root_means[None],
    )


def solution(mesh):
    in_specs = (
        P(None, "ctx", None),
        P(None, "ctx", None),
        P(),
        P("section", None),
        P("section", None),
        P("section", None),
        P("section", None),
        P("section", None, None, "tp"),
        P("section", None, "tp"),
        P("section", "tp", None),
        P("section", None),
        P("section", None, "tp"),
        P("section", "tp"),
        P("section", "tp", None),
        P("section", None),
    )
    out_specs = (
        P("section", None, "ctx", None),
        P("section", None, "ctx", None),
        P("section", None),
        P("section", None),
        P("section", None),
        P("section", None),
        P("section", None, "ctx", "tp"),
        P("section", None, "tp"),
        P("section", "tp", "ctx"),
        P("section", None),
        P("section", "ctx", "tp"),
        P("section", "tp"),
        P("section", "tp", "ctx"),
        P("section", None),
        P("section", None),
    )
    return jax.shard_map(
        on_device, mesh=mesh, in_specs=in_specs, out_specs=out_specs, check_vma=False
    )
```

```python
import functools

import jax
import jax.numpy as jnp
from jax import lax
from jax.experimental import pallas as pl
from jax.experimental.pallas import tpu as pltpu
from jax.sharding import PartitionSpec as P

HEAD = 64
ROT = 16
EPS = 1e-05
ROTARY_BASE = 10000.0
NEGATIVE = -1e30
STACK = 4
GROUP = STACK * HEAD
KEY_TILE = 512
VMEM_LIMIT = 56 * 1024 * 1024
BF16 = jnp.bfloat16
F32 = jnp.float32


def dot(a, b):
    return jnp.dot(a, b, preferred_element_type=F32)


def dot_nt(a, b):
    return lax.dot_general(a, b, (((1,), (1,)), ((), ())), preferred_element_type=F32)


def params_of(**more):
    return pltpu.CompilerParams(vmem_limit_bytes=VMEM_LIMIT, **more)


def whole(shape):
    return pl.BlockSpec(shape, lambda *_: (0,) * len(shape))


def rows_of(tile, *rest):
    return pl.BlockSpec((tile, *rest), lambda r, *_: (r,) + (0,) * len(rest))


def halves_of(tile, count, *rest):
    return [
        pl.BlockSpec((tile, *rest), lambda r, *_: (jnp.minimum(r, count - 1),) + (0,) * len(rest)),
        pl.BlockSpec((tile, *rest), lambda r, *_: (jnp.maximum(r - count, 0),) + (0,) * len(rest)),
    ]


def pick(refs):
    return jnp.where(pl.program_id(0) < pl.num_programs(0) // 2, refs[0][...], refs[1][...])


def put(refs, value):
    first = pl.program_id(0) < pl.num_programs(0) // 2
    for ref, here in zip(refs, (first, jnp.logical_not(first))):

        @pl.when(here)
        def _():
            ref[...] = value


def waiting(kernel, inputs, deps):
    return lambda *refs: kernel(*refs[:inputs], *refs[inputs + len(deps) :])


def exchanged(position, mask):
    for bit in range(mask.bit_length()):
        if mask >> bit & 1:
            position = position + (1 << bit) - (2 << bit) * (position // (1 << bit) % 2)
    return position


def carrying(kernel, inputs, outputs, moves):
    count = len(moves)

    def body(*refs):
        sources = refs[inputs : inputs + count]
        outs = refs[inputs + count : inputs + count + outputs]
        targets = refs[inputs + count + outputs : inputs + 2 * count + outputs]
        *scratch, send, receive = refs[inputs + 2 * count + outputs :]
        partners = [{axis: exchanged(lax.axis_index(axis), mask)} for axis, mask in moves]
        copies = [
            pltpu.make_async_remote_copy(
                source, target, send.at[n], receive.at[n], device_id=partner, device_id_type=pl.DeviceIdType.MESH
            )
            for n, (source, target, partner) in enumerate(zip(sources, targets, partners))
        ]

        @pl.when(pl.program_id(0) == 0)
        def _():
            barrier = pltpu.get_barrier_semaphore()
            for partner in partners:
                pl.semaphore_signal(barrier, inc=1, device_id=partner, device_id_type=pl.DeviceIdType.MESH)
            pl.semaphore_wait(barrier, count)
            for copy in copies:
                copy.start()

        kernel(*refs[:inputs], *outs, *scratch)

        @pl.when(pl.program_id(0) == pl.num_programs(0) - 1)
        def _():
            for copy in copies:
                copy.wait()

    return body


def carrier_semaphores(count):
    return [pltpu.SemaphoreType.DMA((count,)), pltpu.SemaphoreType.DMA((count,))]


def anywhere(count):
    return [pl.BlockSpec(memory_space=pl.ANY)] * count


def cost(flops, size):
    return pl.CostEstimate(flops=int(flops), bytes_accessed=int(size), transcendentals=0)


def shape_of(*shape, dtype=BF16):
    return jax.ShapeDtypeStruct(shape, dtype)


def normalize(values):
    middle = jnp.mean(values, axis=-1, keepdims=True)
    centered = values - middle
    spread = jnp.mean(centered * centered, axis=-1, keepdims=True)
    inverse = lax.rsqrt(spread + EPS)
    return centered * inverse, inverse


def turn(values, cosine, sine):
    pieces = []
    for start in range(0, values.shape[1], 128):
        part = values[:, start : start + 128]
        ahead = pltpu.roll(part, 128 - ROT // 2, 1)
        behind = pltpu.roll(part, ROT // 2, 1)
        entry = lax.broadcasted_iota(jnp.int32, part.shape, 1) % HEAD
        pieces.append(part * cosine + jnp.where(entry < ROT // 2, -ahead, behind) * sine)
    return jnp.concatenate(pieces, axis=1)


def joint_kernel(h0_ref, h1_ref, gain_ref, shift_ref, w_ref, b_ref, cos_ref, sin_ref, n_ref, k_ref, v_ref):
    scaled, _ = normalize(pick((h0_ref, h1_ref)).astype(F32))
    low = (scaled * gain_ref[...] + shift_ref[...]).astype(BF16)
    n_ref[...] = low
    cosine, sine = cos_ref[...], sin_ref[...]
    keys = dot(low, w_ref[1]) + b_ref[1:2]
    values = dot(low, w_ref[2]) + b_ref[2:3]
    k_ref[...] = turn(keys, cosine, sine).astype(BF16)
    v_ref[...] = values.astype(BF16)


def joint_call(pair, gain, shift, w_joint, b_joint, table, offset, deps=()):
    rows, width = pair[0].shape
    local = w_joint.shape[2]
    tile = min(512, rows)
    first = offset // tile
    count = 2
    turns = pl.BlockSpec((tile, 128), lambda r: (first + r, 0))
    return pl.pallas_call(
        waiting(joint_kernel, 8, deps),
        grid=(2 * rows // tile,),
        in_specs=halves_of(tile, rows // tile, width)
        + [whole((1, width)), whole((1, width)), whole(w_joint.shape), whole(b_joint.shape), turns, turns]
        + anywhere(len(deps)),
        out_specs=[rows_of(tile, width)] + [rows_of(tile, local)] * count,
        out_shape=[shape_of(2 * rows, width)] + [shape_of(2 * rows, local)] * count,
        compiler_params=params_of(),
        cost_estimate=cost(4 * rows * width * local * count, 8 * rows * width + 2 * w_joint.size),
        name="joint_projection",
    )(*pair, gain, shift, w_joint, b_joint, *table, *deps)


def gelu_parts(x):
    return 0.5 + 0.5 * lax.erf(x * 0.5**0.5), jnp.exp(-0.5 * x * x)


def front_kernel(
    save, h0_ref, h1_ref, norms_ref, w_ref, b_ref, cos_ref, sin_ref, up_ref, up_b_ref, down_ref,
    n_ref, k_ref, v_ref, q_ref, part0_ref, part1_ref, *saved
):
    scaled, _ = normalize(pick((h0_ref, h1_ref)).astype(F32))
    low = (scaled * norms_ref[0:1] + norms_ref[1:2]).astype(BF16)
    n_ref[...] = low
    cosine, sine = cos_ref[...], sin_ref[...]
    keys = dot(low, w_ref[1]) + b_ref[1:2]
    values = dot(low, w_ref[2]) + b_ref[2:3]
    queries = dot(low, w_ref[0]) + b_ref[0:1]
    q_ref[...] = (turn(queries, cosine, sine) * HEAD ** (-0.5)).astype(BF16)
    k_ref[...] = turn(keys, cosine, sine).astype(BF16)
    v_ref[...] = values.astype(BF16)
    low = (scaled * norms_ref[2:3] + norms_ref[3:4]).astype(BF16)
    if save:
        saved[0][...] = low
    total = None
    for start in range(0, up_ref.shape[1], 512):
        cut = pl.ds(start, 512)
        hidden = dot(low, up_ref[:, cut]) + up_b_ref[:, cut]
        share, bell = gelu_parts(hidden)
        active = (hidden * share).astype(BF16)
        if save:
            saved[1][:, cut] = active
            saved[2][:, cut] = (share + hidden * bell * 0.3989422804014327).astype(BF16)
        term = dot(active, down_ref[cut, :])
        total = term if total is None else total + term
    put((part0_ref, part1_ref), total.astype(BF16))


def front_call(pair, norms, w_joint, b_joint, table, w_up, b_up, w_down, save, moves, moved, name, number):
    rows, width = pair[0].shape
    local = w_joint.shape[2]
    units = w_up.shape[1]
    tile = min(512, rows)
    out = [shape_of(2 * rows, width)] + [shape_of(2 * rows, local)] * 3 + [shape_of(rows, width)] * 2
    out_specs = [rows_of(tile, width)] + [rows_of(tile, local)] * 3 + halves_of(tile, rows // tile, width)
    if save:
        out += [shape_of(2 * rows, width)] + [shape_of(2 * rows, units)] * 2
        out_specs += [rows_of(tile, width), rows_of(tile, units), rows_of(tile, units)]
    ins = (norms, w_joint, b_joint, *table, w_up, b_up, w_down)
    turns = rows_of(tile, 128)
    specs = [turns if x is table[0] or x is table[1] else whole(x.shape) for x in ins]
    outs = pl.pallas_call(
        carrying(functools.partial(front_kernel, save), 2 + len(ins), len(out), moves),
        grid=(2 * rows // tile,),
        in_specs=halves_of(tile, rows // tile, width) + specs + anywhere(len(moves)),
        out_specs=out_specs + anywhere(len(moves)),
        out_shape=out + [shape_of(*x.shape) for x in moved],
        scratch_shapes=carrier_semaphores(len(moves)),
        compiler_params=params_of(collective_id=number, has_side_effects=True),
        cost_estimate=cost(4 * rows * width * (3 * local + 2 * units), 4 * w_up.size + 16 * rows * width),
        name=name,
    )(*pair, *ins, *moved)
    return outs[: len(out)], outs[len(out) :]


def ffn_back_kernel(g0_ref, g1_ref, slope_ref, up_ref, down_ref, part0_ref, part1_ref, hidden_ref, sums_ref):
    upstream = pick((g0_ref, g1_ref))
    units = up_ref.shape[1]

    @pl.when(pl.program_id(0) == 0)
    def _():
        sums_ref[...] = jnp.zeros_like(sums_ref)

    total = None
    for start in range(0, units, 512):
        cut = pl.ds(start, 512)
        d_active = dot_nt(upstream, down_ref[cut, :])
        d_hidden = (d_active * slope_ref[:, cut].astype(F32)).astype(BF16)
        hidden_ref[:, cut] = d_hidden
        sums_ref[:, cut] += jnp.sum(d_hidden.astype(F32), axis=0, keepdims=True)
        term = dot_nt(d_hidden, up_ref[:, cut])
        total = term if total is None else total + term
    put((part0_ref, part1_ref), total.astype(BF16))


def ffn_back_call(pair, slope, w_up, w_down, deps=()):
    rows, width = pair[0].shape
    units = w_up.shape[1]
    tile = min(512, rows)
    return pl.pallas_call(
        waiting(ffn_back_kernel, 5, deps),
        grid=(2 * rows // tile,),
        in_specs=halves_of(tile, rows // tile, width) + [rows_of(tile, units), whole(w_up.shape), whole(w_down.shape)]
        + anywhere(len(deps)),
        out_specs=halves_of(tile, rows // tile, width) + [rows_of(tile, units), whole((1, units))],
        out_shape=[shape_of(rows, width)] * 2 + [shape_of(2 * rows, units), shape_of(1, units, dtype=F32)],
        compiler_params=params_of(),
        cost_estimate=cost(8 * rows * width * units, 4 * w_up.size + 8 * rows * (width + units)),
        name="feed_forward_back",
    )(*pair, slope, w_up, w_down, *deps)


def start_sorted(places_ref, parts, targets, sem, block):
    copies = []
    for refs, target in zip(parts, targets):
        index = 0
        for ref in refs:
            for local in range(ref.shape[0] // block):
                place = pl.ds(pl.multiple_of(places_ref[index] * block, block), block)
                copies.append(pltpu.make_async_copy(ref.at[pl.ds(local * block, block)], target.at[place], sem))
                index += 1
    for copy in copies:
        copy.start()
    return copies


def transpose_into(source, target):
    rows, columns = source.shape

    def step(index, _):
        start = pl.multiple_of(index * 256, 256)
        for column in range(0, columns, 256):
            target[column : column + 256, pl.ds(start, 256)] = source[pl.ds(start, 256), column : column + 256].T
        return 0

    lax.fori_loop(0, rows // 256, step, 0)


def stacked(values):
    owner = lax.broadcasted_iota(jnp.int32, values.shape, 1) // HEAD
    zero = jnp.zeros_like(values)
    return jnp.concatenate([jnp.where(owner == a, values, zero) for a in range(STACK)], axis=0)


def spots_of(places_ref, step, tile, block, shape, axis):
    at = lax.broadcasted_iota(jnp.int32, shape, axis) % tile
    count = tile // block
    spot = at + places_ref[step * count] * block
    for s in range(1, count):
        spot = jnp.where(at >= s * block, at - s * block + places_ref[step * count + s] * block, spot)
    return spot


def attend_kernel(block, tile, remote, places_ref, limits_ref, q_ref, wo_ref, *refs):
    key_refs, value_refs = refs[: 1 + remote], refs[1 + remote : 2 + 2 * remote]
    part0_ref, part1_ref, mix_ref, lse_ref, keys, values, scores_ref, sem = refs[2 + 2 * remote :]
    groups = q_ref.shape[1] // GROUP
    half = part0_ref.shape[0]
    rows = STACK * tile
    lanes = [slice(g * GROUP, (g + 1) * GROUP) for g in range(groups)]
    for copy in start_sorted(places_ref, (key_refs, value_refs), (keys, values), sem, block):
        copy.wait()

    def tile_step(step, _):
        mine = pl.ds(pl.multiple_of(step * tile, tile), tile)
        heads = [stacked(q_ref[mine, lane]) for lane in lanes]
        spots = spots_of(places_ref, step, tile, block, (rows, 128), 0)

        def attend_to(count):
            open_end = (count - 1) * KEY_TILE if tile == block else 0
            tops = []
            for g, lane in enumerate(lanes):
                top = None
                for start in range(0, count * KEY_TILE, KEY_TILE):
                    scores = dot_nt(heads[g], keys[start : start + KEY_TILE, lane])
                    for column in range(0, KEY_TILE, 128):
                        piece = scores[:, column : column + 128]
                        if start + column >= open_end:
                            spot = start + column + lax.broadcasted_iota(jnp.int32, piece.shape, 1)
                            piece = jnp.where(spot <= spots, piece, NEGATIVE)
                        scores_ref[g, :, start + column : start + column + 128] = piece
                        top = piece if top is None else jnp.maximum(top, piece)
                tops.append(jnp.broadcast_to(jnp.max(top, axis=1, keepdims=True), (rows, 128)))
            for g, lane in enumerate(lanes):
                mass, total = None, None
                for start in range(0, count * KEY_TILE, KEY_TILE):
                    raised = []
                    for column in range(start, start + KEY_TILE, 128):
                        piece = jnp.exp(scores_ref[g, :, column : column + 128] - tops[g])
                        mass = piece if mass is None else mass + piece
                        raised.append(piece.astype(BF16))
                    term = dot(jnp.concatenate(raised, axis=1), values[start : start + KEY_TILE, lane])
                    total = term if total is None else total + term
                mass = jnp.broadcast_to(jnp.sum(mass, axis=1, keepdims=True), (rows, 128))
                total = total * jnp.concatenate([1.0 / mass] * (GROUP // 128), axis=1)
                owner = lax.broadcasted_iota(jnp.int32, (tile, GROUP), 1) // HEAD
                mixture = total[:tile]
                for a in range(1, STACK):
                    mixture = jnp.where(owner == a, total[a * tile : (a + 1) * tile], mixture)
                mix_ref[mine, lane] = mixture.astype(BF16)
                lse = tops[g] + jnp.log(mass)
                for a in range(STACK):
                    lse_ref[step, g : g + 1, a * tile : (a + 1) * tile] = lse[a * tile : (a + 1) * tile].T[0:1]

        for count in range(1, keys.shape[0] // KEY_TILE + 1):
            pl.when(limits_ref[step, 1] == count)(functools.partial(attend_to, count))
        return 0

    lax.fori_loop(0, q_ref.shape[0] // tile, tile_step, 0)
    part0_ref[...] = dot(mix_ref[:half], wo_ref[...]).astype(BF16)
    part1_ref[...] = dot(mix_ref[half:], wo_ref[...]).astype(BF16)


def attend_call(queries, key_parts, value_parts, places, limits, w_output, block, deps=()):
    rows, local = queries.shape
    width = w_output.shape[1]
    tile = rows // limits.shape[0]
    length = sum(part.shape[0] for part in key_parts)
    groups = local // GROUP
    outs = [(rows // 2, width), (rows // 2, width), (rows, local), (rows // tile, groups, STACK * tile)]
    return pl.pallas_call(
        waiting(functools.partial(attend_kernel, block, tile, len(key_parts) - 1), 4 + 2 * len(key_parts), deps),
        grid_spec=pltpu.PrefetchScalarGridSpec(
            num_scalar_prefetch=2,
            grid=(1,),
            in_specs=[whole((rows, local)), whole(w_output.shape)] + anywhere(2 * len(key_parts) + len(deps)),
            out_specs=[whole(shape) for shape in outs],
            scratch_shapes=[
                pltpu.VMEM((length, local), BF16),
                pltpu.VMEM((length, local), BF16),
                pltpu.VMEM((groups, STACK * tile, length), F32),
                pltpu.SemaphoreType.DMA,
            ],
        ),
        out_shape=[shape_of(*shape) for shape in outs[:3]] + [shape_of(*outs[3], dtype=F32)],
        compiler_params=params_of(),
        cost_estimate=cost(12 * rows * length * local, 2 * length * local * 4),
        name="attend",
    )(places, limits, queries, w_output, *key_parts, *value_parts, *deps)


def attend_back_kernel(
    block, tile, remote, places_ref, limits_ref, q_ref, g0_ref, g1_ref, mix_ref, lse_ref, wo_ref, cos_ref, sin_ref, *refs
):
    key_refs, value_refs = refs[: 1 + remote], refs[1 + remote : 2 + 2 * remote]
    (dq_ref, dk_ref, dv_ref, sums_ref, keys, values, keys_t, d_keys, d_values, d_mixture, inner, total, d_queries, sem) = refs[
        2 + 2 * remote :
    ]
    groups = q_ref.shape[1] // GROUP
    rows = q_ref.shape[0]
    half = g0_ref.shape[0]
    lanes = [slice(g * GROUP, (g + 1) * GROUP) for g in range(groups)]
    copies = start_sorted(places_ref, (key_refs, value_refs), (keys, values), sem, block)
    d_keys[...] = jnp.zeros_like(d_keys)
    d_values[...] = jnp.zeros_like(d_values)
    head_of = lax.broadcasted_iota(jnp.int32, (8, GROUP), 1) // HEAD
    picker = jnp.where(lax.broadcasted_iota(jnp.int32, (8, GROUP), 0) == head_of, 1.0, 0.0).astype(BF16)
    for index, ref in enumerate((g0_ref, g1_ref)):
        cut = pl.ds(index * half, half)
        low = dot_nt(ref[...], wo_ref[...]).astype(BF16)
        d_mixture[cut, :] = low
        product = low.astype(F32) * mix_ref[cut, :].astype(F32)
        high = product.astype(BF16)
        rest = (product - high.astype(F32)).astype(BF16)
        for g, lane in enumerate(lanes):
            inner[g * 8 : (g + 1) * 8, cut] = dot_nt(picker, high[:, lane]) + dot_nt(picker, rest[:, lane])
    for copy in copies:
        copy.wait()
    transpose_into(keys, keys_t)

    def query_step(step, _):
        mine = pl.ds(pl.multiple_of(step * tile, tile), tile)
        spots = spots_of(places_ref, step, tile, block, (1, STACK * tile), 1)
        heads = [stacked(q_ref[mine, lane]) for lane in lanes]
        sides = [stacked(d_mixture[mine, lane]) for lane in lanes]
        sums = [
            jnp.concatenate([inner[g * 8 + a : g * 8 + a + 1, mine] for a in range(STACK)], axis=1) for g in range(groups)
        ]
        lse = [lse_ref[step, g : g + 1, :] for g in range(groups)]
        total[...] = jnp.zeros_like(total)

        def key_step(masked, index, carry):
            start = pl.multiple_of(index * KEY_TILE, KEY_TILE)
            cut = pl.ds(start, KEY_TILE)
            for g, lane in enumerate(lanes):
                scores = dot_nt(keys[cut, lane], heads[g])
                if masked:
                    spot = start + lax.broadcasted_iota(jnp.int32, scores.shape, 0)
                    scores = jnp.where(spot <= spots, scores, NEGATIVE)
                weights = jnp.exp(scores - lse[g])
                d_weights = dot_nt(values[cut, lane], sides[g])
                d_scores = (weights * (d_weights - sums[g])).astype(BF16)
                d_values[cut, lane] += dot(weights.astype(BF16), sides[g])
                d_keys[cut, lane] += dot(d_scores, heads[g])
                total[lane, :] += dot(keys_t[lane, cut], d_scores)
            return carry

        lax.fori_loop(0, limits_ref[step, 0], functools.partial(key_step, False), 0)
        lax.fori_loop(limits_ref[step, 0], limits_ref[step, 1], functools.partial(key_step, True), 0)
        for lane in lanes:
            picked = [total[lane, :][a * HEAD : (a + 1) * HEAD, a * tile : (a + 1) * tile] for a in range(STACK)]
            d_queries[mine, lane] = jnp.concatenate(picked, axis=0).T
        return 0

    lax.fori_loop(0, rows // tile, query_step, 0)
    turned = turn(d_queries[...] * HEAD ** (-0.5), cos_ref[:rows], -sin_ref[:rows]).astype(BF16)
    dq_ref[...] = turned
    sums_ref[...] = jnp.zeros_like(sums_ref)
    sums_ref[0:1, :] = jnp.sum(turned.astype(F32), axis=0, keepdims=True)

    def block_step(index, _):
        place = pl.ds(pl.multiple_of(places_ref[index] * block, block), block)
        mine = pl.ds(pl.multiple_of(index * block, block), block)
        turned = turn(d_keys[place, :], cos_ref[mine, :], -sin_ref[mine, :]).astype(BF16)
        dk_ref[mine, :] = turned
        low = d_values[place, :].astype(BF16)
        dv_ref[mine, :] = low
        sums_ref[1:2, :] += jnp.sum(turned.astype(F32), axis=0, keepdims=True)
        sums_ref[2:3, :] += jnp.sum(low.astype(F32), axis=0, keepdims=True)
        return 0

    lax.fori_loop(0, dk_ref.shape[0] // block, block_step, 0)


def attend_back_call(
    queries, g_pair, mixture, lse, key_parts, value_parts, places, limits, w_output, table, block, deps=()
):
    rows, local = queries.shape
    width = w_output.shape[1]
    tile = rows // limits.shape[0]
    length = sum(part.shape[0] for part in key_parts)
    groups = local // GROUP
    ins = (queries, *g_pair, mixture, lse, w_output, *table)
    return pl.pallas_call(
        waiting(
            functools.partial(attend_back_kernel, block, tile, len(key_parts) - 1), 2 + len(ins) + 2 * len(key_parts), deps
        ),
        grid_spec=pltpu.PrefetchScalarGridSpec(
            num_scalar_prefetch=2,
            grid=(1,),
            in_specs=[whole(x.shape) for x in ins] + anywhere(2 * len(key_parts) + len(deps)),
            out_specs=[whole((rows, local)), whole((length, local)), whole((length, local)), whole((8, local))],
            scratch_shapes=[
                pltpu.VMEM((length, local), BF16),
                pltpu.VMEM((length, local), BF16),
                pltpu.VMEM((local, length), BF16),
                pltpu.VMEM((length, local), F32),
                pltpu.VMEM((length, local), F32),
                pltpu.VMEM((rows, local), BF16),
                pltpu.VMEM((8 * groups, rows), F32),
                pltpu.VMEM((local, STACK * tile), F32),
                pltpu.VMEM((rows, local), F32),
                pltpu.SemaphoreType.DMA,
            ],
        ),
        out_shape=[shape_of(rows, local), shape_of(length, local), shape_of(length, local), shape_of(8, local, dtype=F32)],
        compiler_params=params_of(),
        cost_estimate=cost(24 * rows * length * local, 2 * length * local * 8),
        name="attend_back",
    )(places, limits, *ins, *key_parts, *value_parts, *deps)


def joint_back_kernel(count, *refs):
    w_ref = refs[count]
    total = None
    for index in range(count):
        term = dot_nt(refs[index][...], w_ref[3 - count + index])
        total = term if total is None else total + term
    put(refs[count + 1 :], total.astype(BF16))


def joint_back_call(grads, offset, rows, w_joint, deps=()):
    width, local = w_joint.shape[1:]
    half = rows // 2
    tile = min(512, half)
    first = offset // tile
    return pl.pallas_call(
        waiting(functools.partial(joint_back_kernel, len(grads)), len(grads) + 1, deps),
        grid=(rows // tile,),
        in_specs=[pl.BlockSpec((tile, local), lambda r: (first + r, 0))] * len(grads)
        + [whole(w_joint.shape)]
        + anywhere(len(deps)),
        out_specs=halves_of(tile, half // tile, width),
        out_shape=[shape_of(half, width)] * 2,
        compiler_params=params_of(),
        cost_estimate=cost(2 * rows * width * local * len(grads), 2 * rows * (width + 3 * local) + 2 * w_joint.size),
        name="joint_projection_back",
    )(*grads, w_joint, *deps)


def rear_kernel(q_ref, k_ref, v_ref, w_ref, g0_ref, g1_ref, slope_ref, up_ref, down_ref, first0_ref, first1_ref, part0_ref, part1_ref):
    total = dot_nt(q_ref[...], w_ref[0]) + dot_nt(k_ref[...], w_ref[1]) + dot_nt(v_ref[...], w_ref[2])
    put((first0_ref, first1_ref), total.astype(BF16))
    upstream = pick((g0_ref, g1_ref))
    total = None
    for start in range(0, up_ref.shape[1], 512):
        cut = pl.ds(start, 512)
        d_active = dot_nt(upstream, down_ref[cut, :])
        d_hidden = (d_active * slope_ref[:, cut].astype(F32)).astype(BF16)
        term = dot_nt(d_hidden, up_ref[:, cut])
        total = term if total is None else total + term
    put((part0_ref, part1_ref), total.astype(BF16))


def rear_call(grads, w_joint, pair, slope, w_up, w_down, moves, moved, name, number):
    rows, width = pair[0].shape
    local = w_joint.shape[2]
    units = w_up.shape[1]
    tile = min(512, rows)
    halves = halves_of(tile, rows // tile, width)
    outs = pl.pallas_call(
        carrying(rear_kernel, 9, 4, moves),
        grid=(2 * rows // tile,),
        in_specs=[rows_of(tile, local)] * 3
        + [whole(w_joint.shape)]
        + halves
        + [rows_of(tile, units), whole(w_up.shape), whole(w_down.shape)]
        + anywhere(len(moves)),
        out_specs=halves + halves + anywhere(len(moves)),
        out_shape=[shape_of(rows, width)] * 4 + [shape_of(*x.shape) for x in moved],
        scratch_shapes=carrier_semaphores(len(moves)),
        compiler_params=params_of(collective_id=number, has_side_effects=True),
        cost_estimate=cost(4 * rows * width * (3 * local + 2 * units), 4 * w_up.size + 16 * rows * width),
        name=name,
    )(*grads, w_joint, *pair, slope, w_up, w_down, *moved)
    return outs[:2], outs[2:4], outs[4:]


def norm_back_kernel(firsts, h_ref, g_ref, gains_ref, *refs):
    first_refs, second_refs, (out_ref, sums_ref) = refs[:firsts], refs[firsts:-2], refs[-2:]

    @pl.when(pl.program_id(0) == 0)
    def _():
        sums_ref[...] = jnp.zeros_like(sums_ref)

    scaled, inverse = normalize(h_ref[...].astype(F32))
    upstream = g_ref[...].astype(F32)
    d_first = sum(ref[...].astype(F32) for ref in first_refs)
    d_second = sum(ref[...].astype(F32) for ref in second_refs)
    for row, term in enumerate((d_first * scaled, d_first, d_second * scaled, d_second, upstream)):
        sums_ref[row : row + 1, :] += jnp.sum(term, axis=0, keepdims=True)
    d_scaled = d_first * gains_ref[0:1] + d_second * gains_ref[1:2]
    middle = jnp.mean(d_scaled, axis=-1, keepdims=True)
    along = jnp.mean(d_scaled * scaled, axis=-1, keepdims=True)
    out_ref[...] = (upstream + inverse * (d_scaled - middle - scaled * along)).astype(BF16)


def norm_back_call(h, g, firsts, seconds, gains, deps=()):
    rows, width = h.shape
    tile = min(128, rows)
    one = rows_of(tile, width)
    return pl.pallas_call(
        waiting(functools.partial(norm_back_kernel, len(firsts)), 3 + len(firsts) + len(seconds), deps),
        grid=(rows // tile,),
        in_specs=[one, one, whole(gains.shape)] + [one] * (len(firsts) + len(seconds)) + anywhere(len(deps)),
        out_specs=[one, whole((8, width))],
        out_shape=[shape_of(rows, width), shape_of(8, width, dtype=F32)],
        compiler_params=params_of(),
        cost_estimate=cost(20 * rows * width, 2 * rows * width * 8),
        name="norm_back",
    )(h, g, gains, *firsts, *seconds, *deps)


def merge_kernel(h_ref, a0_ref, a1_ref, f0_ref, f1_ref, shifts_ref, out_ref, sums_ref):
    @pl.when(pl.program_id(0) == 0)
    def _():
        sums_ref[...] = jnp.zeros_like(sums_ref)

    state = h_ref[...].astype(F32)
    attention = a0_ref[...].astype(F32) + a1_ref[...].astype(F32) + shifts_ref[0:1]
    feedforward = f0_ref[...].astype(F32) + f1_ref[...].astype(F32) + shifts_ref[1:2]
    out_ref[...] = (state + attention + feedforward).astype(BF16)
    for row, term in enumerate((state, attention, feedforward)):
        sums_ref[row : row + 1, :] += jnp.sum(term * term, axis=0, keepdims=True)


def merge_call(h, attn_pair, ffn_pair, shifts, deps=()):
    rows, width = h.shape
    tile = min(128, rows)
    one = rows_of(tile, width)
    return pl.pallas_call(
        waiting(merge_kernel, 6, deps),
        grid=(rows // tile,),
        in_specs=[one] * 5 + [whole(shifts.shape)] + anywhere(len(deps)),
        out_specs=[one, whole((8, width))],
        out_shape=[shape_of(rows, width), shape_of(8, width, dtype=F32)],
        compiler_params=params_of(),
        cost_estimate=cost(10 * rows * width, 2 * rows * width * 6),
        name="merge",
    )(h, *attn_pair, *ffn_pair, shifts, *deps)


def tn(a, b):
    return lax.dot_general(a, b, (((0,), (0,)), ((), ())), preferred_element_type=F32)


def slope_kernel(count, terms, owners_ref, *refs):
    lefts = [jnp.concatenate([ref[...] for ref in refs[t * count : (t + 1) * count]], axis=1) for t in range(terms)]
    rights = refs[terms * count : terms * (count + 1)]
    outs = refs[terms * (count + 1) :]
    share = lefts[0].shape[1] // count
    total = sum(tn(left, right[...]) for left, right in zip(lefts, rights)).astype(BF16)
    first = pl.program_id(0) < pl.num_programs(0) // 2
    for ref, here in zip(outs, (first, jnp.logical_not(first))):

        @pl.when(here)
        def _():
            for index in range(count):
                ref[index] = total[index * share : (index + 1) * share]


def slope_call(owners, terms, name, cut=(0, 1), deps=()):
    total = owners.shape[0]
    share = terms[0][0].shape[1] // total
    columns = terms[0][1].shape[1] // cut[1]
    count = 4
    if share % 128 or total % (2 * count):
        pieces = 0.0
        row = 0
        for left, right, _ in terms:
            left_ordered = jnp.take(left.reshape(left.shape[0], total, share), owners, axis=1).reshape(left.shape)
            part = right[row : row + left.shape[0], cut[0] * columns : (cut[0] + 1) * columns]
            row += left.shape[0]
            pieces = pieces + tn(left_ordered, part)
        pieces = pieces.astype(BF16).reshape(total, share, columns)
        return pieces[: total // 2], pieces[total // 2 :]
    steps = total // count
    ins, specs = [], []
    for left, _, _ in terms:
        for index in range(count):
            ins.append(left)
            specs.append(
                pl.BlockSpec((left.shape[0], share), functools.partial(lambda i, r, o: (0, o[count * r + i]), index))
            )
    for left, right, row in terms:
        ins.append(right)
        specs.append(
            pl.BlockSpec((left.shape[0], columns), functools.partial(lambda i, r, o: (i, cut[0]), row))
        )
    return pl.pallas_call(
        waiting(functools.partial(slope_kernel, count, len(terms)), 1 + len(ins), deps),
        grid_spec=pltpu.PrefetchScalarGridSpec(
            num_scalar_prefetch=1,
            grid=(steps,),
            in_specs=specs + anywhere(len(deps)),
            out_specs=halves_of(count, steps // 2, share, columns),
        ),
        out_shape=[shape_of(total // 2, share, columns)] * 2,
        compiler_params=params_of(),
        cost_estimate=cost(
            sum(2 * a.size * columns for a, _, _ in terms),
            sum(2 * (a.size + a.shape[0] * columns) for a, _, _ in terms) + 2 * total * share * columns,
        ),
        name=name,
    )(owners, *ins, *deps)


def joint_rear_kernel(masks, q_ref, k_ref, v_ref, w_ref, near_ref, far_ref, first0_ref, first1_ref, *outs):
    rows = q_ref.shape[0]
    half = rows // 2
    share = near_ref.shape[1] >> len(masks)
    grads = (q_ref[...], k_ref[:rows], v_ref[:rows])
    for ref, cut in ((first0_ref, slice(0, half)), (first1_ref, slice(half, rows))):
        total = sum(dot_nt(grad[cut], w_ref[t]) for t, grad in enumerate(grads))
        ref[...] = total.astype(BF16)
    me = lax.axis_index("ctx")
    order = mask_order(masks)
    count = 2
    for start in range(0, len(order), count):
        spots = [pl.ds(pl.multiple_of(exchanged(me, m) * share, share), share) for m in order[start : start + count]]
        near = jnp.concatenate([near_ref[:, spot] for spot in spots], axis=1)
        far = jnp.concatenate([far_ref[:, spot] for spot in spots], axis=1)
        totals = (tn(near, grads[0]), tn(near, grads[1]) + tn(far, k_ref[rows:]), tn(near, grads[2]) + tn(far, v_ref[rows:]))
        for t, total in enumerate(totals):
            low = total.astype(BF16)
            for index in range(count):
                piece = start + index
                sent, place = divmod(piece, len(order) // 2)
                outs[2 * t + sent][place] = low[index * share : (index + 1) * share]


def joint_rear_call(grads, w_joint, normals, masks, moves, moved, name, number):
    rows, local = grads[0].shape
    width = w_joint.shape[1]
    total = 1 << len(masks)
    ins = (*grads, w_joint, *normals)
    out = [shape_of(rows // 2, width)] * 2 + [shape_of(total // 2, width // total, local)] * 6
    outs = pl.pallas_call(
        carrying(functools.partial(joint_rear_kernel, masks), len(ins), len(out), moves),
        grid=(1,),
        in_specs=[whole(x.shape) for x in ins] + anywhere(len(moves)),
        out_specs=[whole(x.shape) for x in out] + anywhere(len(moves)),
        out_shape=out + [shape_of(*x.shape) for x in moved],
        scratch_shapes=carrier_semaphores(len(moves)),
        compiler_params=params_of(collective_id=number, has_side_effects=True),
        cost_estimate=cost(16 * rows * width * local, 16 * rows * width),
        name=name,
    )(*ins, *moved)
    return outs[:2], [outs[2 + 2 * t : 4 + 2 * t] for t in range(3)], outs[8:]


def finish_kernel(chains, events, seqs, chips, core_words, *refs):
    count = len(chains)
    ins, refs = refs[: 2 * count], refs[2 * count :]
    d_own_ref, words_ref = refs[:2]
    totals, home_ref, words_out = refs[2 : 2 + count], refs[2 + count], refs[3 + count]
    refs = list(refs[4 + count :])
    current = [refs.pop(0) for _ in chains]
    slots = [[refs.pop(0) for _ in chain[0]] for chain in chains]
    words, other_words, chain_send, chain_receive, home_send, home_receive, word_send, word_receive, local = refs
    me, core = lax.axis_index("ctx"), lax.axis_index("tp")
    size = words.shape[0]
    seq = me // chips
    block = home_ref.shape[2]

    def at_ctx(mask):
        return {"ctx": exchanged(me, mask)}

    other_core = {"tp": 1 - core}

    def remote(source, target, send, receive, device):
        return pltpu.make_async_remote_copy(
            source, target, send, receive, device_id=device, device_id_type=pl.DeviceIdType.MESH
        )

    barrier = pltpu.get_barrier_semaphore()
    for mask in range(1, size):
        pl.semaphore_signal(barrier, inc=1, device_id=at_ctx(mask), device_id_type=pl.DeviceIdType.MESH)
    pl.semaphore_signal(barrier, inc=1, device_id=other_core, device_id_type=pl.DeviceIdType.MESH)
    pl.semaphore_wait(barrier, size)

    started = []

    def begin(copy):
        copy.start()
        started.append(copy)
        return copy

    word_copies = [
        begin(remote(words_ref, words.at[me], word_send.at[mask], word_receive.at[mask], at_ctx(mask)))
        for mask in range(1, size)
    ]
    steps = [0] * count
    running = [None] * count
    number = [sum(len(chain[0]) for chain in chains[:c]) for c in range(count)]

    def launch(c, source):
        masks = chains[c][0]
        step = steps[c]
        n = number[c] + step
        running[c] = begin(
            remote(source, slots[c][step], chain_send.at[n], chain_receive.at[n], at_ctx(masks[step]))
        )

    def split(c):
        pieces = current[c].shape[0] >> (steps[c] + (0 if chains[c][1] else -1))
        launch(c, current[c].at[pl.ds(pieces // 2, pieces // 2)])

    home = []

    def send_home():
        copy = pltpu.make_async_copy(d_own_ref.at[pl.ds(0, block)], home_ref.at[seq, core], local)
        copy.start()
        for s in range(1, seqs):
            home.append(
                begin(
                    remote(
                        d_own_ref.at[pl.ds(s * block, block)], home_ref.at[seq, core],
                        home_send.at[s], home_receive.at[s], at_ctx(s * chips),
                    )
                )
            )
        copy.wait()

    def go_on(c):
        masks, ready = chains[c][:2]
        running[c].wait_recv()
        slot = slots[c][steps[c]]
        pieces = slot.shape[0]
        kept = ins[2 * c] if steps[c] == 0 and not ready else current[c]
        total = kept[:pieces].astype(F32) + slot[...].astype(F32)
        steps[c] += 1
        if steps[c] == len(masks):
            totals[c][...] = total[0]
            return
        current[c][:pieces] = total.astype(BF16)
        split(c)

    for c, (masks, ready, _) in enumerate(chains):
        if not ready:
            launch(c, ins[2 * c + 1])
    for c, (masks, ready, _) in enumerate(chains):
        if ready:
            current[c][...] = (ins[2 * c][...].astype(F32) + ins[2 * c + 1][...].astype(F32)).astype(BF16)
            split(c)
    send_home()
    words[pl.ds(me, 1)] = words_ref[...][None]
    for c in events:
        go_on(c)
    for copy in home:
        copy.wait_recv()
    swaps = []
    for s in range(seqs):
        place = home_ref.at[exchanged(seq, s), core]
        swaps.append(begin(remote(place, place, home_send.at[seqs + s], home_receive.at[seqs + s], other_core)))
    for copy in word_copies:
        copy.wait_recv()
    total = words[0]
    for index in range(1, size):
        total = total + words[index]
    words_out[...] = total
    swap = remote(words_out.at[pl.ds(0, core_words)], other_words, word_send.at[0], word_receive.at[0], other_core)
    swap.start()
    swap.wait()
    words_out[pl.ds(0, core_words)] = total[:core_words] + other_words[...]
    for copy in swaps:
        copy.wait_recv()
    for copy in started:
        copy.wait_send()


def finish_call(chains, events, d_own, words, core_words, seqs, chips, number):
    size = chips * seqs
    rows, width = d_own.shape
    block = rows // seqs
    ins, specs, out, scratch, slots = [], [], [], [], []
    for masks, ready, (kept, other) in chains:
        pieces, share, columns = kept.shape
        ins += [kept, other]
        specs += [whole(kept.shape), whole(other.shape) if ready else anywhere(1)[0]]
        out.append(shape_of(share, columns, dtype=F32))
        scratch.append(pltpu.VMEM((pieces, share, columns), BF16))
        slots += [
            pltpu.VMEM((pieces >> (step + 1 if ready else step), share, columns), BF16) for step in range(len(masks))
        ]
    copies = len(slots)
    scratch += slots + [pltpu.VMEM((size, *words.shape), F32), pltpu.VMEM((core_words, 128), F32)]
    scratch += carrier_semaphores(copies) + carrier_semaphores(2 * seqs) + carrier_semaphores(size)
    scratch += [pltpu.SemaphoreType.DMA]
    home = shape_of(seqs, 2, block, width)
    out_specs = [whole(x.shape) for x in out] + anywhere(1) + [whole(words.shape)]
    return pl.pallas_call(
        functools.partial(finish_kernel, [(m, r, None) for m, r, _ in chains], events, seqs, chips, core_words),
        grid=(1,),
        in_specs=specs + anywhere(1) + [whole(words.shape)],
        out_specs=out_specs,
        out_shape=out + [home, shape_of(*words.shape, dtype=F32)],
        scratch_shapes=scratch,
        compiler_params=params_of(collective_id=number, has_side_effects=True),
        name="finish",
    )(*ins, d_own, words)


def swap_core(shard):
    return lax.ppermute(shard, "tp", [(0, 1), (1, 0)])


def swap_ctx(shard, mask):
    return lax.ppermute(shard, "ctx", [(c, c ^ mask) for c in range(lax.axis_size("ctx"))])


def next_section(shard, by):
    size = lax.axis_size("section")
    return lax.ppermute(shard, "section", [(s, s + by) for s in range(size) if 0 <= s + by < size])


def mask_order(masks):
    order = [0]
    for mask in reversed(masks):
        order = order + [value ^ mask for value in order]
    return order


def on_device(
    tokens,
    cotangent,
    block_order,
    first_gain,
    first_bias,
    second_gain,
    second_bias,
    joint_weight,
    joint_bias,
    output_weight,
    output_bias,
    up_weight,
    up_bias,
    down_weight,
    down_bias,
):
    section = lax.axis_index("section")
    sections = lax.axis_size("section")
    ctx = lax.axis_index("ctx")
    ctx_size = lax.axis_size("ctx")
    core = lax.axis_index("tp")
    seqs, local_len, width = tokens.shape
    block = local_len // 2
    chips = ctx_size // seqs
    seq, member = ctx // chips, ctx % chips
    rows = seqs * block
    chip_rows = 2 * rows
    length = chips * chip_rows
    seq_masks = [chips << b for b in range((seqs - 1).bit_length())]
    member_masks = [1 << b for b in range((chips - 1).bit_length())]

    k, u, a = jnp.meshgrid(jnp.arange(chips), jnp.arange(2), jnp.arange(seqs), indexing="ij")
    stored = (2 * ((seq ^ a) * chips + (member ^ k)) + (core ^ u)).reshape(-1)
    places = block_order[stored]
    spots = (places[:, None] * block + jnp.arange(block, dtype=jnp.int32)).reshape(-1)
    exponent = jnp.arange(ROT // 2, dtype=F32) * (2.0 / ROT)
    inverse = jnp.power(jnp.float32(ROTARY_BASE), -exponent)
    turns = spots.astype(F32)[:, None] * inverse[None, :]
    cosine, sine = jnp.cos(turns), jnp.sin(turns)
    rest = jnp.zeros((length, HEAD - ROT), F32)
    table = (
        jnp.tile(jnp.concatenate([cosine, cosine, rest + 1.0], 1), (1, 128 // HEAD)),
        jnp.tile(jnp.concatenate([sine, sine, rest], 1), (1, 128 // HEAD)),
    )

    tile = max(block, 128)
    tile_places = places[: chip_rows // block].reshape(-1, tile // block)
    lowest, highest = jnp.min(tile_places, 1), jnp.max(tile_places, 1)
    limits = jnp.stack([(lowest * block + 1) // KEY_TILE, (highest * block + block - 1) // KEY_TILE + 1], 1)

    gain_one, shift_one, gain_two, shift_two = first_gain, first_bias, second_gain, second_bias
    w_joint, b_joint = joint_weight[0], joint_bias[0]
    w_output, b_output = output_weight[0], output_bias
    w_up, b_up = up_weight[0], up_bias
    w_down, b_down = down_weight[0], down_bias
    gains = jnp.concatenate([gain_one, gain_two], 0)
    norms = jnp.concatenate([gain_one, shift_one, gain_two, shift_two], 0)
    shifts = jnp.concatenate([b_output, b_down], 0)

    def plane_parts(values):
        mine = lax.dynamic_slice_in_dim(values, core * block, block, 1)
        return [lax.dynamic_index_in_dim(mine, seq ^ shift, 0, keepdims=False) for shift in range(seqs)]

    def from_planes(values):
        parts = values.reshape(seqs, block, width)
        return [parts[s] if s == 0 else swap_ctx(parts[s], s * chips) for s in range(seqs)]

    def in_order(parts):
        parts = jnp.stack(parts)
        both = jnp.stack([parts, swap_core(parts)], 1)
        ordered = [
            lax.dynamic_index_in_dim(lax.dynamic_index_in_dim(both, s ^ seq, 0, False), v ^ core, 0, False)
            for s in range(seqs)
            for v in range(2)
        ]
        return jnp.stack(ordered).reshape(1, seqs, local_len, width)

    def paired(parts):
        count = len(parts) // 2
        return tuple(x[0] if count == 1 else jnp.concatenate(x, 0) for x in (parts[:count], parts[count:]))

    def forward(own, save, moves, moved, name, number):
        chip = (own, swap_core(own))
        moves = [("ctx", k) for k in range(1, chips)] + moves
        outs, arrived = front_call(
            chip, norms, w_joint, b_joint, table, w_up, b_up, w_down, save, moves, [own] * (chips - 1) + moved, name, number
        )
        normal, keys, values, queries, ffn0, ffn1, *kept_ffn = outs
        others, arrived = arrived[: chips - 1], arrived[chips - 1 :]
        key_parts, value_parts, normal_parts = [keys], [values], [normal]
        if chips > 1:
            rest = paired([x for other in others for x in (other, swap_core(other))])
            far_normal, far_keys, far_values = joint_call(
                rest, gain_one, shift_one, w_joint, b_joint, table, chip_rows
            )
            key_parts.append(far_keys)
            value_parts.append(far_values)
            normal_parts.append(far_normal)
        attn0, attn1, mixture, lse = attend_call(queries, key_parts, value_parts, places, limits, w_output, block)
        result, moments = merge_call(own, (attn0, swap_core(attn1)), (ffn0, swap_core(ffn1)), shifts)
        return result, moments, (normal_parts, queries, key_parts, value_parts, mixture, lse, *kept_ffn), arrived

    def attention_back(g_pair, kept, deps=()):
        normal_parts, queries, key_parts, value_parts, mixture, lse, second_in, active, slope = kept
        return attend_back_call(
            queries, g_pair, mixture, lse, key_parts, value_parts, places, limits, w_output, table, block, deps
        )

    def far_back(d_keys, d_values, deps=()):
        if chips == 1:
            return []
        far = joint_back_call([d_keys, d_values], chip_rows, length - chip_rows, w_joint, deps)
        if chips > 2:
            far = jnp.concatenate(far, 0).reshape(chips - 1, 2, rows, width)
            far = far[:, 0], far[:, 1]
        sums = (far[0].astype(F32) + swap_core(far[1]).astype(F32)).astype(BF16).reshape(chips - 1, rows, width)
        return [sums[k - 1] for k in range(1, chips)]

    others = [("ctx", k) for k in range(1, chips)]
    planes = [("ctx", s * chips) for s in range(1, seqs)]
    token_parts = plane_parts(tokens)
    token_rows = jnp.concatenate([token_parts[0]] + [swap_ctx(token_parts[s], s * chips) for s in range(1, seqs)], 0)
    g_parts = plane_parts(cotangent)
    own = token_rows
    for tick in range(sections):
        first = tick == 0
        result, moments, kept, arrived = forward(
            own, tick == sections - 1, planes if first else [], g_parts[1:] if first else [], "front" + str(tick), tick
        )
        if first:
            g_rows = jnp.concatenate([g_parts[0], *arrived], 0)
        if tick < sections - 1:
            own = jnp.where(section == 0, token_rows, next_section(result, 1))
    out_parts = from_planes(result)
    moments = jnp.sum(moments[:3], axis=1)
    normal_parts, queries, key_parts, value_parts, mixture, lse, second_in, active, slope = kept
    g_own = g_rows
    for tick in range(sections - 1):
        g_pair = (g_own, swap_core(g_own))
        d_queries, d_keys, d_values, _ = attention_back(g_pair, kept)
        sums = far_back(d_keys, d_values, tuple(out_parts) if tick == 0 else ())
        near, second, arrivals = rear_call(
            (d_queries, d_keys, d_values), w_joint, g_pair, slope, w_up, w_down, others, sums, "rear" + str(tick), sections + tick
        )
        firsts = [near[0], swap_core(near[1]), *arrivals]
        d_own, _ = norm_back_call(own, g_own, firsts, [second[0], swap_core(second[1])], gains)
        g_own = jnp.where(section == sections - 1, g_rows, next_section(d_own, -1))
    section_out = in_order(out_parts)

    late = tuple(member_masks + seq_masks)
    early = tuple(seq_masks + member_masks)
    late_owners = jnp.stack([ctx ^ m for m in mask_order(late)]).astype(jnp.int32)
    early_owners = jnp.stack([ctx ^ m for m in mask_order(early)]).astype(jnp.int32)
    local = w_output.shape[0]
    units = w_up.shape[1]
    share = width // ctx_size
    g_pair = (g_own, swap_core(g_own))
    by_blocks = share % 128 == 0 and chips == 2

    def of_g(right, name, deps=()):
        if by_blocks:
            terms = [(g_pair[0], right, 0), (g_pair[1], right, 1)]
        else:
            terms = [(jnp.concatenate(g_pair, 0), right, 0)]
        return slope_call(late_owners, terms, name, (0, 1), deps)

    down = of_g(active, "down_slope")
    down_arrived = swap_ctx(down[1], late[0])
    output = of_g(mixture, "output_slope", (down[0],))
    second0, second1, d_hidden, up_sums = ffn_back_call(g_pair, slope, w_up, w_down, (output[0],))
    ups = [slope_call(early_owners, [(second_in, d_hidden, 0)], "up_slope", (0, 2))]
    ups.append(slope_call(early_owners, [(second_in, d_hidden, 0)], "up_slope", (1, 2), (ups[0][0],)))
    ups_arrived = [swap_ctx(part[1], early[0]) for part in ups]
    d_queries, d_keys, d_values, joint_sums = attention_back(g_pair, kept, (ups[1][0], output[0]))
    sums = far_back(d_keys, d_values, (down_arrived, *ups_arrived))

    def halved(pair, arrived):
        total = (pair[0].astype(F32) + arrived.astype(F32)).astype(BF16)
        return total[: total.shape[0] // 2], total[total.shape[0] // 2 :]

    down = halved(down, down_arrived)
    ups[0] = halved(ups[0], ups_arrived[0])
    grads = (d_queries, d_keys, d_values)
    if by_blocks:
        moves = others + [("ctx", late[1]), ("ctx", early[1])]
        near, joints, (*arrivals, down_arrived, ups_arrived[0]) = joint_rear_call(
            grads, w_joint, normal_parts, late, moves, [*sums, down[1], ups[0][1]], "joint_rear", 2 * sections
        )
    else:
        near = joint_back_call(grads, 0, chip_rows, w_joint)
        down_arrived, ups_arrived[0] = swap_ctx(down[1], late[1]), swap_ctx(ups[0][1], early[1])
        arrivals = [swap_ctx(part, k + 1) for k, part in enumerate(sums)]
        joints = [slope_call(late_owners, [(normal_parts[0], d_queries, 0)], "query_slope")]
        for grad in grads[1:]:
            joints.append(slope_call(late_owners, [(part, grad, n) for n, part in enumerate(normal_parts)], "key_slope"))
    firsts = [near[0], swap_core(near[1]), *arrivals]
    seconds = [second0, swap_core(second1)]
    d_own, norm_sums = norm_back_call(own, g_own, firsts, seconds, gains)

    def in_words(values):
        values = values.reshape(-1)
        return jnp.pad(values, (0, -values.size % 1024)).reshape(-1, 128)

    both = in_words(jnp.concatenate([norm_sums[:5].reshape(-1), moments]))
    ones = in_words(jnp.concatenate([joint_sums[:3].reshape(-1), up_sums.reshape(-1)]))
    chains = [
        (late, False, output),
        (late, False, joints[0]),
        (late, False, joints[1]),
        (late, False, joints[2]),
        (early[1:], True, (ups[1][0], ups_arrived[1])),
        (late[2:], True, (down[0], down_arrived)),
        (early[2:], True, (ups[0][0], ups_arrived[0])),
    ]
    events = [0, 6, 1, 2, 0, 3, 1, 4, 5, 0, 2, 1, 3, 4, 2, 3]
    if len(late) != 3:
        events = [c for step in range(len(late)) for c, chain in enumerate(chains) if step < len(chain[0])]
    output_total, *joint_total, up_right, down_total, up_left, home, small = finish_call(
        chains, events, d_own, jnp.concatenate([both, ones], 0), both.shape[0], seqs, chips, 2 * sections + 1
    )
    section_in_grad = home.reshape(1, seqs, local_len, width)
    joint_total = jnp.stack(joint_total)
    up_total = jnp.concatenate([up_left, up_right], 1)
    output_total, down_total = output_total.T, down_total.T
    both, ones = small[: both.shape[0]].reshape(-1), small[both.shape[0] :].reshape(-1)
    norm_total = both[: 5 * width].reshape(5, 1, width)
    root_means = jnp.sqrt(both[5 * width : 5 * width + 3] / (length * seqs * width))
    joint_shift = ones[: 3 * local].reshape(1, 3, local)
    up_shift = ones[3 * local : 3 * local + units].reshape(1, units)
    return (
        section_out,
        section_in_grad,
        norm_total[0],
        norm_total[1],
        norm_total[2],
        norm_total[3],
        joint_total[None],
        joint_shift,
        output_total[None],
        norm_total[4],
        up_total[None],
        up_shift,
        down_total[None],
        norm_total[4],
        root_means[None],
    )


def solution(mesh):
    in_specs = (
        P(None, "ctx", None),
        P(None, "ctx", None),
        P(),
        P("section", None),
        P("section", None),
        P("section", None),
        P("section", None),
        P("section", None, None, "tp"),
        P("section", None, "tp"),
        P("section", "tp", None),
        P("section", None),
        P("section", None, "tp"),
        P("section", "tp"),
        P("section", "tp", None),
        P("section", None),
    )
    out_specs = (
        P("section", None, "ctx", None),
        P("section", None, "ctx", None),
        P("section", None),
        P("section", None),
        P("section", None),
        P("section", None),
        P("section", None, "ctx", "tp"),
        P("section", None, "tp"),
        P("section", "tp", "ctx"),
        P("section", None),
        P("section", "ctx", "tp"),
        P("section", "tp"),
        P("section", "tp", "ctx"),
        P("section", None),
        P("section", None),
    )
    return jax.shard_map(
        on_device, mesh=mesh, in_specs=in_specs, out_specs=out_specs, check_vma=False
    )
```

```python
import functools

import jax
import jax.numpy as jnp
from jax import lax
from jax.experimental import pallas as pl
from jax.experimental.pallas import tpu as pltpu
from jax.sharding import PartitionSpec as P

HEAD = 64
ROT = 16
EPS = 1e-05
ROTARY_BASE = 10000.0
NEGATIVE = -1e30
STACK = 4
GROUP = STACK * HEAD
KEY_TILE = 512
VMEM_LIMIT = 60 * 1024 * 1024
BF16 = jnp.bfloat16
F32 = jnp.float32


def dot(a, b):
    return jnp.dot(a, b, preferred_element_type=F32)


def dot_nt(a, b):
    return lax.dot_general(a, b, (((1,), (1,)), ((), ())), preferred_element_type=F32)


def params_of(**more):
    return pltpu.CompilerParams(vmem_limit_bytes=VMEM_LIMIT, **more)


def whole(shape):
    return pl.BlockSpec(shape, lambda *_: (0,) * len(shape))


def rows_of(tile, *rest):
    return pl.BlockSpec((tile, *rest), lambda r, *_: (r,) + (0,) * len(rest))


def halves_of(tile, count, *rest):
    return [
        pl.BlockSpec((tile, *rest), lambda r, *_: (jnp.minimum(r, count - 1),) + (0,) * len(rest)),
        pl.BlockSpec((tile, *rest), lambda r, *_: (jnp.maximum(r - count, 0),) + (0,) * len(rest)),
    ]


def pick(refs):
    return jnp.where(pl.program_id(0) < pl.num_programs(0) // 2, refs[0][...], refs[1][...])


def put(refs, value):
    first = pl.program_id(0) < pl.num_programs(0) // 2
    for ref, here in zip(refs, (first, jnp.logical_not(first))):

        @pl.when(here)
        def _():
            ref[...] = value


def waiting(kernel, inputs, deps):
    return lambda *refs: kernel(*refs[:inputs], *refs[inputs + len(deps) :])


def exchanged(position, mask):
    for bit in range(mask.bit_length()):
        if mask >> bit & 1:
            position = position + (1 << bit) - (2 << bit) * (position // (1 << bit) % 2)
    return position


def carrying(kernel, inputs, outputs, moves):
    count = len(moves)

    def body(*refs):
        sources = refs[inputs : inputs + count]
        outs = refs[inputs + count : inputs + count + outputs]
        targets = refs[inputs + count + outputs : inputs + 2 * count + outputs]
        *scratch, send, receive = refs[inputs + 2 * count + outputs :]
        partners = [{axis: exchanged(lax.axis_index(axis), mask)} for axis, mask in moves]
        copies = [
            pltpu.make_async_remote_copy(
                source, target, send.at[n], receive.at[n], device_id=partner, device_id_type=pl.DeviceIdType.MESH
            )
            for n, (source, target, partner) in enumerate(zip(sources, targets, partners))
        ]

        @pl.when(pl.program_id(0) == 0)
        def _():
            barrier = pltpu.get_barrier_semaphore()
            for partner in partners:
                pl.semaphore_signal(barrier, inc=1, device_id=partner, device_id_type=pl.DeviceIdType.MESH)
            pl.semaphore_wait(barrier, count)
            for copy in copies:
                copy.start()

        kernel(*refs[:inputs], *outs, *scratch)

        @pl.when(pl.program_id(0) == pl.num_programs(0) - 1)
        def _():
            for copy in copies:
                copy.wait()

    return body


def carrier_semaphores(count):
    return [pltpu.SemaphoreType.DMA((count,)), pltpu.SemaphoreType.DMA((count,))]


def anywhere(count):
    return [pl.BlockSpec(memory_space=pl.ANY)] * count


def cost(flops, size):
    return pl.CostEstimate(flops=int(flops), bytes_accessed=int(size), transcendentals=0)


def shape_of(*shape, dtype=BF16):
    return jax.ShapeDtypeStruct(shape, dtype)


def normalize(values):
    middle = jnp.mean(values, axis=-1, keepdims=True)
    centered = values - middle
    spread = jnp.mean(centered * centered, axis=-1, keepdims=True)
    inverse = lax.rsqrt(spread + EPS)
    return centered * inverse, inverse


def turn(values, cosine, sine):
    pieces = []
    for start in range(0, values.shape[1], 128):
        part = values[:, start : start + 128]
        ahead = pltpu.roll(part, 128 - ROT // 2, 1)
        behind = pltpu.roll(part, ROT // 2, 1)
        entry = lax.broadcasted_iota(jnp.int32, part.shape, 1) % HEAD
        pieces.append(part * cosine + jnp.where(entry < ROT // 2, -ahead, behind) * sine)
    return jnp.concatenate(pieces, axis=1)


def joint_kernel(h0_ref, h1_ref, gain_ref, shift_ref, w_ref, b_ref, cos_ref, sin_ref, n_ref, k_ref, v_ref):
    scaled, _ = normalize(pick((h0_ref, h1_ref)).astype(F32))
    low = (scaled * gain_ref[...] + shift_ref[...]).astype(BF16)
    n_ref[...] = low
    cosine, sine = cos_ref[...], sin_ref[...]
    keys = dot(low, w_ref[1]) + b_ref[1:2]
    values = dot(low, w_ref[2]) + b_ref[2:3]
    k_ref[...] = turn(keys, cosine, sine).astype(BF16)
    v_ref[...] = values.astype(BF16)


def joint_call(pair, gain, shift, w_joint, b_joint, table, offset, deps=()):
    rows, width = pair[0].shape
    local = w_joint.shape[2]
    tile = min(512, rows)
    first = offset // tile
    count = 2
    turns = pl.BlockSpec((tile, 128), lambda r: (first + r, 0))
    return pl.pallas_call(
        waiting(joint_kernel, 8, deps),
        grid=(2 * rows // tile,),
        in_specs=halves_of(tile, rows // tile, width)
        + [whole((1, width)), whole((1, width)), whole(w_joint.shape), whole(b_joint.shape), turns, turns]
        + anywhere(len(deps)),
        out_specs=[rows_of(tile, width)] + [rows_of(tile, local)] * count,
        out_shape=[shape_of(2 * rows, width)] + [shape_of(2 * rows, local)] * count,
        compiler_params=params_of(),
        cost_estimate=cost(4 * rows * width * local * count, 8 * rows * width + 2 * w_joint.size),
        name="joint_projection",
    )(*pair, gain, shift, w_joint, b_joint, *table, *deps)


def gelu_parts(x):
    return 0.5 + 0.5 * lax.erf(x * 0.5**0.5), jnp.exp(-0.5 * x * x)


def front_kernel(
    save, h0_ref, h1_ref, norms_ref, w_ref, b_ref, cos_ref, sin_ref, up_ref, up_b_ref, down_ref,
    n_ref, k_ref, v_ref, q_ref, part0_ref, part1_ref, *saved
):
    scaled, _ = normalize(pick((h0_ref, h1_ref)).astype(F32))
    low = (scaled * norms_ref[0:1] + norms_ref[1:2]).astype(BF16)
    n_ref[...] = low
    cosine, sine = cos_ref[...], sin_ref[...]
    keys = dot(low, w_ref[1]) + b_ref[1:2]
    values = dot(low, w_ref[2]) + b_ref[2:3]
    queries = dot(low, w_ref[0]) + b_ref[0:1]
    q_ref[...] = (turn(queries, cosine, sine) * HEAD ** (-0.5)).astype(BF16)
    k_ref[...] = turn(keys, cosine, sine).astype(BF16)
    v_ref[...] = values.astype(BF16)
    low = (scaled * norms_ref[2:3] + norms_ref[3:4]).astype(BF16)
    if save:
        saved[0][...] = low
    total = None
    for start in range(0, up_ref.shape[1], 512):
        cut = pl.ds(start, 512)
        hidden = dot(low, up_ref[:, cut]) + up_b_ref[:, cut]
        share, bell = gelu_parts(hidden)
        active = (hidden * share).astype(BF16)
        if save:
            saved[1][:, cut] = active
            saved[2][:, cut] = (share + hidden * bell * 0.3989422804014327).astype(BF16)
        term = dot(active, down_ref[cut, :])
        total = term if total is None else total + term
    put((part0_ref, part1_ref), total.astype(BF16))


def front_call(pair, norms, w_joint, b_joint, table, w_up, b_up, w_down, save, moves, moved, name, number):
    rows, width = pair[0].shape
    local = w_joint.shape[2]
    units = w_up.shape[1]
    tile = min(512, rows)
    out = [shape_of(2 * rows, width)] + [shape_of(2 * rows, local)] * 3 + [shape_of(rows, width)] * 2
    out_specs = [rows_of(tile, width)] + [rows_of(tile, local)] * 3 + halves_of(tile, rows // tile, width)
    if save:
        out += [shape_of(2 * rows, width)] + [shape_of(2 * rows, units)] * 2
        out_specs += [rows_of(tile, width), rows_of(tile, units), rows_of(tile, units)]
    ins = (norms, w_joint, b_joint, *table, w_up, b_up, w_down)
    turns = rows_of(tile, 128)
    specs = [turns if x is table[0] or x is table[1] else whole(x.shape) for x in ins]
    outs = pl.pallas_call(
        carrying(functools.partial(front_kernel, save), 2 + len(ins), len(out), moves),
        grid=(2 * rows // tile,),
        in_specs=halves_of(tile, rows // tile, width) + specs + anywhere(len(moves)),
        out_specs=out_specs + anywhere(len(moves)),
        out_shape=out + [shape_of(*x.shape) for x in moved],
        scratch_shapes=carrier_semaphores(len(moves)),
        compiler_params=params_of(collective_id=number, has_side_effects=True),
        cost_estimate=cost(4 * rows * width * (3 * local + 2 * units), 4 * w_up.size + 16 * rows * width),
        name=name,
    )(*pair, *ins, *moved)
    return outs[: len(out)], outs[len(out) :]


def ffn_back_kernel(g0_ref, g1_ref, slope_ref, up_ref, down_ref, part0_ref, part1_ref, hidden_ref, sums_ref):
    upstream = pick((g0_ref, g1_ref))
    units = up_ref.shape[1]

    @pl.when(pl.program_id(0) == 0)
    def _():
        sums_ref[...] = jnp.zeros_like(sums_ref)

    total = None
    for start in range(0, units, 512):
        cut = pl.ds(start, 512)
        d_active = dot_nt(upstream, down_ref[cut, :])
        d_hidden = (d_active * slope_ref[:, cut].astype(F32)).astype(BF16)
        hidden_ref[:, cut] = d_hidden
        sums_ref[:, cut] += jnp.sum(d_hidden.astype(F32), axis=0, keepdims=True)
        term = dot_nt(d_hidden, up_ref[:, cut])
        total = term if total is None else total + term
    put((part0_ref, part1_ref), total.astype(BF16))


def ffn_back_call(pair, slope, w_up, w_down, deps=()):
    rows, width = pair[0].shape
    units = w_up.shape[1]
    tile = min(512, rows)
    return pl.pallas_call(
        waiting(ffn_back_kernel, 5, deps),
        grid=(2 * rows // tile,),
        in_specs=halves_of(tile, rows // tile, width) + [rows_of(tile, units), whole(w_up.shape), whole(w_down.shape)]
        + anywhere(len(deps)),
        out_specs=halves_of(tile, rows // tile, width) + [rows_of(tile, units), whole((1, units))],
        out_shape=[shape_of(rows, width)] * 2 + [shape_of(2 * rows, units), shape_of(1, units, dtype=F32)],
        compiler_params=params_of(),
        cost_estimate=cost(8 * rows * width * units, 4 * w_up.size + 8 * rows * (width + units)),
        name="feed_forward_back",
    )(*pair, slope, w_up, w_down, *deps)


def start_sorted(places_ref, parts, targets, sem, block):
    copies = []
    for refs, target in zip(parts, targets):
        index = 0
        for ref in refs:
            for local in range(ref.shape[0] // block):
                place = pl.ds(pl.multiple_of(places_ref[index] * block, block), block)
                copies.append(pltpu.make_async_copy(ref.at[pl.ds(local * block, block)], target.at[place], sem))
                index += 1
    for copy in copies:
        copy.start()
    return copies


def transpose_into(source, target):
    rows, columns = source.shape

    def step(index, _):
        start = pl.multiple_of(index * 256, 256)
        for column in range(0, columns, 256):
            target[column : column + 256, pl.ds(start, 256)] = source[pl.ds(start, 256), column : column + 256].T
        return 0

    lax.fori_loop(0, rows // 256, step, 0)


def stacked(values):
    owner = lax.broadcasted_iota(jnp.int32, values.shape, 1) // HEAD
    zero = jnp.zeros_like(values)
    return jnp.concatenate([jnp.where(owner == a, values, zero) for a in range(STACK)], axis=0)


def spots_of(places_ref, step, tile, block, shape, axis):
    at = lax.broadcasted_iota(jnp.int32, shape, axis) % tile
    count = tile // block
    spot = at + places_ref[step * count] * block
    for s in range(1, count):
        spot = jnp.where(at >= s * block, at - s * block + places_ref[step * count + s] * block, spot)
    return spot


def attend_kernel(block, tile, remote, places_ref, limits_ref, q_ref, wo_ref, *refs):
    key_refs, value_refs = refs[: 1 + remote], refs[1 + remote : 2 + 2 * remote]
    part0_ref, part1_ref, mix_ref, lse_ref, keys, values, scores_ref, sem = refs[2 + 2 * remote :]
    groups = q_ref.shape[1] // GROUP
    half = part0_ref.shape[0]
    rows = STACK * tile
    lanes = [slice(g * GROUP, (g + 1) * GROUP) for g in range(groups)]
    for copy in start_sorted(places_ref, (key_refs, value_refs), (keys, values), sem, block):
        copy.wait()

    def tile_step(step, _):
        mine = pl.ds(pl.multiple_of(step * tile, tile), tile)
        heads = [stacked(q_ref[mine, lane]) for lane in lanes]
        spots = spots_of(places_ref, step, tile, block, (rows, 128), 0)

        def attend_to(count):
            open_end = (count - 1) * KEY_TILE if tile == block else 0
            tops = []
            for g, lane in enumerate(lanes):
                top = None
                for start in range(0, count * KEY_TILE, KEY_TILE):
                    scores = dot_nt(heads[g], keys[start : start + KEY_TILE, lane])
                    for column in range(0, KEY_TILE, 128):
                        piece = scores[:, column : column + 128]
                        if start + column >= open_end:
                            spot = start + column + lax.broadcasted_iota(jnp.int32, piece.shape, 1)
                            piece = jnp.where(spot <= spots, piece, NEGATIVE)
                        scores_ref[g, :, start + column : start + column + 128] = piece
                        top = piece if top is None else jnp.maximum(top, piece)
                tops.append(jnp.broadcast_to(jnp.max(top, axis=1, keepdims=True), (rows, 128)))
            for g, lane in enumerate(lanes):
                mass, total = None, None
                for start in range(0, count * KEY_TILE, KEY_TILE):
                    raised = []
                    for column in range(start, start + KEY_TILE, 128):
                        piece = jnp.exp(scores_ref[g, :, column : column + 128] - tops[g])
                        mass = piece if mass is None else mass + piece
                        raised.append(piece.astype(BF16))
                    term = dot(jnp.concatenate(raised, axis=1), values[start : start + KEY_TILE, lane])
                    total = term if total is None else total + term
                mass = jnp.broadcast_to(jnp.sum(mass, axis=1, keepdims=True), (rows, 128))
                total = total * jnp.concatenate([1.0 / mass] * (GROUP // 128), axis=1)
                owner = lax.broadcasted_iota(jnp.int32, (tile, GROUP), 1) // HEAD
                mixture = total[:tile]
                for a in range(1, STACK):
                    mixture = jnp.where(owner == a, total[a * tile : (a + 1) * tile], mixture)
                mix_ref[mine, lane] = mixture.astype(BF16)
                lse = tops[g] + jnp.log(mass)
                for a in range(STACK):
                    lse_ref[step, g : g + 1, a * tile : (a + 1) * tile] = lse[a * tile : (a + 1) * tile].T[0:1]

        for count in range(1, keys.shape[0] // KEY_TILE + 1):
            pl.when(limits_ref[step, 1] == count)(functools.partial(attend_to, count))
        return 0

    lax.fori_loop(0, q_ref.shape[0] // tile, tile_step, 0)
    part0_ref[...] = dot(mix_ref[:half], wo_ref[...]).astype(BF16)
    part1_ref[...] = dot(mix_ref[half:], wo_ref[...]).astype(BF16)


def attend_call(queries, key_parts, value_parts, places, limits, w_output, block, deps=()):
    rows, local = queries.shape
    width = w_output.shape[1]
    tile = rows // limits.shape[0]
    length = sum(part.shape[0] for part in key_parts)
    groups = local // GROUP
    outs = [(rows // 2, width), (rows // 2, width), (rows, local), (rows // tile, groups, STACK * tile)]
    return pl.pallas_call(
        waiting(functools.partial(attend_kernel, block, tile, len(key_parts) - 1), 4 + 2 * len(key_parts), deps),
        grid_spec=pltpu.PrefetchScalarGridSpec(
            num_scalar_prefetch=2,
            grid=(1,),
            in_specs=[whole((rows, local)), whole(w_output.shape)] + anywhere(2 * len(key_parts) + len(deps)),
            out_specs=[whole(shape) for shape in outs],
            scratch_shapes=[
                pltpu.VMEM((length, local), BF16),
                pltpu.VMEM((length, local), BF16),
                pltpu.VMEM((groups, STACK * tile, length), F32),
                pltpu.SemaphoreType.DMA,
            ],
        ),
        out_shape=[shape_of(*shape) for shape in outs[:3]] + [shape_of(*outs[3], dtype=F32)],
        compiler_params=params_of(),
        cost_estimate=cost(12 * rows * length * local, 2 * length * local * 4),
        name="attend",
    )(places, limits, queries, w_output, *key_parts, *value_parts, *deps)


def attend_back_kernel(
    block, tile, remote, places_ref, limits_ref, q_ref, g0_ref, g1_ref, mix_ref, lse_ref, wo_ref, cos_ref, sin_ref, *refs
):
    key_refs, value_refs = refs[: 1 + remote], refs[1 + remote : 2 + 2 * remote]
    (dq_ref, dk_ref, dv_ref, sums_ref, keys, values, keys_t, d_keys, d_values, d_mixture, inner, total, d_queries, sem) = refs[
        2 + 2 * remote :
    ]
    groups = q_ref.shape[1] // GROUP
    rows = q_ref.shape[0]
    half = g0_ref.shape[0]
    lanes = [slice(g * GROUP, (g + 1) * GROUP) for g in range(groups)]
    copies = start_sorted(places_ref, (key_refs, value_refs), (keys, values), sem, block)
    d_keys[...] = jnp.zeros_like(d_keys)
    d_values[...] = jnp.zeros_like(d_values)
    head_of = lax.broadcasted_iota(jnp.int32, (8, GROUP), 1) // HEAD
    picker = jnp.where(lax.broadcasted_iota(jnp.int32, (8, GROUP), 0) == head_of, 1.0, 0.0).astype(BF16)
    for index, ref in enumerate((g0_ref, g1_ref)):
        cut = pl.ds(index * half, half)
        low = dot_nt(ref[...], wo_ref[...]).astype(BF16)
        d_mixture[cut, :] = low
        product = low.astype(F32) * mix_ref[cut, :].astype(F32)
        high = product.astype(BF16)
        rest = (product - high.astype(F32)).astype(BF16)
        for g, lane in enumerate(lanes):
            inner[g * 8 : (g + 1) * 8, cut] = dot_nt(picker, high[:, lane]) + dot_nt(picker, rest[:, lane])
    for copy in copies:
        copy.wait()
    transpose_into(keys, keys_t)

    def query_step(step, _):
        mine = pl.ds(pl.multiple_of(step * tile, tile), tile)
        spots = spots_of(places_ref, step, tile, block, (1, STACK * tile), 1)
        heads = [stacked(q_ref[mine, lane]) for lane in lanes]
        sides = [stacked(d_mixture[mine, lane]) for lane in lanes]
        sums = [
            jnp.concatenate([inner[g * 8 + a : g * 8 + a + 1, mine] for a in range(STACK)], axis=1) for g in range(groups)
        ]
        lse = [lse_ref[step, g : g + 1, :] for g in range(groups)]
        total[...] = jnp.zeros_like(total)

        def key_step(masked, index, carry):
            start = pl.multiple_of(index * KEY_TILE, KEY_TILE)
            cut = pl.ds(start, KEY_TILE)
            for g, lane in enumerate(lanes):
                scores = dot_nt(keys[cut, lane], heads[g])
                if masked:
                    spot = start + lax.broadcasted_iota(jnp.int32, scores.shape, 0)
                    scores = jnp.where(spot <= spots, scores, NEGATIVE)
                weights = jnp.exp(scores - lse[g])
                d_weights = dot_nt(values[cut, lane], sides[g])
                d_scores = (weights * (d_weights - sums[g])).astype(BF16)
                d_values[cut, lane] += dot(weights.astype(BF16), sides[g])
                d_keys[cut, lane] += dot(d_scores, heads[g])
                total[lane, :] += dot(keys_t[lane, cut], d_scores)
            return carry

        lax.fori_loop(0, limits_ref[step, 0], functools.partial(key_step, False), 0)
        lax.fori_loop(limits_ref[step, 0], limits_ref[step, 1], functools.partial(key_step, True), 0)
        for lane in lanes:
            picked = [total[lane, :][a * HEAD : (a + 1) * HEAD, a * tile : (a + 1) * tile] for a in range(STACK)]
            d_queries[mine, lane] = jnp.concatenate(picked, axis=0).T
        return 0

    lax.fori_loop(0, rows // tile, query_step, 0)
    turned = turn(d_queries[...] * HEAD ** (-0.5), cos_ref[:rows], -sin_ref[:rows]).astype(BF16)
    dq_ref[...] = turned
    sums_ref[...] = jnp.zeros_like(sums_ref)
    sums_ref[0:1, :] = jnp.sum(turned.astype(F32), axis=0, keepdims=True)

    def block_step(index, _):
        place = pl.ds(pl.multiple_of(places_ref[index] * block, block), block)
        mine = pl.ds(pl.multiple_of(index * block, block), block)
        turned = turn(d_keys[place, :], cos_ref[mine, :], -sin_ref[mine, :]).astype(BF16)
        dk_ref[mine, :] = turned
        low = d_values[place, :].astype(BF16)
        dv_ref[mine, :] = low
        sums_ref[1:2, :] += jnp.sum(turned.astype(F32), axis=0, keepdims=True)
        sums_ref[2:3, :] += jnp.sum(low.astype(F32), axis=0, keepdims=True)
        return 0

    lax.fori_loop(0, dk_ref.shape[0] // block, block_step, 0)


def attend_back_call(
    queries, g_pair, mixture, lse, key_parts, value_parts, places, limits, w_output, table, block, deps=()
):
    rows, local = queries.shape
    width = w_output.shape[1]
    tile = rows // limits.shape[0]
    length = sum(part.shape[0] for part in key_parts)
    groups = local // GROUP
    ins = (queries, *g_pair, mixture, lse, w_output, *table)
    return pl.pallas_call(
        waiting(
            functools.partial(attend_back_kernel, block, tile, len(key_parts) - 1), 2 + len(ins) + 2 * len(key_parts), deps
        ),
        grid_spec=pltpu.PrefetchScalarGridSpec(
            num_scalar_prefetch=2,
            grid=(1,),
            in_specs=[whole(x.shape) for x in ins] + anywhere(2 * len(key_parts) + len(deps)),
            out_specs=[whole((rows, local)), whole((length, local)), whole((length, local)), whole((8, local))],
            scratch_shapes=[
                pltpu.VMEM((length, local), BF16),
                pltpu.VMEM((length, local), BF16),
                pltpu.VMEM((local, length), BF16),
                pltpu.VMEM((length, local), F32),
                pltpu.VMEM((length, local), F32),
                pltpu.VMEM((rows, local), BF16),
                pltpu.VMEM((8 * groups, rows), F32),
                pltpu.VMEM((local, STACK * tile), F32),
                pltpu.VMEM((rows, local), F32),
                pltpu.SemaphoreType.DMA,
            ],
        ),
        out_shape=[shape_of(rows, local), shape_of(length, local), shape_of(length, local), shape_of(8, local, dtype=F32)],
        compiler_params=params_of(),
        cost_estimate=cost(24 * rows * length * local, 2 * length * local * 8),
        name="attend_back",
    )(places, limits, *ins, *key_parts, *value_parts, *deps)


def joint_back_kernel(count, *refs):
    w_ref = refs[count]
    total = None
    for index in range(count):
        term = dot_nt(refs[index][...], w_ref[3 - count + index])
        total = term if total is None else total + term
    put(refs[count + 1 :], total.astype(BF16))


def joint_back_call(grads, offset, rows, w_joint, deps=()):
    width, local = w_joint.shape[1:]
    half = rows // 2
    tile = min(512, half)
    first = offset // tile
    return pl.pallas_call(
        waiting(functools.partial(joint_back_kernel, len(grads)), len(grads) + 1, deps),
        grid=(rows // tile,),
        in_specs=[pl.BlockSpec((tile, local), lambda r: (first + r, 0))] * len(grads)
        + [whole(w_joint.shape)]
        + anywhere(len(deps)),
        out_specs=halves_of(tile, half // tile, width),
        out_shape=[shape_of(half, width)] * 2,
        compiler_params=params_of(),
        cost_estimate=cost(2 * rows * width * local * len(grads), 2 * rows * (width + 3 * local) + 2 * w_joint.size),
        name="joint_projection_back",
    )(*grads, w_joint, *deps)


def rear_kernel(q_ref, k_ref, v_ref, w_ref, g0_ref, g1_ref, slope_ref, up_ref, down_ref, first0_ref, first1_ref, part0_ref, part1_ref):
    total = dot_nt(q_ref[...], w_ref[0]) + dot_nt(k_ref[...], w_ref[1]) + dot_nt(v_ref[...], w_ref[2])
    put((first0_ref, first1_ref), total.astype(BF16))
    upstream = pick((g0_ref, g1_ref))
    total = None
    for start in range(0, up_ref.shape[1], 512):
        cut = pl.ds(start, 512)
        d_active = dot_nt(upstream, down_ref[cut, :])
        d_hidden = (d_active * slope_ref[:, cut].astype(F32)).astype(BF16)
        term = dot_nt(d_hidden, up_ref[:, cut])
        total = term if total is None else total + term
    put((part0_ref, part1_ref), total.astype(BF16))


def rear_call(grads, w_joint, pair, slope, w_up, w_down, moves, moved, name, number):
    rows, width = pair[0].shape
    local = w_joint.shape[2]
    units = w_up.shape[1]
    tile = min(512, rows)
    halves = halves_of(tile, rows // tile, width)
    outs = pl.pallas_call(
        carrying(rear_kernel, 9, 4, moves),
        grid=(2 * rows // tile,),
        in_specs=[rows_of(tile, local)] * 3
        + [whole(w_joint.shape)]
        + halves
        + [rows_of(tile, units), whole(w_up.shape), whole(w_down.shape)]
        + anywhere(len(moves)),
        out_specs=halves + halves + anywhere(len(moves)),
        out_shape=[shape_of(rows, width)] * 4 + [shape_of(*x.shape) for x in moved],
        scratch_shapes=carrier_semaphores(len(moves)),
        compiler_params=params_of(collective_id=number, has_side_effects=True),
        cost_estimate=cost(4 * rows * width * (3 * local + 2 * units), 4 * w_up.size + 16 * rows * width),
        name=name,
    )(*grads, w_joint, *pair, slope, w_up, w_down, *moved)
    return outs[:2], outs[2:4], outs[4:]


def norm_back_kernel(firsts, h_ref, g_ref, gains_ref, *refs):
    first_refs, second_refs, (out_ref, sums_ref) = refs[:firsts], refs[firsts:-2], refs[-2:]

    @pl.when(pl.program_id(0) == 0)
    def _():
        sums_ref[...] = jnp.zeros_like(sums_ref)

    scaled, inverse = normalize(h_ref[...].astype(F32))
    upstream = g_ref[...].astype(F32)
    d_first = sum(ref[...].astype(F32) for ref in first_refs)
    d_second = sum(ref[...].astype(F32) for ref in second_refs)
    for row, term in enumerate((d_first * scaled, d_first, d_second * scaled, d_second, upstream)):
        sums_ref[row : row + 1, :] += jnp.sum(term, axis=0, keepdims=True)
    d_scaled = d_first * gains_ref[0:1] + d_second * gains_ref[1:2]
    middle = jnp.mean(d_scaled, axis=-1, keepdims=True)
    along = jnp.mean(d_scaled * scaled, axis=-1, keepdims=True)
    out_ref[...] = (upstream + inverse * (d_scaled - middle - scaled * along)).astype(BF16)


def norm_back_call(h, g, firsts, seconds, gains, deps=()):
    rows, width = h.shape
    tile = min(128, rows)
    one = rows_of(tile, width)
    return pl.pallas_call(
        waiting(functools.partial(norm_back_kernel, len(firsts)), 3 + len(firsts) + len(seconds), deps),
        grid=(rows // tile,),
        in_specs=[one, one, whole(gains.shape)] + [one] * (len(firsts) + len(seconds)) + anywhere(len(deps)),
        out_specs=[one, whole((8, width))],
        out_shape=[shape_of(rows, width), shape_of(8, width, dtype=F32)],
        compiler_params=params_of(),
        cost_estimate=cost(20 * rows * width, 2 * rows * width * 8),
        name="norm_back",
    )(h, g, gains, *firsts, *seconds, *deps)


def merge_kernel(h_ref, a0_ref, a1_ref, f0_ref, f1_ref, shifts_ref, out_ref, sums_ref):
    @pl.when(pl.program_id(0) == 0)
    def _():
        sums_ref[...] = jnp.zeros_like(sums_ref)

    state = h_ref[...].astype(F32)
    attention = a0_ref[...].astype(F32) + a1_ref[...].astype(F32) + shifts_ref[0:1]
    feedforward = f0_ref[...].astype(F32) + f1_ref[...].astype(F32) + shifts_ref[1:2]
    out_ref[...] = (state + attention + feedforward).astype(BF16)
    for row, term in enumerate((state, attention, feedforward)):
        sums_ref[row : row + 1, :] += jnp.sum(term * term, axis=0, keepdims=True)


def merge_call(h, attn_pair, ffn_pair, shifts, deps=()):
    rows, width = h.shape
    tile = min(128, rows)
    one = rows_of(tile, width)
    return pl.pallas_call(
        waiting(merge_kernel, 6, deps),
        grid=(rows // tile,),
        in_specs=[one] * 5 + [whole(shifts.shape)] + anywhere(len(deps)),
        out_specs=[one, whole((8, width))],
        out_shape=[shape_of(rows, width), shape_of(8, width, dtype=F32)],
        compiler_params=params_of(),
        cost_estimate=cost(10 * rows * width, 2 * rows * width * 6),
        name="merge",
    )(h, *attn_pair, *ffn_pair, shifts, *deps)


def tn(a, b):
    return lax.dot_general(a, b, (((0,), (0,)), ((), ())), preferred_element_type=F32)


def slope_kernel(count, terms, owners_ref, *refs):
    lefts = [jnp.concatenate([ref[...] for ref in refs[t * count : (t + 1) * count]], axis=1) for t in range(terms)]
    rights = refs[terms * count : terms * (count + 1)]
    outs = refs[terms * (count + 1) :]
    share = lefts[0].shape[1] // count
    total = sum(tn(left, right[...]) for left, right in zip(lefts, rights)).astype(BF16)
    first = pl.program_id(0) < pl.num_programs(0) // 2
    for ref, here in zip(outs, (first, jnp.logical_not(first))):

        @pl.when(here)
        def _():
            for index in range(count):
                ref[index] = total[index * share : (index + 1) * share]


def slope_call(owners, terms, name, cut=(0, 1), deps=()):
    total = owners.shape[0]
    share = terms[0][0].shape[1] // total
    columns = terms[0][1].shape[1] // cut[1]
    count = 4
    if share % 128 or total % (2 * count):
        pieces = 0.0
        row = 0
        for left, right, _ in terms:
            left_ordered = jnp.take(left.reshape(left.shape[0], total, share), owners, axis=1).reshape(left.shape)
            part = right[row : row + left.shape[0], cut[0] * columns : (cut[0] + 1) * columns]
            row += left.shape[0]
            pieces = pieces + tn(left_ordered, part)
        pieces = pieces.astype(BF16).reshape(total, share, columns)
        return pieces[: total // 2], pieces[total // 2 :]
    steps = total // count
    ins, specs = [], []
    for left, _, _ in terms:
        for index in range(count):
            ins.append(left)
            specs.append(
                pl.BlockSpec((left.shape[0], share), functools.partial(lambda i, r, o: (0, o[count * r + i]), index))
            )
    for left, right, row in terms:
        ins.append(right)
        specs.append(
            pl.BlockSpec((left.shape[0], columns), functools.partial(lambda i, r, o: (i, cut[0]), row))
        )
    return pl.pallas_call(
        waiting(functools.partial(slope_kernel, count, len(terms)), 1 + len(ins), deps),
        grid_spec=pltpu.PrefetchScalarGridSpec(
            num_scalar_prefetch=1,
            grid=(steps,),
            in_specs=specs + anywhere(len(deps)),
            out_specs=halves_of(count, steps // 2, share, columns),
        ),
        out_shape=[shape_of(total // 2, share, columns)] * 2,
        compiler_params=params_of(),
        cost_estimate=cost(
            sum(2 * a.size * columns for a, _, _ in terms),
            sum(2 * (a.size + a.shape[0] * columns) for a, _, _ in terms) + 2 * total * share * columns,
        ),
        name=name,
    )(owners, *ins, *deps)


class Sums:
    def __init__(self, masks, slots, send, receive, remote, totals):
        self.masks, self.slots, self.send, self.receive = masks, slots, send, receive
        self.remote, self.totals = remote, totals
        self.steps = [0] * len(masks)
        self.running = [None] * len(masks)
        self.kept = [None] * len(masks)
        self.first = [sum(len(m) for m in masks[:c]) for c in range(len(masks))]

    def launch(self, c, kept, sent):
        step = self.steps[c]
        number = self.first[c] + step
        self.kept[c] = kept
        self.running[c] = self.remote(
            sent, self.slots[c][step], self.send.at[number], self.receive.at[number], self.masks[c][step]
        )

    def halve(self, c, pieces, count):
        self.launch(c, pieces, pieces.at[pl.ds(count // 2, count // 2)])

    def go_on(self, c):
        self.running[c].wait_recv()
        slot = self.slots[c][self.steps[c]]
        count = slot.shape[0]
        total = self.kept[c][:count].astype(F32) + slot[...].astype(F32)
        self.steps[c] += 1
        if self.steps[c] == len(self.masks[c]):
            self.totals[c](total[0])
            return
        self.kept[c][:count] = total.astype(BF16)
        self.halve(c, self.kept[c], count)


def tail_kernel(masks, *refs):
    late, early = masks
    (dq_in, dk_in, dv_in, w_in, near_in, far_in, h_in, g_in, second0_in, second1_in, gains_ref, words_in, o0_in, o1_in,
     d0_in, d1_in, ua0_in, ua1_in, ub0_in, ub1_in) = refs[:20]
    o_out, joint_out, down_out, up_out, home_ref, words_out = refs[20:26]
    (dq, dk, dv, w, near, far, h, g, second0, second1, o0, d0, d1, ua0, ua1, ub0, ub1, jq, jk, jv,
     far1, far1_got, sums, arrived, near0, near1, near1_got, d_own, words, other_words) = refs[26:56]
    slots = refs[56:74]
    load, chain_send, chain_receive, side_send, side_receive, word_send, word_receive = refs[74:]
    me, core = lax.axis_index("ctx"), lax.axis_index("tp")
    size = words.shape[0]
    rows, width = h.shape
    seqs, _, block, _ = home_ref.shape
    chips = size // seqs
    seq = me // chips
    chip_rows = 2 * rows
    other_core = {"tp": 1 - core}
    started = []

    def at_ctx(mask):
        return {"ctx": exchanged(me, mask)}

    def send(source, target, first, second, device):
        copy = pltpu.make_async_remote_copy(
            source, target, first, second, device_id=device, device_id_type=pl.DeviceIdType.MESH
        )
        copy.start()
        started.append(copy)
        return copy

    def to_core(source, target, number):
        return send(source, target, side_send.at[number], side_receive.at[number], other_core)

    loads = {}
    order = (
        ("d0", d0_in, d0), ("d1", d1_in, d1), ("ua0", ua0_in, ua0), ("ua1", ua1_in, ua1), ("ub0", ub0_in, ub0),
        ("ub1", ub1_in, ub1), ("dk", dk_in, dk), ("dv", dv_in, dv), ("w", w_in, w), ("dq", dq_in, dq), ("near", near_in, near),
        ("far", far_in, far), ("o0", o0_in, o0), ("h", h_in, h), ("g", g_in, g), ("second0", second0_in, second0),
    )
    for number, (name, source, target) in enumerate(order):
        loads[name] = pltpu.make_async_copy(source, target, load.at[number])
        loads[name].start()

    barrier = pltpu.get_barrier_semaphore()
    for mask in range(1, size):
        pl.semaphore_signal(barrier, inc=1, device_id=at_ctx(mask), device_id_type=pl.DeviceIdType.MESH)
    pl.semaphore_signal(barrier, inc=1, device_id=other_core, device_id_type=pl.DeviceIdType.MESH)
    pl.semaphore_wait(barrier, size)

    units = up_out.shape[1]

    def put_output(total):
        o_out[...] = total.T

    def put_down(total):
        down_out[...] = total.T

    def put_joint(t):
        def write(total):
            joint_out[t] = total

        return write

    def put_up(start):
        def write(total):
            up_out[:, start : start + units // 2] = total

        return write

    chains = [late, late, late, late, early[1:], early[1:], late[1:]]
    parts, used = [], 0
    for chain in chains:
        parts.append(slots[used : used + len(chain)])
        used += len(chain)
    totals = [put_output, put_joint(0), put_joint(1), put_joint(2), put_up(0), put_up(units // 2), put_down]
    run = Sums(
        chains, parts, chain_send, chain_receive,
        lambda source, target, first, second, mask: send(source, target, first, second, at_ctx(mask)), totals,
    )
    run.launch(0, o0, o1_in)
    second_swap = to_core(second1_in, second1, 0)

    def ready(c, kept, other, names):
        for name in names:
            loads[name].wait()
        for index in range(kept.shape[0]):
            kept[index] = (kept[index].astype(F32) + other[index].astype(F32)).astype(BF16)
        run.halve(c, kept, kept.shape[0])

    ready(6, d0, d1, ("d0", "d1"))
    ready(4, ua0, ua1, ("ua0", "ua1"))
    ready(5, ub0, ub1, ("ub0", "ub1"))
    for name in ("dk", "dv", "w"):
        loads[name].wait()

    def from_far(start):
        cut = slice(start, start + rows)
        return dot_nt(dk[cut], w[1]) + dot_nt(dv[cut], w[2])

    far1[...] = from_far(chip_rows + rows).astype(BF16)
    swap = to_core(far1, far1_got, 1)
    mine = from_far(chip_rows)
    swap.wait_recv()
    sums[...] = (mine + far1_got[...].astype(F32)).astype(BF16)
    arrival = send(sums, arrived, side_send.at[2], side_receive.at[2], at_ctx(1))
    loads["dq"].wait()
    loads["near"].wait()
    loads["far"].wait()
    loads["o0"].wait()

    def from_near(cut):
        return sum(dot_nt(grad[cut], w[t]) for t, grad in enumerate((dq, dk, dv)))

    near1[...] = from_near(slice(rows, chip_rows)).astype(BF16)
    near_swap = to_core(near1, near1_got, 3)
    near0[...] = from_near(slice(0, rows)).astype(BF16)
    run.go_on(0)
    share = width // size
    count = 4
    owners = mask_order(late)
    for t, (target, grad) in enumerate(((jq, dq), (jk, dk), (jv, dv))):
        for start in range(0, size, count):
            spots = [pl.ds(pl.multiple_of(exchanged(me, m) * share, share), share) for m in owners[start : start + count]]
            total = tn(jnp.concatenate([near[:, spot] for spot in spots], axis=1), grad[:chip_rows])
            if t:
                total = total + tn(jnp.concatenate([far[:, spot] for spot in spots], axis=1), grad[chip_rows:])
            low = total.astype(BF16)
            for index in range(count):
                target[start + index] = low[index * share : (index + 1) * share]
        run.halve(1 + t, target, size)
        if t == 1:
            run.go_on(6)
    for name in ("h", "g", "second0"):
        loads[name].wait()
    for copy in (second_swap, near_swap, arrival):
        copy.wait_recv()
    gradients = [jnp.zeros((1, width), F32) for _ in range(5)]
    for s in range(seqs):
        cut = slice(s * block, (s + 1) * block)
        scaled, inverse = normalize(h[cut].astype(F32))
        upstream = g[cut].astype(F32)
        d_first = near0[cut].astype(F32) + near1_got[cut].astype(F32) + arrived[cut].astype(F32)
        d_second = second0[cut].astype(F32) + second1[cut].astype(F32)
        for row, term in enumerate((d_first * scaled, d_first, d_second * scaled, d_second, upstream)):
            gradients[row] = gradients[row] + jnp.sum(term, axis=0, keepdims=True)
        d_scaled = d_first * gains_ref[0:1] + d_second * gains_ref[1:2]
        middle = jnp.mean(d_scaled, axis=-1, keepdims=True)
        along = jnp.mean(d_scaled * scaled, axis=-1, keepdims=True)
        d_own[cut] = (upstream + inverse * (d_scaled - middle - scaled * along)).astype(BF16)
    home = []
    for s in range(seqs):
        source = d_own.at[pl.ds(s * block, block)]
        if s == 0:
            stay = pltpu.make_async_copy(source, home_ref.at[seq, core], load.at[len(order)])
            stay.start()
        else:
            number = 4 + s
            home.append(
                send(source, home_ref.at[seq, core], side_send.at[number], side_receive.at[number], at_ctx(s * chips))
            )
    lines = width // 128
    words_out[...] = words_in[...]
    for row in range(5):
        for line in range(lines):
            words_out[row * lines + line : row * lines + line + 1] = gradients[row][:, line * 128 : (line + 1) * 128]
    words[pl.ds(me, 1)] = words_out[...][None]
    word_copies = [
        send(words.at[me], words.at[me], word_send.at[mask], word_receive.at[mask], at_ctx(mask))
        for mask in range(1, size)
    ]
    for c in (0, 4, 1, 2, 5, 3, 1, 6, 4, 2, 0, 5, 3):
        run.go_on(c)
    stay.wait()
    swaps = []
    for s in range(seqs):
        if s:
            home[s - 1].wait_recv()
        place = home_ref.at[exchanged(seq, s), core]
        swaps.append(to_core(place, place, 4 + seqs + s))
    for copy in word_copies:
        copy.wait_recv()
    total = words[0]
    for index in range(1, size):
        total = total + words[index]
    core_words = other_words.shape[0]
    for copy in word_copies:
        copy.wait_send()
    words_out[...] = total
    swap = to_core(words_out.at[pl.ds(0, core_words)], other_words, 4)
    swap.wait_recv()
    swap.wait_send()
    words_out[pl.ds(0, core_words)] = total[:core_words] + other_words[...]
    for c in (1, 2, 3):
        run.go_on(c)
    for copy in swaps:
        copy.wait_recv()
    for copy in started:
        if copy is not swap and not any(copy is x for x in word_copies):
            copy.wait_send()


def tail_call(grads, w_joint, normals, h, g, seconds, gains, words, core_words, output, down, ups, masks, seqs, number):
    late, early = masks
    rows, width = h.shape
    chip_rows, local = grads[0].shape
    size = 1 << len(late)
    units = down[0].shape[2]
    share = width // size
    ins = (*grads, w_joint, *normals, h, g, *seconds, gains, words, *output, *down, *ups[0], *ups[1])
    specs = anywhere(len(ins))
    specs[10], specs[11] = whole(gains.shape), whole(words.shape)
    out = [
        shape_of(local, share, dtype=F32),
        shape_of(3, share, local, dtype=F32),
        shape_of(units, share, dtype=F32),
        shape_of(share, units, dtype=F32),
        shape_of(seqs, 2, rows // seqs, width),
        shape_of(*words.shape, dtype=F32),
    ]
    half = size // 2
    wide = (rows, width)
    scratch = [x.shape for x in (*grads, w_joint, *normals)] + [wide] * 4 + [output[0].shape]
    scratch += [down[0].shape] * 2 + [ups[0][0].shape] * 4 + [(size, share, local)] * 3 + [wide] * 8
    scratch = [pltpu.VMEM(shape, BF16) for shape in scratch]
    scratch += [pltpu.VMEM((size, *words.shape), F32), pltpu.VMEM((core_words, 128), F32)]
    for chain, columns, pieces in (
        (late, local, half), (late, local, half), (late, local, half), (late, local, half),
        (early[1:], units // 2, half // 2), (early[1:], units // 2, half // 2), (late[1:], units, half // 2),
    ):
        scratch += [pltpu.VMEM((pieces >> step, share, columns), BF16) for step in range(len(chain))]
    scratch += [pltpu.SemaphoreType.DMA((17,))] + carrier_semaphores(18)
    scratch += carrier_semaphores(4 + 2 * seqs) + carrier_semaphores(size)
    return pl.pallas_call(
        functools.partial(tail_kernel, masks),
        grid=(1,),
        in_specs=specs,
        out_specs=[pl.BlockSpec(memory_space=pl.ANY) if n == 4 else whole(x.shape) for n, x in enumerate(out)],
        out_shape=out,
        scratch_shapes=scratch,
        compiler_params=params_of(collective_id=number, has_side_effects=True),
        name="tail",
    )(*ins)


def finish_kernel(chains, events, seqs, chips, core_words, *refs):
    count = len(chains)
    ins, refs = refs[: 2 * count], refs[2 * count :]
    d_own_ref, words_ref = refs[:2]
    totals, home_ref, words_out = refs[2 : 2 + count], refs[2 + count], refs[3 + count]
    refs = list(refs[4 + count :])
    current = [refs.pop(0) for _ in chains]
    slots = [[refs.pop(0) for _ in chain[0]] for chain in chains]
    words, other_words, chain_send, chain_receive, home_send, home_receive, word_send, word_receive, local = refs
    me, core = lax.axis_index("ctx"), lax.axis_index("tp")
    size = words.shape[0]
    seq = me // chips
    block = home_ref.shape[2]

    def at_ctx(mask):
        return {"ctx": exchanged(me, mask)}

    other_core = {"tp": 1 - core}

    def remote(source, target, send, receive, device):
        return pltpu.make_async_remote_copy(
            source, target, send, receive, device_id=device, device_id_type=pl.DeviceIdType.MESH
        )

    barrier = pltpu.get_barrier_semaphore()
    for mask in range(1, size):
        pl.semaphore_signal(barrier, inc=1, device_id=at_ctx(mask), device_id_type=pl.DeviceIdType.MESH)
    pl.semaphore_signal(barrier, inc=1, device_id=other_core, device_id_type=pl.DeviceIdType.MESH)
    pl.semaphore_wait(barrier, size)

    started = []

    def begin(copy):
        copy.start()
        started.append(copy)
        return copy

    word_copies = [
        begin(remote(words_ref, words.at[me], word_send.at[mask], word_receive.at[mask], at_ctx(mask)))
        for mask in range(1, size)
    ]
    steps = [0] * count
    running = [None] * count
    number = [sum(len(chain[0]) for chain in chains[:c]) for c in range(count)]

    def launch(c, source):
        masks = chains[c][0]
        step = steps[c]
        n = number[c] + step
        running[c] = begin(
            remote(source, slots[c][step], chain_send.at[n], chain_receive.at[n], at_ctx(masks[step]))
        )

    def split(c):
        pieces = current[c].shape[0] >> (steps[c] + (0 if chains[c][1] else -1))
        launch(c, current[c].at[pl.ds(pieces // 2, pieces // 2)])

    home = []

    def send_home():
        copy = pltpu.make_async_copy(d_own_ref.at[pl.ds(0, block)], home_ref.at[seq, core], local)
        copy.start()
        for s in range(1, seqs):
            home.append(
                begin(
                    remote(
                        d_own_ref.at[pl.ds(s * block, block)], home_ref.at[seq, core],
                        home_send.at[s], home_receive.at[s], at_ctx(s * chips),
                    )
                )
            )
        copy.wait()

    def go_on(c):
        masks, ready = chains[c][:2]
        running[c].wait_recv()
        slot = slots[c][steps[c]]
        pieces = slot.shape[0]
        kept = ins[2 * c] if steps[c] == 0 and not ready else current[c]
        total = kept[:pieces].astype(F32) + slot[...].astype(F32)
        steps[c] += 1
        if steps[c] == len(masks):
            totals[c][...] = total[0]
            return
        current[c][:pieces] = total.astype(BF16)
        split(c)

    for c, (masks, ready, _) in enumerate(chains):
        if not ready:
            launch(c, ins[2 * c + 1])
    for c, (masks, ready, _) in enumerate(chains):
        if ready:
            current[c][...] = (ins[2 * c][...].astype(F32) + ins[2 * c + 1][...].astype(F32)).astype(BF16)
            split(c)
    send_home()
    words[pl.ds(me, 1)] = words_ref[...][None]
    for c in events:
        go_on(c)
    for copy in home:
        copy.wait_recv()
    swaps = []
    for s in range(seqs):
        place = home_ref.at[exchanged(seq, s), core]
        swaps.append(begin(remote(place, place, home_send.at[seqs + s], home_receive.at[seqs + s], other_core)))
    for copy in word_copies:
        copy.wait_recv()
    total = words[0]
    for index in range(1, size):
        total = total + words[index]
    words_out[...] = total
    swap = remote(words_out.at[pl.ds(0, core_words)], other_words, word_send.at[0], word_receive.at[0], other_core)
    swap.start()
    swap.wait()
    words_out[pl.ds(0, core_words)] = total[:core_words] + other_words[...]
    for copy in swaps:
        copy.wait_recv()
    for copy in started:
        copy.wait_send()


def finish_call(chains, events, d_own, words, core_words, seqs, chips, number):
    size = chips * seqs
    rows, width = d_own.shape
    block = rows // seqs
    ins, specs, out, scratch, slots = [], [], [], [], []
    for masks, ready, (kept, other) in chains:
        pieces, share, columns = kept.shape
        ins += [kept, other]
        specs += [whole(kept.shape), whole(other.shape) if ready else anywhere(1)[0]]
        out.append(shape_of(share, columns, dtype=F32))
        scratch.append(pltpu.VMEM((pieces, share, columns), BF16))
        slots += [
            pltpu.VMEM((pieces >> (step + 1 if ready else step), share, columns), BF16) for step in range(len(masks))
        ]
    copies = len(slots)
    scratch += slots + [pltpu.VMEM((size, *words.shape), F32), pltpu.VMEM((core_words, 128), F32)]
    scratch += carrier_semaphores(copies) + carrier_semaphores(2 * seqs) + carrier_semaphores(size)
    scratch += [pltpu.SemaphoreType.DMA]
    home = shape_of(seqs, 2, block, width)
    out_specs = [whole(x.shape) for x in out] + anywhere(1) + [whole(words.shape)]
    return pl.pallas_call(
        functools.partial(finish_kernel, [(m, r, None) for m, r, _ in chains], events, seqs, chips, core_words),
        grid=(1,),
        in_specs=specs + anywhere(1) + [whole(words.shape)],
        out_specs=out_specs,
        out_shape=out + [home, shape_of(*words.shape, dtype=F32)],
        scratch_shapes=scratch,
        compiler_params=params_of(collective_id=number, has_side_effects=True),
        name="finish",
    )(*ins, d_own, words)


def swap_core(shard):
    return lax.ppermute(shard, "tp", [(0, 1), (1, 0)])


def swap_ctx(shard, mask):
    return lax.ppermute(shard, "ctx", [(c, c ^ mask) for c in range(lax.axis_size("ctx"))])


def next_section(shard, by):
    size = lax.axis_size("section")
    return lax.ppermute(shard, "section", [(s, s + by) for s in range(size) if 0 <= s + by < size])


def mask_order(masks):
    order = [0]
    for mask in reversed(masks):
        order = order + [value ^ mask for value in order]
    return order


def on_device(
    tokens,
    cotangent,
    block_order,
    first_gain,
    first_bias,
    second_gain,
    second_bias,
    joint_weight,
    joint_bias,
    output_weight,
    output_bias,
    up_weight,
    up_bias,
    down_weight,
    down_bias,
):
    section = lax.axis_index("section")
    sections = lax.axis_size("section")
    ctx = lax.axis_index("ctx")
    ctx_size = lax.axis_size("ctx")
    core = lax.axis_index("tp")
    seqs, local_len, width = tokens.shape
    block = local_len // 2
    chips = ctx_size // seqs
    seq, member = ctx // chips, ctx % chips
    rows = seqs * block
    chip_rows = 2 * rows
    length = chips * chip_rows
    seq_masks = [chips << b for b in range((seqs - 1).bit_length())]
    member_masks = [1 << b for b in range((chips - 1).bit_length())]

    k, u, a = jnp.meshgrid(jnp.arange(chips), jnp.arange(2), jnp.arange(seqs), indexing="ij")
    stored = (2 * ((seq ^ a) * chips + (member ^ k)) + (core ^ u)).reshape(-1)
    places = block_order[stored]
    spots = (places[:, None] * block + jnp.arange(block, dtype=jnp.int32)).reshape(-1)
    exponent = jnp.arange(ROT // 2, dtype=F32) * (2.0 / ROT)
    inverse = jnp.power(jnp.float32(ROTARY_BASE), -exponent)
    turns = spots.astype(F32)[:, None] * inverse[None, :]
    cosine, sine = jnp.cos(turns), jnp.sin(turns)
    rest = jnp.zeros((length, HEAD - ROT), F32)
    table = (
        jnp.tile(jnp.concatenate([cosine, cosine, rest + 1.0], 1), (1, 128 // HEAD)),
        jnp.tile(jnp.concatenate([sine, sine, rest], 1), (1, 128 // HEAD)),
    )

    tile = max(block, 128)
    tile_places = places[: chip_rows // block].reshape(-1, tile // block)
    lowest, highest = jnp.min(tile_places, 1), jnp.max(tile_places, 1)
    limits = jnp.stack([(lowest * block + 1) // KEY_TILE, (highest * block + block - 1) // KEY_TILE + 1], 1)

    gain_one, shift_one, gain_two, shift_two = first_gain, first_bias, second_gain, second_bias
    w_joint, b_joint = joint_weight[0], joint_bias[0]
    w_output, b_output = output_weight[0], output_bias
    w_up, b_up = up_weight[0], up_bias
    w_down, b_down = down_weight[0], down_bias
    gains = jnp.concatenate([gain_one, gain_two], 0)
    norms = jnp.concatenate([gain_one, shift_one, gain_two, shift_two], 0)
    shifts = jnp.concatenate([b_output, b_down], 0)

    def plane_parts(values):
        mine = lax.dynamic_slice_in_dim(values, core * block, block, 1)
        return [lax.dynamic_index_in_dim(mine, seq ^ shift, 0, keepdims=False) for shift in range(seqs)]

    def from_planes(values):
        parts = values.reshape(seqs, block, width)
        return [parts[s] if s == 0 else swap_ctx(parts[s], s * chips) for s in range(seqs)]

    def in_order(parts):
        parts = jnp.stack(parts)
        both = jnp.stack([parts, swap_core(parts)], 1)
        ordered = [
            lax.dynamic_index_in_dim(lax.dynamic_index_in_dim(both, s ^ seq, 0, False), v ^ core, 0, False)
            for s in range(seqs)
            for v in range(2)
        ]
        return jnp.stack(ordered).reshape(1, seqs, local_len, width)

    def paired(parts):
        count = len(parts) // 2
        return tuple(x[0] if count == 1 else jnp.concatenate(x, 0) for x in (parts[:count], parts[count:]))

    def forward(own, save, moves, moved, name, number):
        chip = (own, swap_core(own))
        moves = [("ctx", k) for k in range(1, chips)] + moves
        outs, arrived = front_call(
            chip, norms, w_joint, b_joint, table, w_up, b_up, w_down, save, moves, [own] * (chips - 1) + moved, name, number
        )
        normal, keys, values, queries, ffn0, ffn1, *kept_ffn = outs
        others, arrived = arrived[: chips - 1], arrived[chips - 1 :]
        key_parts, value_parts, normal_parts = [keys], [values], [normal]
        if chips > 1:
            rest = paired([x for other in others for x in (other, swap_core(other))])
            far_normal, far_keys, far_values = joint_call(
                rest, gain_one, shift_one, w_joint, b_joint, table, chip_rows
            )
            key_parts.append(far_keys)
            value_parts.append(far_values)
            normal_parts.append(far_normal)
        attn0, attn1, mixture, lse = attend_call(queries, key_parts, value_parts, places, limits, w_output, block)
        result, moments = merge_call(own, (attn0, swap_core(attn1)), (ffn0, swap_core(ffn1)), shifts)
        return result, moments, (normal_parts, queries, key_parts, value_parts, mixture, lse, *kept_ffn), arrived

    def attention_back(g_pair, kept, deps=()):
        normal_parts, queries, key_parts, value_parts, mixture, lse, second_in, active, slope = kept
        return attend_back_call(
            queries, g_pair, mixture, lse, key_parts, value_parts, places, limits, w_output, table, block, deps
        )

    def far_back(d_keys, d_values, deps=()):
        if chips == 1:
            return []
        far = joint_back_call([d_keys, d_values], chip_rows, length - chip_rows, w_joint, deps)
        if chips > 2:
            far = jnp.concatenate(far, 0).reshape(chips - 1, 2, rows, width)
            far = far[:, 0], far[:, 1]
        sums = (far[0].astype(F32) + swap_core(far[1]).astype(F32)).astype(BF16).reshape(chips - 1, rows, width)
        return [sums[k - 1] for k in range(1, chips)]

    others = [("ctx", k) for k in range(1, chips)]
    planes = [("ctx", s * chips) for s in range(1, seqs)]
    token_parts = plane_parts(tokens)
    token_rows = jnp.concatenate([token_parts[0]] + [swap_ctx(token_parts[s], s * chips) for s in range(1, seqs)], 0)
    g_parts = plane_parts(cotangent)
    own = token_rows
    for tick in range(sections):
        first = tick == 0
        result, moments, kept, arrived = forward(
            own, tick == sections - 1, planes if first else [], g_parts[1:] if first else [], "front" + str(tick), tick
        )
        if first:
            g_rows = jnp.concatenate([g_parts[0], *arrived], 0)
        if tick < sections - 1:
            own = jnp.where(section == 0, token_rows, next_section(result, 1))
    out_parts = from_planes(result)
    moments = jnp.sum(moments[:3], axis=1)
    normal_parts, queries, key_parts, value_parts, mixture, lse, second_in, active, slope = kept
    g_own = g_rows
    for tick in range(sections - 1):
        g_pair = (g_own, swap_core(g_own))
        d_queries, d_keys, d_values, _ = attention_back(g_pair, kept)
        sums = far_back(d_keys, d_values, tuple(out_parts) if tick == 0 else ())
        near, second, arrivals = rear_call(
            (d_queries, d_keys, d_values), w_joint, g_pair, slope, w_up, w_down, others, sums, "rear" + str(tick), sections + tick
        )
        firsts = [near[0], swap_core(near[1]), *arrivals]
        d_own, _ = norm_back_call(own, g_own, firsts, [second[0], swap_core(second[1])], gains)
        g_own = jnp.where(section == sections - 1, g_rows, next_section(d_own, -1))
    section_out = in_order(out_parts)

    local = w_output.shape[0]
    units = w_up.shape[1]

    def results(section_out, home, small, core_words, joint_total, output_total, up_total, down_total):
        both, ones = small[:core_words].reshape(-1), small[core_words:].reshape(-1)
        norm_total = both[: 5 * width].reshape(5, 1, width)
        root_means = jnp.sqrt(both[5 * width : 5 * width + 3] / (length * seqs * width))
        return (
            section_out,
            home.reshape(1, seqs, local_len, width),
            norm_total[0],
            norm_total[1],
            norm_total[2],
            norm_total[3],
            joint_total[None],
            ones[: 3 * local].reshape(1, 3, local),
            output_total[None],
            norm_total[4],
            up_total[None],
            ones[3 * local : 3 * local + units].reshape(1, units),
            down_total[None],
            norm_total[4],
            root_means[None],
        )

    late = tuple(member_masks + seq_masks)
    early = tuple(seq_masks + member_masks)
    late_owners = jnp.stack([ctx ^ m for m in mask_order(late)]).astype(jnp.int32)
    early_owners = jnp.stack([ctx ^ m for m in mask_order(early)]).astype(jnp.int32)
    share = width // ctx_size
    g_pair = (g_own, swap_core(g_own))
    by_blocks = share % 128 == 0 and chips == 2

    def of_g(right, name, deps=()):
        if by_blocks:
            terms = [(g_pair[0], right, 0), (g_pair[1], right, 1)]
        else:
            terms = [(jnp.concatenate(g_pair, 0), right, 0)]
        return slope_call(late_owners, terms, name, (0, 1), deps)

    down = of_g(active, "down_slope")
    down_arrived = swap_ctx(down[1], late[0])
    output = of_g(mixture, "output_slope", (down[0],))
    second0, second1, d_hidden, up_sums = ffn_back_call(g_pair, slope, w_up, w_down, (output[0],))
    ups = [slope_call(early_owners, [(second_in, d_hidden, 0)], "up_slope", (0, 2))]
    ups.append(slope_call(early_owners, [(second_in, d_hidden, 0)], "up_slope", (1, 2), (ups[0][0],)))
    ups_arrived = [swap_ctx(part[1], early[0]) for part in ups]
    d_queries, d_keys, d_values, joint_sums = attention_back(g_pair, kept, (ups[1][0], output[0]))
    seconds = [second0, second1]

    def in_words(values):
        values = values.reshape(-1)
        return jnp.pad(values, (0, -values.size % 1024)).reshape(-1, 128)

    grads = (d_queries, d_keys, d_values)
    ones = in_words(jnp.concatenate([joint_sums[:3].reshape(-1), up_sums.reshape(-1)]))
    if by_blocks and len(late) == 3:
        both = in_words(jnp.concatenate([jnp.zeros((5 * width,), F32), moments]))
        pairs = [(part[0], there) for part, there in zip(ups, ups_arrived)]
        output_total, joint_total, down_total, up_total, home, small = tail_call(
            grads, w_joint, normal_parts, own, g_own, seconds, gains, jnp.concatenate([both, ones], 0), both.shape[0],
            output, (down[0], down_arrived), pairs, (late, early), seqs, 2 * sections,
        )
        return results(section_out, home, small, both.shape[0], joint_total, output_total, up_total, down_total)
    sums = far_back(d_keys, d_values, (down_arrived, *ups_arrived))

    def halved(pair, arrived):
        total = (pair[0].astype(F32) + arrived.astype(F32)).astype(BF16)
        return total[: total.shape[0] // 2], total[total.shape[0] // 2 :]

    down = halved(down, down_arrived)
    ups[0] = halved(ups[0], ups_arrived[0])
    near = joint_back_call(grads, 0, chip_rows, w_joint)
    down_arrived, ups_arrived[0] = swap_ctx(down[1], late[1]), swap_ctx(ups[0][1], early[1])
    arrivals = [swap_ctx(part, k + 1) for k, part in enumerate(sums)]
    joints = [slope_call(late_owners, [(normal_parts[0], d_queries, 0)], "query_slope")]
    for grad in grads[1:]:
        joints.append(slope_call(late_owners, [(part, grad, n) for n, part in enumerate(normal_parts)], "key_slope"))
    firsts = [near[0], swap_core(near[1]), *arrivals]
    d_own, norm_sums = norm_back_call(own, g_own, firsts, [second0, swap_core(second1)], gains)
    both = in_words(jnp.concatenate([norm_sums[:5].reshape(-1), moments]))
    chains = [
        (late, False, output),
        (late, False, joints[0]),
        (late, False, joints[1]),
        (late, False, joints[2]),
        (early[1:], True, (ups[1][0], ups_arrived[1])),
        (late[2:], True, (down[0], down_arrived)),
        (early[2:], True, (ups[0][0], ups_arrived[0])),
    ]
    events = [c for step in range(len(late)) for c, chain in enumerate(chains) if step < len(chain[0])]
    output_total, *joint_total, up_right, down_total, up_left, home, small = finish_call(
        chains, events, d_own, jnp.concatenate([both, ones], 0), both.shape[0], seqs, chips, 2 * sections + 1
    )
    joint_total = jnp.stack(joint_total)
    up_total = jnp.concatenate([up_left, up_right], 1)
    output_total, down_total = output_total.T, down_total.T
    return results(section_out, home, small, both.shape[0], joint_total, output_total, up_total, down_total)


def solution(mesh):
    in_specs = (
        P(None, "ctx", None),
        P(None, "ctx", None),
        P(),
        P("section", None),
        P("section", None),
        P("section", None),
        P("section", None),
        P("section", None, None, "tp"),
        P("section", None, "tp"),
        P("section", "tp", None),
        P("section", None),
        P("section", None, "tp"),
        P("section", "tp"),
        P("section", "tp", None),
        P("section", None),
    )
    out_specs = (
        P("section", None, "ctx", None),
        P("section", None, "ctx", None),
        P("section", None),
        P("section", None),
        P("section", None),
        P("section", None),
        P("section", None, "ctx", "tp"),
        P("section", None, "tp"),
        P("section", "tp", "ctx"),
        P("section", None),
        P("section", "ctx", "tp"),
        P("section", "tp"),
        P("section", "tp", "ctx"),
        P("section", None),
        P("section", None),
    )
    return jax.shard_map(
        on_device, mesh=mesh, in_specs=in_specs, out_specs=out_specs, check_vma=False
    )
```

```python
import functools

import jax
import jax.numpy as jnp
from jax import lax
from jax.experimental import pallas as pl
from jax.experimental.pallas import tpu as pltpu
from jax.sharding import PartitionSpec as P

HEAD = 64
ROT = 16
EPS = 1e-05
ROTARY_BASE = 10000.0
NEGATIVE = -1e30
SEQS = 4
STACK = 4
GROUP = STACK * HEAD
KEY_TILE = 512
VMEM_LIMIT = 60 * 1024 * 1024
BF16 = jnp.bfloat16
F32 = jnp.float32


def dot(a, b):
    return jnp.dot(a, b, preferred_element_type=F32)


def dot_nt(a, b):
    return lax.dot_general(a, b, (((1,), (1,)), ((), ())), preferred_element_type=F32)


def params_of(**more):
    return pltpu.CompilerParams(vmem_limit_bytes=VMEM_LIMIT, **more)


def whole(shape):
    return pl.BlockSpec(shape, lambda *_: (0,) * len(shape))


def rows_of(tile, *rest):
    return pl.BlockSpec((tile, *rest), lambda r, *_: (r,) + (0,) * len(rest))


def halves_of(tile, count, *rest):
    return [
        pl.BlockSpec((tile, *rest), lambda r, *_: (jnp.minimum(r, count - 1),) + (0,) * len(rest)),
        pl.BlockSpec((tile, *rest), lambda r, *_: (jnp.maximum(r - count, 0),) + (0,) * len(rest)),
    ]


def pick(refs):
    return jnp.where(pl.program_id(0) < pl.num_programs(0) // 2, refs[0][...], refs[1][...])


def put(refs, value):
    first = pl.program_id(0) < pl.num_programs(0) // 2
    for ref, here in zip(refs, (first, jnp.logical_not(first))):

        @pl.when(here)
        def _():
            ref[...] = value


def waiting(kernel, inputs, deps):
    return lambda *refs: kernel(*refs[:inputs], *refs[inputs + len(deps) :])


def exchanged(position, mask):
    for bit in range(mask.bit_length()):
        if mask >> bit & 1:
            position = position + (1 << bit) - (2 << bit) * (position // (1 << bit) % 2)
    return position


def carrying(kernel, inputs, outputs, moves):
    count = len(moves)

    def body(*refs):
        sources = refs[inputs : inputs + count]
        outs = refs[inputs + count : inputs + count + outputs]
        targets = refs[inputs + count + outputs : inputs + 2 * count + outputs]
        *scratch, send, receive = refs[inputs + 2 * count + outputs :]
        partners = [{axis: exchanged(lax.axis_index(axis), mask)} for axis, mask in moves]
        copies = [
            pltpu.make_async_remote_copy(
                source, target, send.at[n], receive.at[n], device_id=partner, device_id_type=pl.DeviceIdType.MESH
            )
            for n, (source, target, partner) in enumerate(zip(sources, targets, partners))
        ]

        @pl.when(pl.program_id(0) == 0)
        def _():
            barrier = pltpu.get_barrier_semaphore()
            for partner in partners:
                pl.semaphore_signal(barrier, inc=1, device_id=partner, device_id_type=pl.DeviceIdType.MESH)
            pl.semaphore_wait(barrier, count)
            for copy in copies:
                copy.start()

        kernel(*refs[:inputs], *outs, *scratch)

        @pl.when(pl.program_id(0) == pl.num_programs(0) - 1)
        def _():
            for copy in copies:
                copy.wait()

    return body


def carrier_semaphores(count):
    return [pltpu.SemaphoreType.DMA((count,)), pltpu.SemaphoreType.DMA((count,))]


def anywhere(count):
    return [pl.BlockSpec(memory_space=pl.ANY)] * count


def cost(flops, size):
    return pl.CostEstimate(flops=int(flops), bytes_accessed=int(size), transcendentals=0)


def shape_of(*shape, dtype=BF16):
    return jax.ShapeDtypeStruct(shape, dtype)


def normalize(values):
    middle = jnp.mean(values, axis=-1, keepdims=True)
    centered = values - middle
    spread = jnp.mean(centered * centered, axis=-1, keepdims=True)
    inverse = lax.rsqrt(spread + EPS)
    return centered * inverse, inverse


def turn(values, cosine, sine):
    pieces = []
    for start in range(0, values.shape[1], 128):
        part = values[:, start : start + 128]
        ahead = pltpu.roll(part, 128 - ROT // 2, 1)
        behind = pltpu.roll(part, ROT // 2, 1)
        entry = lax.broadcasted_iota(jnp.int32, part.shape, 1) % HEAD
        pieces.append(part * cosine + jnp.where(entry < ROT // 2, -ahead, behind) * sine)
    return jnp.concatenate(pieces, axis=1)


def joint_kernel(h0_ref, h1_ref, gain_ref, shift_ref, w_ref, b_ref, cos_ref, sin_ref, n_ref, k_ref, v_ref):
    scaled, _ = normalize(pick((h0_ref, h1_ref)).astype(F32))
    low = (scaled * gain_ref[...] + shift_ref[...]).astype(BF16)
    n_ref[...] = low
    cosine, sine = cos_ref[...], sin_ref[...]
    keys = dot(low, w_ref[1]) + b_ref[1:2]
    values = dot(low, w_ref[2]) + b_ref[2:3]
    k_ref[...] = turn(keys, cosine, sine).astype(BF16)
    v_ref[...] = values.astype(BF16)


def joint_call(pair, gain, shift, w_joint, b_joint, table, offset, deps=()):
    rows, width = pair[0].shape
    local = w_joint.shape[2]
    tile = min(512, rows)
    first = offset // tile
    count = 2
    turns = pl.BlockSpec((tile, 128), lambda r: (first + r, 0))
    return pl.pallas_call(
        waiting(joint_kernel, 8, deps),
        grid=(2 * rows // tile,),
        in_specs=halves_of(tile, rows // tile, width)
        + [whole((1, width)), whole((1, width)), whole(w_joint.shape), whole(b_joint.shape), turns, turns]
        + anywhere(len(deps)),
        out_specs=[rows_of(tile, width)] + [rows_of(tile, local)] * count,
        out_shape=[shape_of(2 * rows, width)] + [shape_of(2 * rows, local)] * count,
        compiler_params=params_of(),
        cost_estimate=cost(4 * rows * width * local * count, 8 * rows * width + 2 * w_joint.size),
        name="joint_projection",
    )(*pair, gain, shift, w_joint, b_joint, *table, *deps)


def gelu_parts(x):
    return 0.5 + 0.5 * lax.erf(x * 0.5**0.5), jnp.exp(-0.5 * x * x)


def front_kernel(
    save, h0_ref, h1_ref, norms_ref, w_ref, b_ref, cos_ref, sin_ref, up_ref, up_b_ref, down_ref,
    n_ref, k_ref, v_ref, q_ref, part0_ref, part1_ref, *saved
):
    scaled, _ = normalize(pick((h0_ref, h1_ref)).astype(F32))
    low = (scaled * norms_ref[0:1] + norms_ref[1:2]).astype(BF16)
    n_ref[...] = low
    cosine, sine = cos_ref[...], sin_ref[...]
    keys = dot(low, w_ref[1]) + b_ref[1:2]
    values = dot(low, w_ref[2]) + b_ref[2:3]
    queries = dot(low, w_ref[0]) + b_ref[0:1]
    q_ref[...] = (turn(queries, cosine, sine) * HEAD ** (-0.5)).astype(BF16)
    k_ref[...] = turn(keys, cosine, sine).astype(BF16)
    v_ref[...] = values.astype(BF16)
    low = (scaled * norms_ref[2:3] + norms_ref[3:4]).astype(BF16)
    if save:
        saved[0][...] = low
    total = None
    for start in range(0, up_ref.shape[1], 512):
        cut = pl.ds(start, 512)
        hidden = dot(low, up_ref[:, cut]) + up_b_ref[:, cut]
        share, bell = gelu_parts(hidden)
        active = (hidden * share).astype(BF16)
        if save:
            saved[1][:, cut] = active
            saved[2][:, cut] = (share + hidden * bell * 0.3989422804014327).astype(BF16)
        term = dot(active, down_ref[cut, :])
        total = term if total is None else total + term
    put((part0_ref, part1_ref), total.astype(BF16))


def front_call(pair, norms, w_joint, b_joint, table, w_up, b_up, w_down, save, moves, moved, name, number):
    rows, width = pair[0].shape
    local = w_joint.shape[2]
    units = w_up.shape[1]
    tile = min(512, rows)
    out = [shape_of(2 * rows, width)] + [shape_of(2 * rows, local)] * 3 + [shape_of(rows, width)] * 2
    out_specs = [rows_of(tile, width)] + [rows_of(tile, local)] * 3 + halves_of(tile, rows // tile, width)
    if save:
        out += [shape_of(2 * rows, width)] + [shape_of(2 * rows, units)] * 2
        out_specs += [rows_of(tile, width), rows_of(tile, units), rows_of(tile, units)]
    ins = (norms, w_joint, b_joint, *table, w_up, b_up, w_down)
    turns = rows_of(tile, 128)
    specs = [turns if x is table[0] or x is table[1] else whole(x.shape) for x in ins]
    outs = pl.pallas_call(
        carrying(functools.partial(front_kernel, save), 2 + len(ins), len(out), moves),
        grid=(2 * rows // tile,),
        in_specs=halves_of(tile, rows // tile, width) + specs + anywhere(len(moves)),
        out_specs=out_specs + anywhere(len(moves)),
        out_shape=out + [shape_of(*x.shape) for x in moved],
        scratch_shapes=carrier_semaphores(len(moves)),
        compiler_params=params_of(collective_id=number, has_side_effects=True),
        cost_estimate=cost(4 * rows * width * (3 * local + 2 * units), 4 * w_up.size + 16 * rows * width),
        name=name,
    )(*pair, *ins, *moved)
    return outs[: len(out)], outs[len(out) :]


class Traffic:
    def __init__(self):
        self.started = []

    def send(self, source, target, first, second, device):
        copy = pltpu.make_async_remote_copy(
            source, target, first, second, device_id=device, device_id_type=pl.DeviceIdType.MESH
        )
        copy.start()
        self.started.append(copy)
        return copy

    def finish(self):
        for copy in self.started:
            copy.wait_send()


def greet(partners):
    barrier = pltpu.get_barrier_semaphore()
    for partner in partners:
        pl.semaphore_signal(barrier, inc=1, device_id=partner, device_id_type=pl.DeviceIdType.MESH)
    pl.semaphore_wait(barrier, len(partners))


def gather_kernel(first, save, seqs, *refs):
    refs = list(refs)
    take = lambda count: [refs.pop(0) for _ in range(count)]
    norms_ref, b_joint_ref, cos_ref, sin_ref, up_b_ref, w_in, up_in, down_in = take(8)
    if first:
        tokens_ref, cotangent_ref = take(2)
    else:
        shifts_ref, a0_in, a1_in, f0_in, f1_in, h_in = take(6)
    outs = take(13 if save else 10)
    own_out, far_outs, near_outs = outs[0], outs[1:4], outs[4:]
    if first:
        g_out = take(1)[0]
    own, other, far0, far1, w, up, down = take(7)
    far_stage = take(3)
    near_stage = take(len(near_outs))
    if not first:
        a0, a1, f0, f1, h, got, a_got, f_got = take(8)
    load, store, arrive_s, arrive_r, core_s, core_r, chip_s, chip_r, far_s, far_r, side_s, side_r = refs
    me, core, section = lax.axis_index("ctx"), lax.axis_index("tp"), lax.axis_index("section")
    rows, width = own.shape
    block = rows // seqs
    chips = 2
    seq = me // chips
    other_core, other_chip, twin = {"tp": 1 - core}, {"ctx": exchanged(me, 1)}, {"section": 1 - section}
    traffic = Traffic()

    def at(c):
        return pl.ds(c * block, block)

    copies = [pltpu.make_async_copy(a, b, load.at[n]) for n, (a, b) in enumerate(((w_in, w), (up_in, up), (down_in, down)))]
    if not first:
        extra = [
            pltpu.make_async_copy(a, b, load.at[3 + n])
            for n, (a, b) in enumerate(((a0_in, a0), (f0_in, f0), (h_in, h)))
        ]
        for copy in extra:
            copy.start()
    for copy in copies:
        copy.start()
    if first:
        planes = [{"ctx": exchanged(me, c * chips)} for c in range(1, seqs)]
        greet([other_core, other_chip] + planes)
        mine = pl.ds(pl.multiple_of(core * block, block), block)
        stay = [
            pltpu.make_async_copy(tokens_ref.at[seq, mine], own.at[at(0)], load.at[3]),
            pltpu.make_async_copy(cotangent_ref.at[seq, mine], g_out.at[at(0)], load.at[4]),
        ]
        for copy in stay:
            copy.start()
        arrivals = [None]
        for c in range(1, seqs):
            source = tokens_ref.at[exchanged(seq, c), mine]
            arrivals.append(traffic.send(source, own.at[at(c)], arrive_s.at[c], arrive_r.at[c], planes[c - 1]))
        sides = []
        for c in range(1, seqs):
            source = cotangent_ref.at[exchanged(seq, c), mine]
            sides.append(traffic.send(source, g_out.at[at(c)], side_s.at[c], side_r.at[c], planes[c - 1]))
    else:
        greet([other_core, other_chip, twin])
        swaps = [
            traffic.send(a1_in, a_got, side_s.at[0], side_r.at[0], other_core),
            traffic.send(f1_in, f_got, side_s.at[1], side_r.at[1], other_core),
        ]
        for copy in extra:
            copy.wait()
        for copy in swaps:
            copy.wait_recv()
        arrivals = []
        for c in range(seqs):
            cut = slice(c * block, (c + 1) * block)
            attention = a0[cut].astype(F32) + a_got[cut].astype(F32) + shifts_ref[0:1]
            feedforward = f0[cut].astype(F32) + f_got[cut].astype(F32) + shifts_ref[1:2]
            a1[cut] = (h[cut].astype(F32) + attention + feedforward).astype(BF16)
            arrivals.append(traffic.send(a1.at[at(c)], got.at[at(c)], arrive_s.at[c], arrive_r.at[c], twin))

    to_core, to_chip, to_far = [None] * seqs, [None] * seqs, [None] * seqs

    def arrive(c):
        if first and c == 0:
            stay[0].wait()
        else:
            arrivals[c].wait_recv()
        if not first:
            cut = slice(c * block, (c + 1) * block)
            own[cut] = jnp.where(section == 0, h[cut], got[cut])
        here = own.at[at(c)]
        to_core[c] = traffic.send(here, other.at[at(c)], core_s.at[c], core_r.at[c], other_core)
        to_chip[c] = traffic.send(here, far0.at[at(c)], chip_s.at[c], chip_r.at[c], other_chip)

    def arrive_far(c):
        to_chip[c].wait_recv()
        to_far[c] = traffic.send(far0.at[at(c)], far1.at[at(c)], far_s.at[c], far_r.at[c], other_core)

    n_st, k_st, v_st, q_st, part0_st, part1_st = near_stage[:6]
    half = rows // 2

    def near_rows(ref, part, value, base=0):
        ref[base + part * half : base + (part + 1) * half] = value

    def near_joint(part):
        cut = slice(part * half, (part + 1) * half)
        scaled, _ = normalize(jnp.concatenate([own[cut], other[cut]], 0).astype(F32))
        low = (scaled * norms_ref[0:1] + norms_ref[1:2]).astype(BF16)
        second = (scaled * norms_ref[2:3] + norms_ref[3:4]).astype(BF16)
        turns = [
            jnp.concatenate([ref[cut], ref[rows + part * half : rows + (part + 1) * half]], 0) for ref in (cos_ref, sin_ref)
        ]
        queries = turn(dot(low, w[0]) + b_joint_ref[0:1], *turns) * HEAD ** (-0.5)
        keys = turn(dot(low, w[1]) + b_joint_ref[1:2], *turns)
        values = dot(low, w[2]) + b_joint_ref[2:3]
        for ref, value in ((n_st, low), (q_st, queries), (k_st, keys), (v_st, values)):
            value = value.astype(BF16)
            near_rows(ref, part, value[:half])
            near_rows(ref, part, value[half:], rows)
        if save:
            near_rows(near_stage[6], part, second[:half])
            near_rows(near_stage[6], part, second[half:], rows)
        return second

    def near_ffn(part, low):
        total = None
        for start in range(0, up.shape[1], 512):
            cut = slice(start, start + 512)
            hidden = dot(low, up[:, cut]) + up_b_ref[:, cut]
            share, bell = gelu_parts(hidden)
            active = (hidden * share).astype(BF16)
            if save:
                slope = (share + hidden * bell * 0.3989422804014327).astype(BF16)
                for ref, value in ((near_stage[7], active), (near_stage[8], slope)):
                    ref[part * half : (part + 1) * half, cut] = value[:half]
                    ref[rows + part * half : rows + (part + 1) * half, cut] = value[half:]
            term = dot(active, down[cut, :])
            total = term if total is None else total + term
        near_rows(part0_st, part, total[:half].astype(BF16))
        near_rows(part1_st, part, total[half:].astype(BF16))

    def far_joint(u, ref):
        scaled, _ = normalize(ref[...].astype(F32))
        low = (scaled * norms_ref[0:1] + norms_ref[1:2]).astype(BF16)
        cut = slice(u * rows, (u + 1) * rows)
        turns = [table[2 * rows + u * rows : 2 * rows + (u + 1) * rows] for table in (cos_ref, sin_ref)]
        far_stage[0][cut] = low
        far_stage[1][cut] = turn(dot(low, w[1]) + b_joint_ref[1:2], *turns).astype(BF16)
        far_stage[2][cut] = (dot(low, w[2]) + b_joint_ref[2:3]).astype(BF16)

    arrive(0)
    arrive(1)
    copies[0].wait()
    for c in (0, 1):
        to_core[c].wait_recv()
    low = near_joint(0)
    if not first:
        arrive(2)
    copies[1].wait()
    copies[2].wait()
    near_ffn(0, low)
    if first:
        arrive(2)
    arrive(3)
    arrive_far(0)
    arrive_far(1)
    for c in (2, 3):
        to_core[c].wait_recv()
    low = near_joint(1)
    arrive_far(2)
    near_ffn(1, low)
    arrive_far(3)
    stores = [pltpu.make_async_copy(own, own_out, store.at[0])]
    stores += [pltpu.make_async_copy(a, b, store.at[1 + n]) for n, (a, b) in enumerate(zip(near_stage, near_outs))]
    for copy in stores:
        copy.start()
    far_joint(0, far0)
    for c in range(seqs):
        to_far[c].wait_recv()
    far_joint(1, far1)
    base = 1 + len(near_outs)
    late = [pltpu.make_async_copy(a, b, store.at[base + n]) for n, (a, b) in enumerate(zip(far_stage, far_outs))]
    for copy in late:
        copy.start()
    if first:
        stay[1].wait()
        for copy in sides:
            copy.wait_recv()
    traffic.finish()
    for copy in stores + late:
        copy.wait()


def gather_call(first, save, norms, w_joint, b_joint, table, w_up, b_up, w_down, sources, name, number):
    rows = (sources[0].shape[0] * sources[0].shape[1] // 2) if first else sources[-1].shape[0]
    seqs = SEQS
    width, local, units = w_up.shape[0], w_joint.shape[2], w_up.shape[1]
    wide, narrow = (rows, width), (2 * rows, local)
    near = [(2 * rows, width), narrow, narrow, narrow, wide, wide]
    if save:
        near += [(2 * rows, width), (2 * rows, units), (2 * rows, units)]
    far = [(2 * rows, width), narrow, narrow]
    out = [wide, *far, *near] + ([wide] if first else [])
    ins = (norms, b_joint, *table, b_up)
    extra = [] if first else [whole(sources[0].shape)]
    scratch = [wide] * 4 + [w_joint.shape, w_up.shape, w_down.shape] + far + near + ([] if first else [wide] * 8)
    pair = carrier_semaphores(seqs)
    return pl.pallas_call(
        functools.partial(gather_kernel, first, save, seqs),
        grid=(1,),
        in_specs=[whole(x.shape) for x in ins] + anywhere(3) + extra + anywhere(len(sources) - len(extra)),
        out_specs=anywhere(len(out)),
        out_shape=[shape_of(*x) for x in out],
        scratch_shapes=[pltpu.VMEM(x, BF16) for x in scratch]
        + [pltpu.SemaphoreType.DMA((6,)), pltpu.SemaphoreType.DMA((len(out),))]
        + pair * 5,
        compiler_params=params_of(collective_id=number, has_side_effects=True),
        name=name,
    )(*ins, w_joint, w_up, w_down, *sources)


def ffn_back_kernel(g0_ref, g1_ref, slope_ref, up_ref, down_ref, part0_ref, part1_ref, hidden_ref, sums_ref):
    upstream = pick((g0_ref, g1_ref))
    units = up_ref.shape[1]

    @pl.when(pl.program_id(0) == 0)
    def _():
        sums_ref[...] = jnp.zeros_like(sums_ref)

    total = None
    for start in range(0, units, 512):
        cut = pl.ds(start, 512)
        d_active = dot_nt(upstream, down_ref[cut, :])
        d_hidden = (d_active * slope_ref[:, cut].astype(F32)).astype(BF16)
        hidden_ref[:, cut] = d_hidden
        sums_ref[:, cut] += jnp.sum(d_hidden.astype(F32), axis=0, keepdims=True)
        term = dot_nt(d_hidden, up_ref[:, cut])
        total = term if total is None else total + term
    put((part0_ref, part1_ref), total.astype(BF16))


def ffn_back_call(pair, slope, w_up, w_down, deps=()):
    rows, width = pair[0].shape
    units = w_up.shape[1]
    tile = min(512, rows)
    return pl.pallas_call(
        waiting(ffn_back_kernel, 5, deps),
        grid=(2 * rows // tile,),
        in_specs=halves_of(tile, rows // tile, width) + [rows_of(tile, units), whole(w_up.shape), whole(w_down.shape)]
        + anywhere(len(deps)),
        out_specs=halves_of(tile, rows // tile, width) + [rows_of(tile, units), whole((1, units))],
        out_shape=[shape_of(rows, width)] * 2 + [shape_of(2 * rows, units), shape_of(1, units, dtype=F32)],
        compiler_params=params_of(),
        cost_estimate=cost(8 * rows * width * units, 4 * w_up.size + 8 * rows * (width + units)),
        name="feed_forward_back",
    )(*pair, slope, w_up, w_down, *deps)


def start_sorted(places_ref, parts, targets, sem, block):
    copies = []
    for refs, target in zip(parts, targets):
        index = 0
        for ref in refs:
            for local in range(ref.shape[0] // block):
                place = pl.ds(pl.multiple_of(places_ref[index] * block, block), block)
                copies.append(pltpu.make_async_copy(ref.at[pl.ds(local * block, block)], target.at[place], sem))
                index += 1
    for copy in copies:
        copy.start()
    return copies


def transpose_into(source, target):
    rows, columns = source.shape

    def step(index, _):
        start = pl.multiple_of(index * 256, 256)
        for column in range(0, columns, 256):
            target[column : column + 256, pl.ds(start, 256)] = source[pl.ds(start, 256), column : column + 256].T
        return 0

    lax.fori_loop(0, rows // 256, step, 0)


def stacked(values):
    owner = lax.broadcasted_iota(jnp.int32, values.shape, 1) // HEAD
    zero = jnp.zeros_like(values)
    return jnp.concatenate([jnp.where(owner == a, values, zero) for a in range(STACK)], axis=0)


def spots_of(places_ref, step, tile, block, shape, axis):
    at = lax.broadcasted_iota(jnp.int32, shape, axis) % tile
    count = tile // block
    spot = at + places_ref[step * count] * block
    for s in range(1, count):
        spot = jnp.where(at >= s * block, at - s * block + places_ref[step * count + s] * block, spot)
    return spot


def attend_kernel(block, tile, remote, places_ref, limits_ref, q_ref, wo_ref, *refs):
    key_refs, value_refs = refs[: 1 + remote], refs[1 + remote : 2 + 2 * remote]
    part0_ref, part1_ref, mix_ref, lse_ref, keys, values, scores_ref, sem = refs[2 + 2 * remote :]
    groups = q_ref.shape[1] // GROUP
    half = part0_ref.shape[0]
    rows = STACK * tile
    lanes = [slice(g * GROUP, (g + 1) * GROUP) for g in range(groups)]
    for copy in start_sorted(places_ref, (key_refs, value_refs), (keys, values), sem, block):
        copy.wait()

    def tile_step(step, _):
        mine = pl.ds(pl.multiple_of(step * tile, tile), tile)
        heads = [stacked(q_ref[mine, lane]) for lane in lanes]
        spots = spots_of(places_ref, step, tile, block, (rows, 128), 0)

        def attend_to(count):
            open_end = (count - 1) * KEY_TILE if tile == block else 0
            tops = []
            for g, lane in enumerate(lanes):
                top = None
                for start in range(0, count * KEY_TILE, KEY_TILE):
                    scores = dot_nt(heads[g], keys[start : start + KEY_TILE, lane])
                    for column in range(0, KEY_TILE, 128):
                        piece = scores[:, column : column + 128]
                        if start + column >= open_end:
                            spot = start + column + lax.broadcasted_iota(jnp.int32, piece.shape, 1)
                            piece = jnp.where(spot <= spots, piece, NEGATIVE)
                        scores_ref[g, :, start + column : start + column + 128] = piece
                        top = piece if top is None else jnp.maximum(top, piece)
                tops.append(jnp.broadcast_to(jnp.max(top, axis=1, keepdims=True), (rows, 128)))
            for g, lane in enumerate(lanes):
                mass, total = None, None
                for start in range(0, count * KEY_TILE, KEY_TILE):
                    raised = []
                    for column in range(start, start + KEY_TILE, 128):
                        piece = jnp.exp(scores_ref[g, :, column : column + 128] - tops[g])
                        mass = piece if mass is None else mass + piece
                        raised.append(piece.astype(BF16))
                    term = dot(jnp.concatenate(raised, axis=1), values[start : start + KEY_TILE, lane])
                    total = term if total is None else total + term
                mass = jnp.broadcast_to(jnp.sum(mass, axis=1, keepdims=True), (rows, 128))
                total = total * jnp.concatenate([1.0 / mass] * (GROUP // 128), axis=1)
                owner = lax.broadcasted_iota(jnp.int32, (tile, GROUP), 1) // HEAD
                mixture = total[:tile]
                for a in range(1, STACK):
                    mixture = jnp.where(owner == a, total[a * tile : (a + 1) * tile], mixture)
                mix_ref[mine, lane] = mixture.astype(BF16)
                lse = tops[g] + jnp.log(mass)
                for a in range(STACK):
                    lse_ref[step, g : g + 1, a * tile : (a + 1) * tile] = lse[a * tile : (a + 1) * tile].T[0:1]

        for count in range(1, keys.shape[0] // KEY_TILE + 1):
            pl.when(limits_ref[step, 1] == count)(functools.partial(attend_to, count))
        return 0

    lax.fori_loop(0, q_ref.shape[0] // tile, tile_step, 0)
    part0_ref[...] = dot(mix_ref[:half], wo_ref[...]).astype(BF16)
    part1_ref[...] = dot(mix_ref[half:], wo_ref[...]).astype(BF16)


def attend_call(queries, key_parts, value_parts, places, limits, w_output, block, deps=()):
    rows, local = queries.shape
    width = w_output.shape[1]
    tile = rows // limits.shape[0]
    length = sum(part.shape[0] for part in key_parts)
    groups = local // GROUP
    outs = [(rows // 2, width), (rows // 2, width), (rows, local), (rows // tile, groups, STACK * tile)]
    return pl.pallas_call(
        waiting(functools.partial(attend_kernel, block, tile, len(key_parts) - 1), 4 + 2 * len(key_parts), deps),
        grid_spec=pltpu.PrefetchScalarGridSpec(
            num_scalar_prefetch=2,
            grid=(1,),
            in_specs=[whole((rows, local)), whole(w_output.shape)] + anywhere(2 * len(key_parts) + len(deps)),
            out_specs=[whole(shape) for shape in outs],
            scratch_shapes=[
                pltpu.VMEM((length, local), BF16),
                pltpu.VMEM((length, local), BF16),
                pltpu.VMEM((groups, STACK * tile, length), F32),
                pltpu.SemaphoreType.DMA,
            ],
        ),
        out_shape=[shape_of(*shape) for shape in outs[:3]] + [shape_of(*outs[3], dtype=F32)],
        compiler_params=params_of(),
        cost_estimate=cost(12 * rows * length * local, 2 * length * local * 4),
        name="attend",
    )(places, limits, queries, w_output, *key_parts, *value_parts, *deps)


def attend_back_kernel(
    block, tile, remote, places_ref, limits_ref, q_ref, g0_ref, g1_ref, mix_ref, lse_ref, wo_ref, cos_ref, sin_ref, *refs
):
    key_refs, value_refs = refs[: 1 + remote], refs[1 + remote : 2 + 2 * remote]
    (dq_ref, dk_ref, dv_ref, sums_ref, keys, values, keys_t, d_keys, d_values, d_mixture, inner, total, d_queries, sem) = refs[
        2 + 2 * remote :
    ]
    groups = q_ref.shape[1] // GROUP
    rows = q_ref.shape[0]
    half = g0_ref.shape[0]
    lanes = [slice(g * GROUP, (g + 1) * GROUP) for g in range(groups)]
    copies = start_sorted(places_ref, (key_refs, value_refs), (keys, values), sem, block)
    d_keys[...] = jnp.zeros_like(d_keys)
    d_values[...] = jnp.zeros_like(d_values)
    head_of = lax.broadcasted_iota(jnp.int32, (8, GROUP), 1) // HEAD
    picker = jnp.where(lax.broadcasted_iota(jnp.int32, (8, GROUP), 0) == head_of, 1.0, 0.0).astype(BF16)
    for index, ref in enumerate((g0_ref, g1_ref)):
        cut = pl.ds(index * half, half)
        low = dot_nt(ref[...], wo_ref[...]).astype(BF16)
        d_mixture[cut, :] = low
        product = low.astype(F32) * mix_ref[cut, :].astype(F32)
        high = product.astype(BF16)
        rest = (product - high.astype(F32)).astype(BF16)
        for g, lane in enumerate(lanes):
            inner[g * 8 : (g + 1) * 8, cut] = dot_nt(picker, high[:, lane]) + dot_nt(picker, rest[:, lane])
    for copy in copies:
        copy.wait()
    transpose_into(keys, keys_t)

    def query_step(step, _):
        mine = pl.ds(pl.multiple_of(step * tile, tile), tile)
        spots = spots_of(places_ref, step, tile, block, (1, STACK * tile), 1)
        heads = [stacked(q_ref[mine, lane]) for lane in lanes]
        sides = [stacked(d_mixture[mine, lane]) for lane in lanes]
        sums = [
            jnp.concatenate([inner[g * 8 + a : g * 8 + a + 1, mine] for a in range(STACK)], axis=1) for g in range(groups)
        ]
        lse = [lse_ref[step, g : g + 1, :] for g in range(groups)]
        total[...] = jnp.zeros_like(total)

        def key_step(masked, index, carry):
            start = pl.multiple_of(index * KEY_TILE, KEY_TILE)
            cut = pl.ds(start, KEY_TILE)
            for g, lane in enumerate(lanes):
                scores = dot_nt(keys[cut, lane], heads[g])
                if masked:
                    spot = start + lax.broadcasted_iota(jnp.int32, scores.shape, 0)
                    scores = jnp.where(spot <= spots, scores, NEGATIVE)
                weights = jnp.exp(scores - lse[g])
                d_weights = dot_nt(values[cut, lane], sides[g])
                d_scores = (weights * (d_weights - sums[g])).astype(BF16)
                d_values[cut, lane] += dot(weights.astype(BF16), sides[g])
                d_keys[cut, lane] += dot(d_scores, heads[g])
                total[lane, :] += dot(keys_t[lane, cut], d_scores)
            return carry

        lax.fori_loop(0, limits_ref[step, 0], functools.partial(key_step, False), 0)
        lax.fori_loop(limits_ref[step, 0], limits_ref[step, 1], functools.partial(key_step, True), 0)
        for lane in lanes:
            picked = [total[lane, :][a * HEAD : (a + 1) * HEAD, a * tile : (a + 1) * tile] for a in range(STACK)]
            d_queries[mine, lane] = jnp.concatenate(picked, axis=0).T
        return 0

    lax.fori_loop(0, rows // tile, query_step, 0)
    turned = turn(d_queries[...] * HEAD ** (-0.5), cos_ref[:rows], -sin_ref[:rows]).astype(BF16)
    dq_ref[...] = turned
    sums_ref[...] = jnp.zeros_like(sums_ref)
    sums_ref[0:1, :] = jnp.sum(turned.astype(F32), axis=0, keepdims=True)

    def block_step(index, _):
        place = pl.ds(pl.multiple_of(places_ref[index] * block, block), block)
        mine = pl.ds(pl.multiple_of(index * block, block), block)
        turned = turn(d_keys[place, :], cos_ref[mine, :], -sin_ref[mine, :]).astype(BF16)
        dk_ref[mine, :] = turned
        low = d_values[place, :].astype(BF16)
        dv_ref[mine, :] = low
        sums_ref[1:2, :] += jnp.sum(turned.astype(F32), axis=0, keepdims=True)
        sums_ref[2:3, :] += jnp.sum(low.astype(F32), axis=0, keepdims=True)
        return 0

    lax.fori_loop(0, dk_ref.shape[0] // block, block_step, 0)


def attend_back_call(
    queries, g_pair, mixture, lse, key_parts, value_parts, places, limits, w_output, table, block, deps=()
):
    rows, local = queries.shape
    width = w_output.shape[1]
    tile = rows // limits.shape[0]
    length = sum(part.shape[0] for part in key_parts)
    groups = local // GROUP
    ins = (queries, *g_pair, mixture, lse, w_output, *table)
    return pl.pallas_call(
        waiting(
            functools.partial(attend_back_kernel, block, tile, len(key_parts) - 1), 2 + len(ins) + 2 * len(key_parts), deps
        ),
        grid_spec=pltpu.PrefetchScalarGridSpec(
            num_scalar_prefetch=2,
            grid=(1,),
            in_specs=[whole(x.shape) for x in ins] + anywhere(2 * len(key_parts) + len(deps)),
            out_specs=[whole((rows, local)), whole((length, local)), whole((length, local)), whole((8, local))],
            scratch_shapes=[
                pltpu.VMEM((length, local), BF16),
                pltpu.VMEM((length, local), BF16),
                pltpu.VMEM((local, length), BF16),
                pltpu.VMEM((length, local), F32),
                pltpu.VMEM((length, local), F32),
                pltpu.VMEM((rows, local), BF16),
                pltpu.VMEM((8 * groups, rows), F32),
                pltpu.VMEM((local, STACK * tile), F32),
                pltpu.VMEM((rows, local), F32),
                pltpu.SemaphoreType.DMA,
            ],
        ),
        out_shape=[shape_of(rows, local), shape_of(length, local), shape_of(length, local), shape_of(8, local, dtype=F32)],
        compiler_params=params_of(),
        cost_estimate=cost(24 * rows * length * local, 2 * length * local * 8),
        name="attend_back",
    )(places, limits, *ins, *key_parts, *value_parts, *deps)


def joint_back_kernel(count, *refs):
    w_ref = refs[count]
    total = None
    for index in range(count):
        term = dot_nt(refs[index][...], w_ref[3 - count + index])
        total = term if total is None else total + term
    put(refs[count + 1 :], total.astype(BF16))


def joint_back_call(grads, offset, rows, w_joint, deps=()):
    width, local = w_joint.shape[1:]
    half = rows // 2
    tile = min(512, half)
    first = offset // tile
    return pl.pallas_call(
        waiting(functools.partial(joint_back_kernel, len(grads)), len(grads) + 1, deps),
        grid=(rows // tile,),
        in_specs=[pl.BlockSpec((tile, local), lambda r: (first + r, 0))] * len(grads)
        + [whole(w_joint.shape)]
        + anywhere(len(deps)),
        out_specs=halves_of(tile, half // tile, width),
        out_shape=[shape_of(half, width)] * 2,
        compiler_params=params_of(),
        cost_estimate=cost(2 * rows * width * local * len(grads), 2 * rows * (width + 3 * local) + 2 * w_joint.size),
        name="joint_projection_back",
    )(*grads, w_joint, *deps)


def rear_kernel(q_ref, k_ref, v_ref, w_ref, g0_ref, g1_ref, slope_ref, up_ref, down_ref, first0_ref, first1_ref, part0_ref, part1_ref):
    total = dot_nt(q_ref[...], w_ref[0]) + dot_nt(k_ref[...], w_ref[1]) + dot_nt(v_ref[...], w_ref[2])
    put((first0_ref, first1_ref), total.astype(BF16))
    upstream = pick((g0_ref, g1_ref))
    total = None
    for start in range(0, up_ref.shape[1], 512):
        cut = pl.ds(start, 512)
        d_active = dot_nt(upstream, down_ref[cut, :])
        d_hidden = (d_active * slope_ref[:, cut].astype(F32)).astype(BF16)
        term = dot_nt(d_hidden, up_ref[:, cut])
        total = term if total is None else total + term
    put((part0_ref, part1_ref), total.astype(BF16))


def rear_call(grads, w_joint, pair, slope, w_up, w_down, moves, moved, name, number):
    rows, width = pair[0].shape
    local = w_joint.shape[2]
    units = w_up.shape[1]
    tile = min(512, rows)
    halves = halves_of(tile, rows // tile, width)
    outs = pl.pallas_call(
        carrying(rear_kernel, 9, 4, moves),
        grid=(2 * rows // tile,),
        in_specs=[rows_of(tile, local)] * 3
        + [whole(w_joint.shape)]
        + halves
        + [rows_of(tile, units), whole(w_up.shape), whole(w_down.shape)]
        + anywhere(len(moves)),
        out_specs=halves + halves + anywhere(len(moves)),
        out_shape=[shape_of(rows, width)] * 4 + [shape_of(*x.shape) for x in moved],
        scratch_shapes=carrier_semaphores(len(moves)),
        compiler_params=params_of(collective_id=number, has_side_effects=True),
        cost_estimate=cost(4 * rows * width * (3 * local + 2 * units), 4 * w_up.size + 16 * rows * width),
        name=name,
    )(*grads, w_joint, *pair, slope, w_up, w_down, *moved)
    return outs[:2], outs[2:4], outs[4:]


def norm_back_kernel(firsts, h_ref, g_ref, gains_ref, *refs):
    first_refs, second_refs, (out_ref, sums_ref) = refs[:firsts], refs[firsts:-2], refs[-2:]

    @pl.when(pl.program_id(0) == 0)
    def _():
        sums_ref[...] = jnp.zeros_like(sums_ref)

    scaled, inverse = normalize(h_ref[...].astype(F32))
    upstream = g_ref[...].astype(F32)
    d_first = sum(ref[...].astype(F32) for ref in first_refs)
    d_second = sum(ref[...].astype(F32) for ref in second_refs)
    for row, term in enumerate((d_first * scaled, d_first, d_second * scaled, d_second, upstream)):
        sums_ref[row : row + 1, :] += jnp.sum(term, axis=0, keepdims=True)
    d_scaled = d_first * gains_ref[0:1] + d_second * gains_ref[1:2]
    middle = jnp.mean(d_scaled, axis=-1, keepdims=True)
    along = jnp.mean(d_scaled * scaled, axis=-1, keepdims=True)
    out_ref[...] = (upstream + inverse * (d_scaled - middle - scaled * along)).astype(BF16)


def norm_back_call(h, g, firsts, seconds, gains, deps=()):
    rows, width = h.shape
    tile = min(128, rows)
    one = rows_of(tile, width)
    return pl.pallas_call(
        waiting(functools.partial(norm_back_kernel, len(firsts)), 3 + len(firsts) + len(seconds), deps),
        grid=(rows // tile,),
        in_specs=[one, one, whole(gains.shape)] + [one] * (len(firsts) + len(seconds)) + anywhere(len(deps)),
        out_specs=[one, whole((8, width))],
        out_shape=[shape_of(rows, width), shape_of(8, width, dtype=F32)],
        compiler_params=params_of(),
        cost_estimate=cost(20 * rows * width, 2 * rows * width * 8),
        name="norm_back",
    )(h, g, gains, *firsts, *seconds, *deps)


def merge_kernel(h_ref, a0_ref, a1_ref, f0_ref, f1_ref, shifts_ref, out_ref, sums_ref):
    @pl.when(pl.program_id(0) == 0)
    def _():
        sums_ref[...] = jnp.zeros_like(sums_ref)

    state = h_ref[...].astype(F32)
    attention = a0_ref[...].astype(F32) + a1_ref[...].astype(F32) + shifts_ref[0:1]
    feedforward = f0_ref[...].astype(F32) + f1_ref[...].astype(F32) + shifts_ref[1:2]
    out_ref[...] = (state + attention + feedforward).astype(BF16)
    for row, term in enumerate((state, attention, feedforward)):
        sums_ref[row : row + 1, :] += jnp.sum(term * term, axis=0, keepdims=True)


def merge_call(h, attn_pair, ffn_pair, shifts, deps=()):
    rows, width = h.shape
    tile = min(128, rows)
    one = rows_of(tile, width)
    return pl.pallas_call(
        waiting(merge_kernel, 6, deps),
        grid=(rows // tile,),
        in_specs=[one] * 5 + [whole(shifts.shape)] + anywhere(len(deps)),
        out_specs=[one, whole((8, width))],
        out_shape=[shape_of(rows, width), shape_of(8, width, dtype=F32)],
        compiler_params=params_of(),
        cost_estimate=cost(10 * rows * width, 2 * rows * width * 6),
        name="merge",
    )(h, *attn_pair, *ffn_pair, shifts, *deps)


def tn(a, b):
    return lax.dot_general(a, b, (((0,), (0,)), ((), ())), preferred_element_type=F32)


def slope_kernel(count, terms, owners_ref, *refs):
    lefts = [jnp.concatenate([ref[...] for ref in refs[t * count : (t + 1) * count]], axis=1) for t in range(terms)]
    rights = refs[terms * count : terms * (count + 1)]
    outs = refs[terms * (count + 1) :]
    share = lefts[0].shape[1] // count
    total = sum(tn(left, right[...]) for left, right in zip(lefts, rights)).astype(BF16)
    first = pl.program_id(0) < pl.num_programs(0) // 2
    for ref, here in zip(outs, (first, jnp.logical_not(first))):

        @pl.when(here)
        def _():
            for index in range(count):
                ref[index] = total[index * share : (index + 1) * share]


def slope_call(owners, terms, name, cut=(0, 1), deps=()):
    total = owners.shape[0]
    share = terms[0][0].shape[1] // total
    columns = terms[0][1].shape[1] // cut[1]
    count = 4
    if share % 128 or total % (2 * count):
        pieces = 0.0
        row = 0
        for left, right, _ in terms:
            left_ordered = jnp.take(left.reshape(left.shape[0], total, share), owners, axis=1).reshape(left.shape)
            part = right[row : row + left.shape[0], cut[0] * columns : (cut[0] + 1) * columns]
            row += left.shape[0]
            pieces = pieces + tn(left_ordered, part)
        pieces = pieces.astype(BF16).reshape(total, share, columns)
        return pieces[: total // 2], pieces[total // 2 :]
    steps = total // count
    ins, specs = [], []
    for left, _, _ in terms:
        for index in range(count):
            ins.append(left)
            specs.append(
                pl.BlockSpec((left.shape[0], share), functools.partial(lambda i, r, o: (0, o[count * r + i]), index))
            )
    for left, right, row in terms:
        ins.append(right)
        specs.append(
            pl.BlockSpec((left.shape[0], columns), functools.partial(lambda i, r, o: (i, cut[0]), row))
        )
    return pl.pallas_call(
        waiting(functools.partial(slope_kernel, count, len(terms)), 1 + len(ins), deps),
        grid_spec=pltpu.PrefetchScalarGridSpec(
            num_scalar_prefetch=1,
            grid=(steps,),
            in_specs=specs + anywhere(len(deps)),
            out_specs=halves_of(count, steps // 2, share, columns),
        ),
        out_shape=[shape_of(total // 2, share, columns)] * 2,
        compiler_params=params_of(),
        cost_estimate=cost(
            sum(2 * a.size * columns for a, _, _ in terms),
            sum(2 * (a.size + a.shape[0] * columns) for a, _, _ in terms) + 2 * total * share * columns,
        ),
        name=name,
    )(owners, *ins, *deps)


def hand_back_kernel(seqs, *refs):
    refs = list(refs)
    take = lambda count: [refs.pop(0) for _ in range(count)]
    gains_ref, shifts_ref = take(2)
    sources = take(12)
    a1_in, f1_in = take(2)
    g0_out, g1_out, home_ref, moments_ref = take(4)
    targets = take(12)
    dk, dv, w, dq, g1, g0, down, up, slope, a0, f0, h = targets
    far1, far1_got, sums, arrived, near0, near1, near1_got = take(7)
    second0, second1, second1_got, d_own, got, fresh, fresh_other, a_got, f_got, result = take(10)
    load, side_s, side_r, chip_s, chip_r, core_s, core_r, twin_s, twin_r, new_s, new_r, home_s, home_r, swap_s, swap_r = refs
    me, core, section = lax.axis_index("ctx"), lax.axis_index("tp"), lax.axis_index("section")
    rows, width = far1.shape
    block = rows // seqs
    chips = 2
    seq = me // chips
    chip_rows = 2 * rows
    other_core, other_chip, twin = {"tp": 1 - core}, {"ctx": exchanged(me, 1)}, {"section": 1 - section}
    planes = [{"ctx": exchanged(me, c * chips)} for c in range(1, seqs)]
    traffic = Traffic()

    def at(c):
        return pl.ds(c * block, block)

    def span(c):
        return slice(c * block, (c + 1) * block)

    loads = [pltpu.make_async_copy(a, b, load.at[n]) for n, (a, b) in enumerate(zip(sources, targets))]
    for copy in loads:
        copy.start()
    greet([other_core, other_chip, twin] + planes)
    out_swaps = [
        traffic.send(a1_in, a_got, side_s.at[0], side_r.at[0], other_core),
        traffic.send(f1_in, f_got, side_s.at[1], side_r.at[1], other_core),
    ]
    for n in (0, 1, 2):
        loads[n].wait()

    def from_far(start):
        cut = slice(start, start + rows)
        return dot_nt(dk[cut], w[1]) + dot_nt(dv[cut], w[2])

    far1[...] = from_far(chip_rows + rows).astype(BF16)
    swap = traffic.send(far1, far1_got, side_s.at[2], side_r.at[2], other_core)
    mine = from_far(chip_rows)
    swap.wait_recv()
    sums[...] = (mine + far1_got[...].astype(F32)).astype(BF16)
    arrivals = [
        traffic.send(sums.at[at(c)], arrived.at[at(c)], chip_s.at[c], chip_r.at[c], other_chip) for c in range(seqs)
    ]
    for n in range(3, 12):
        loads[n].wait()

    def from_near(cut):
        return sum(dot_nt(grad[cut], w[t]) for t, grad in enumerate((dq, dk, dv)))

    near1[...] = from_near(slice(rows, chip_rows)).astype(BF16)
    near_swap = traffic.send(near1, near1_got, side_s.at[3], side_r.at[3], other_core)
    near0[...] = from_near(slice(0, rows)).astype(BF16)
    for copy in out_swaps:
        copy.wait_recv()
    moments_ref[...] = jnp.zeros_like(moments_ref)
    home = []
    for c in range(seqs):
        cut = span(c)
        state = h[cut].astype(F32)
        attention = a0[cut].astype(F32) + a_got[cut].astype(F32) + shifts_ref[0:1]
        feedforward = f0[cut].astype(F32) + f_got[cut].astype(F32) + shifts_ref[1:2]
        result[cut] = (state + attention + feedforward).astype(BF16)
        for row, term in enumerate((state, attention, feedforward)):
            moments_ref[row : row + 1, :] += jnp.sum(term * term, axis=0, keepdims=True)
        place = home_ref.at[seq, core]
        if c == 0:
            stay = pltpu.make_async_copy(result.at[at(0)], place, load.at[12])
            stay.start()
        else:
            home.append(traffic.send(result.at[at(c)], place, home_s.at[c], home_r.at[c], planes[c - 1]))
    near_swap.wait_recv()
    handed = []
    for c in range(seqs):
        cut = span(c)
        upstream = jnp.concatenate([g0[cut], g1[cut]], 0)
        slopes = [slice(part * rows + c * block, part * rows + (c + 1) * block) for part in range(2)]
        total = None
        for start in range(0, up.shape[1], 512):
            unit = slice(start, start + 512)
            d_active = dot_nt(upstream, down[unit, :])
            bend = jnp.concatenate([slope[rows_cut, unit] for rows_cut in slopes], 0).astype(F32)
            term = dot_nt((d_active * bend).astype(BF16), up[:, unit])
            total = term if total is None else total + term
        second1[cut] = total[block:].astype(BF16)
        swap = traffic.send(second1.at[at(c)], second1_got.at[at(c)], core_s.at[c], core_r.at[c], other_core)
        arrivals[c].wait_recv()
        scaled, inverse = normalize(h[cut].astype(F32))
        d_first = near0[cut].astype(F32) + near1_got[cut].astype(F32) + arrived[cut].astype(F32)
        swap.wait_recv()
        d_second = total[:block] + second1_got[cut].astype(F32)
        d_scaled = d_first * gains_ref[0:1] + d_second * gains_ref[1:2]
        middle = jnp.mean(d_scaled, axis=-1, keepdims=True)
        along = jnp.mean(d_scaled * scaled, axis=-1, keepdims=True)
        d_own[cut] = (g0[cut].astype(F32) + inverse * (d_scaled - middle - scaled * along)).astype(BF16)
        handed.append(traffic.send(d_own.at[at(c)], got.at[at(c)], twin_s.at[c], twin_r.at[c], twin))
    stay.wait()
    swaps = []
    for s in range(seqs):
        if s:
            home[s - 1].wait_recv()
        place = home_ref.at[exchanged(seq, s), core]
        swaps.append(traffic.send(place, place, swap_s.at[s], swap_r.at[s], other_core))
    news = []
    for c in range(seqs):
        handed[c].wait_recv()
        cut = span(c)
        fresh[cut] = jnp.where(section == 1, g0[cut], got[cut])
        news.append(traffic.send(fresh.at[at(c)], fresh_other.at[at(c)], new_s.at[c], new_r.at[c], other_core))
    first = pltpu.make_async_copy(fresh, g0_out, load.at[0])
    first.start()
    for copy in news:
        copy.wait_recv()
    last = pltpu.make_async_copy(fresh_other, g1_out, load.at[1])
    last.start()
    for copy in swaps:
        copy.wait_recv()
    traffic.finish()
    first.wait()
    last.wait()


def hand_back_call(grads, w_joint, h, g_pair, slope, w_up, w_down, gains, shifts, attn, ffn, name, number):
    d_queries, d_keys, d_values = grads
    rows, width = h.shape
    seqs = SEQS
    wide = (rows, width)
    sources = (d_keys, d_values, w_joint, d_queries, g_pair[1], g_pair[0], w_down, w_up, slope, attn[0], ffn[0], h)
    home = (seqs, 2, rows // seqs, width)
    scratch = [x.shape for x in sources] + [wide] * 17
    quads = carrier_semaphores(seqs)
    return pl.pallas_call(
        functools.partial(hand_back_kernel, seqs),
        grid=(1,),
        in_specs=[whole(gains.shape), whole(shifts.shape)] + anywhere(14),
        out_specs=anywhere(3) + [whole((8, width))],
        out_shape=[shape_of(*wide), shape_of(*wide), shape_of(*home), shape_of(8, width, dtype=F32)],
        scratch_shapes=[pltpu.VMEM(x, BF16) for x in scratch] + [pltpu.SemaphoreType.DMA((14,))] + quads * 7,
        compiler_params=params_of(collective_id=number, has_side_effects=True),
        name=name,
    )(gains, shifts, *sources, attn[1], ffn[1])


class Sums:
    def __init__(self, masks, slots, send, receive, remote, totals):
        self.masks, self.slots, self.send, self.receive = masks, slots, send, receive
        self.remote, self.totals = remote, totals
        self.steps = [0] * len(masks)
        self.running = [None] * len(masks)
        self.kept = [None] * len(masks)
        self.first = [sum(len(m) for m in masks[:c]) for c in range(len(masks))]

    def launch(self, c, kept, sent):
        step = self.steps[c]
        number = self.first[c] + step
        self.kept[c] = kept
        self.running[c] = self.remote(
            sent, self.slots[c][step], self.send.at[number], self.receive.at[number], self.masks[c][step]
        )

    def halve(self, c, pieces, count):
        self.launch(c, pieces, pieces.at[pl.ds(count // 2, count // 2)])

    def go_on(self, c):
        self.running[c].wait_recv()
        slot = self.slots[c][self.steps[c]]
        count = slot.shape[0]
        total = self.kept[c][:count].astype(F32) + slot[...].astype(F32)
        self.steps[c] += 1
        if self.steps[c] == len(self.masks[c]):
            self.totals[c](total[0])
            return
        self.kept[c][:count] = total.astype(BF16)
        self.halve(c, self.kept[c], count)


def tail_kernel(masks, *refs):
    late, early = masks
    (dq_in, dk_in, dv_in, w_in, near_in, far_in, h_in, g_in, second0_in, second1_in, gains_ref, words_in, o0_in, o1_in,
     d0_in, d1_in, ua0_in, ua1_in, ub0_in, ub1_in) = refs[:20]
    o_out, joint_out, down_out, up_out, home_ref, words_out = refs[20:26]
    (dq, dk, dv, w, near, far, h, g, second0, second1, o0, d0, d1, ua0, ua1, ub0, ub1, jq, jk, jv,
     far1, far1_got, sums, arrived, near0, near1, near1_got, d_own, words, other_words) = refs[26:56]
    slots = refs[56:74]
    load, chain_send, chain_receive, side_send, side_receive, word_send, word_receive = refs[74:]
    me, core = lax.axis_index("ctx"), lax.axis_index("tp")
    size = words.shape[0]
    rows, width = h.shape
    seqs, _, block, _ = home_ref.shape
    chips = size // seqs
    seq = me // chips
    chip_rows = 2 * rows
    other_core = {"tp": 1 - core}
    started = []

    def at_ctx(mask):
        return {"ctx": exchanged(me, mask)}

    def send(source, target, first, second, device):
        copy = pltpu.make_async_remote_copy(
            source, target, first, second, device_id=device, device_id_type=pl.DeviceIdType.MESH
        )
        copy.start()
        started.append(copy)
        return copy

    def to_core(source, target, number):
        return send(source, target, side_send.at[number], side_receive.at[number], other_core)

    loads = {}
    order = (
        ("d0", d0_in, d0), ("d1", d1_in, d1), ("ua0", ua0_in, ua0), ("ua1", ua1_in, ua1), ("ub0", ub0_in, ub0),
        ("ub1", ub1_in, ub1), ("dk", dk_in, dk), ("dv", dv_in, dv), ("w", w_in, w), ("dq", dq_in, dq), ("near", near_in, near),
        ("far", far_in, far), ("o0", o0_in, o0), ("h", h_in, h), ("g", g_in, g), ("second0", second0_in, second0),
    )
    for number, (name, source, target) in enumerate(order):
        loads[name] = pltpu.make_async_copy(source, target, load.at[number])
        loads[name].start()

    barrier = pltpu.get_barrier_semaphore()
    for mask in range(1, size):
        pl.semaphore_signal(barrier, inc=1, device_id=at_ctx(mask), device_id_type=pl.DeviceIdType.MESH)
    pl.semaphore_signal(barrier, inc=1, device_id=other_core, device_id_type=pl.DeviceIdType.MESH)
    pl.semaphore_wait(barrier, size)

    units = up_out.shape[1]

    def put_output(total):
        o_out[...] = total.T

    def put_down(total):
        down_out[...] = total.T

    def put_joint(t):
        def write(total):
            joint_out[t] = total

        return write

    def put_up(start):
        def write(total):
            up_out[:, start : start + units // 2] = total

        return write

    chains = [late, late, late, late, early[1:], early[1:], late[1:]]
    parts, used = [], 0
    for chain in chains:
        parts.append(slots[used : used + len(chain)])
        used += len(chain)
    totals = [put_output, put_joint(0), put_joint(1), put_joint(2), put_up(0), put_up(units // 2), put_down]
    run = Sums(
        chains, parts, chain_send, chain_receive,
        lambda source, target, first, second, mask: send(source, target, first, second, at_ctx(mask)), totals,
    )
    run.launch(0, o0, o1_in)
    second_swap = to_core(second1_in, second1, 0)

    def ready(c, kept, other, names):
        for name in names:
            loads[name].wait()
        for index in range(kept.shape[0]):
            kept[index] = (kept[index].astype(F32) + other[index].astype(F32)).astype(BF16)
        run.halve(c, kept, kept.shape[0])

    ready(6, d0, d1, ("d0", "d1"))
    ready(4, ua0, ua1, ("ua0", "ua1"))
    ready(5, ub0, ub1, ("ub0", "ub1"))
    for name in ("dk", "dv", "w"):
        loads[name].wait()

    def from_far(start):
        cut = slice(start, start + rows)
        return dot_nt(dk[cut], w[1]) + dot_nt(dv[cut], w[2])

    far1[...] = from_far(chip_rows + rows).astype(BF16)
    swap = to_core(far1, far1_got, 1)
    mine = from_far(chip_rows)
    swap.wait_recv()
    sums[...] = (mine + far1_got[...].astype(F32)).astype(BF16)
    arrival = send(sums, arrived, side_send.at[2], side_receive.at[2], at_ctx(1))
    loads["dq"].wait()
    loads["near"].wait()
    loads["far"].wait()
    loads["o0"].wait()

    def from_near(cut):
        return sum(dot_nt(grad[cut], w[t]) for t, grad in enumerate((dq, dk, dv)))

    near1[...] = from_near(slice(rows, chip_rows)).astype(BF16)
    near_swap = to_core(near1, near1_got, 3)
    near0[...] = from_near(slice(0, rows)).astype(BF16)
    run.go_on(0)
    share = width // size
    count = 4
    owners = mask_order(late)
    for t, (target, grad) in enumerate(((jq, dq), (jk, dk), (jv, dv))):
        for start in range(0, size, count):
            spots = [pl.ds(pl.multiple_of(exchanged(me, m) * share, share), share) for m in owners[start : start + count]]
            total = tn(jnp.concatenate([near[:, spot] for spot in spots], axis=1), grad[:chip_rows])
            if t:
                total = total + tn(jnp.concatenate([far[:, spot] for spot in spots], axis=1), grad[chip_rows:])
            low = total.astype(BF16)
            for index in range(count):
                target[start + index] = low[index * share : (index + 1) * share]
        run.halve(1 + t, target, size)
        if t == 1:
            run.go_on(6)
    for name in ("h", "g", "second0"):
        loads[name].wait()
    for copy in (second_swap, near_swap, arrival):
        copy.wait_recv()
    gradients = [jnp.zeros((1, width), F32) for _ in range(5)]
    for s in range(seqs):
        cut = slice(s * block, (s + 1) * block)
        scaled, inverse = normalize(h[cut].astype(F32))
        upstream = g[cut].astype(F32)
        d_first = near0[cut].astype(F32) + near1_got[cut].astype(F32) + arrived[cut].astype(F32)
        d_second = second0[cut].astype(F32) + second1[cut].astype(F32)
        for row, term in enumerate((d_first * scaled, d_first, d_second * scaled, d_second, upstream)):
            gradients[row] = gradients[row] + jnp.sum(term, axis=0, keepdims=True)
        d_scaled = d_first * gains_ref[0:1] + d_second * gains_ref[1:2]
        middle = jnp.mean(d_scaled, axis=-1, keepdims=True)
        along = jnp.mean(d_scaled * scaled, axis=-1, keepdims=True)
        d_own[cut] = (upstream + inverse * (d_scaled - middle - scaled * along)).astype(BF16)
    home = []
    for s in range(seqs):
        source = d_own.at[pl.ds(s * block, block)]
        if s == 0:
            stay = pltpu.make_async_copy(source, home_ref.at[seq, core], load.at[len(order)])
            stay.start()
        else:
            number = 4 + s
            home.append(
                send(source, home_ref.at[seq, core], side_send.at[number], side_receive.at[number], at_ctx(s * chips))
            )
    lines = width // 128
    words_out[...] = words_in[...]
    for row in range(5):
        for line in range(lines):
            words_out[row * lines + line : row * lines + line + 1] = gradients[row][:, line * 128 : (line + 1) * 128]
    words[pl.ds(me, 1)] = words_out[...][None]
    word_copies = [
        send(words.at[me], words.at[me], word_send.at[mask], word_receive.at[mask], at_ctx(mask))
        for mask in range(1, size)
    ]
    for c in (0, 4, 1, 2, 5, 3, 1, 6, 4, 2, 0, 5, 3):
        run.go_on(c)
    stay.wait()
    swaps = []
    for s in range(seqs):
        if s:
            home[s - 1].wait_recv()
        place = home_ref.at[exchanged(seq, s), core]
        swaps.append(to_core(place, place, 4 + seqs + s))
    for copy in word_copies:
        copy.wait_recv()
    total = words[0]
    for index in range(1, size):
        total = total + words[index]
    core_words = other_words.shape[0]
    for copy in word_copies:
        copy.wait_send()
    words_out[...] = total
    swap = to_core(words_out.at[pl.ds(0, core_words)], other_words, 4)
    swap.wait_recv()
    swap.wait_send()
    words_out[pl.ds(0, core_words)] = total[:core_words] + other_words[...]
    for c in (1, 2, 3):
        run.go_on(c)
    for copy in swaps:
        copy.wait_recv()
    for copy in started:
        if copy is not swap and not any(copy is x for x in word_copies):
            copy.wait_send()


def tail_call(grads, w_joint, normals, h, g, seconds, gains, words, core_words, output, down, ups, masks, seqs, number):
    late, early = masks
    rows, width = h.shape
    chip_rows, local = grads[0].shape
    size = 1 << len(late)
    units = down[0].shape[2]
    share = width // size
    ins = (*grads, w_joint, *normals, h, g, *seconds, gains, words, *output, *down, *ups[0], *ups[1])
    specs = anywhere(len(ins))
    specs[10], specs[11] = whole(gains.shape), whole(words.shape)
    out = [
        shape_of(local, share, dtype=F32),
        shape_of(3, share, local, dtype=F32),
        shape_of(units, share, dtype=F32),
        shape_of(share, units, dtype=F32),
        shape_of(seqs, 2, rows // seqs, width),
        shape_of(*words.shape, dtype=F32),
    ]
    half = size // 2
    wide = (rows, width)
    scratch = [x.shape for x in (*grads, w_joint, *normals)] + [wide] * 4 + [output[0].shape]
    scratch += [down[0].shape] * 2 + [ups[0][0].shape] * 4 + [(size, share, local)] * 3 + [wide] * 8
    scratch = [pltpu.VMEM(shape, BF16) for shape in scratch]
    scratch += [pltpu.VMEM((size, *words.shape), F32), pltpu.VMEM((core_words, 128), F32)]
    for chain, columns, pieces in (
        (late, local, half), (late, local, half), (late, local, half), (late, local, half),
        (early[1:], units // 2, half // 2), (early[1:], units // 2, half // 2), (late[1:], units, half // 2),
    ):
        scratch += [pltpu.VMEM((pieces >> step, share, columns), BF16) for step in range(len(chain))]
    scratch += [pltpu.SemaphoreType.DMA((17,))] + carrier_semaphores(18)
    scratch += carrier_semaphores(4 + 2 * seqs) + carrier_semaphores(size)
    return pl.pallas_call(
        functools.partial(tail_kernel, masks),
        grid=(1,),
        in_specs=specs,
        out_specs=[pl.BlockSpec(memory_space=pl.ANY) if n == 4 else whole(x.shape) for n, x in enumerate(out)],
        out_shape=out,
        scratch_shapes=scratch,
        compiler_params=params_of(collective_id=number, has_side_effects=True),
        name="tail",
    )(*ins)


def finish_kernel(chains, events, seqs, chips, core_words, *refs):
    count = len(chains)
    ins, refs = refs[: 2 * count], refs[2 * count :]
    d_own_ref, words_ref = refs[:2]
    totals, home_ref, words_out = refs[2 : 2 + count], refs[2 + count], refs[3 + count]
    refs = list(refs[4 + count :])
    current = [refs.pop(0) for _ in chains]
    slots = [[refs.pop(0) for _ in chain[0]] for chain in chains]
    words, other_words, chain_send, chain_receive, home_send, home_receive, word_send, word_receive, local = refs
    me, core = lax.axis_index("ctx"), lax.axis_index("tp")
    size = words.shape[0]
    seq = me // chips
    block = home_ref.shape[2]

    def at_ctx(mask):
        return {"ctx": exchanged(me, mask)}

    other_core = {"tp": 1 - core}

    def remote(source, target, send, receive, device):
        return pltpu.make_async_remote_copy(
            source, target, send, receive, device_id=device, device_id_type=pl.DeviceIdType.MESH
        )

    barrier = pltpu.get_barrier_semaphore()
    for mask in range(1, size):
        pl.semaphore_signal(barrier, inc=1, device_id=at_ctx(mask), device_id_type=pl.DeviceIdType.MESH)
    pl.semaphore_signal(barrier, inc=1, device_id=other_core, device_id_type=pl.DeviceIdType.MESH)
    pl.semaphore_wait(barrier, size)

    started = []

    def begin(copy):
        copy.start()
        started.append(copy)
        return copy

    word_copies = [
        begin(remote(words_ref, words.at[me], word_send.at[mask], word_receive.at[mask], at_ctx(mask)))
        for mask in range(1, size)
    ]
    steps = [0] * count
    running = [None] * count
    number = [sum(len(chain[0]) for chain in chains[:c]) for c in range(count)]

    def launch(c, source):
        masks = chains[c][0]
        step = steps[c]
        n = number[c] + step
        running[c] = begin(
            remote(source, slots[c][step], chain_send.at[n], chain_receive.at[n], at_ctx(masks[step]))
        )

    def split(c):
        pieces = current[c].shape[0] >> (steps[c] + (0 if chains[c][1] else -1))
        launch(c, current[c].at[pl.ds(pieces // 2, pieces // 2)])

    home = []

    def send_home():
        copy = pltpu.make_async_copy(d_own_ref.at[pl.ds(0, block)], home_ref.at[seq, core], local)
        copy.start()
        for s in range(1, seqs):
            home.append(
                begin(
                    remote(
                        d_own_ref.at[pl.ds(s * block, block)], home_ref.at[seq, core],
                        home_send.at[s], home_receive.at[s], at_ctx(s * chips),
                    )
                )
            )
        copy.wait()

    def go_on(c):
        masks, ready = chains[c][:2]
        running[c].wait_recv()
        slot = slots[c][steps[c]]
        pieces = slot.shape[0]
        kept = ins[2 * c] if steps[c] == 0 and not ready else current[c]
        total = kept[:pieces].astype(F32) + slot[...].astype(F32)
        steps[c] += 1
        if steps[c] == len(masks):
            totals[c][...] = total[0]
            return
        current[c][:pieces] = total.astype(BF16)
        split(c)

    for c, (masks, ready, _) in enumerate(chains):
        if not ready:
            launch(c, ins[2 * c + 1])
    for c, (masks, ready, _) in enumerate(chains):
        if ready:
            current[c][...] = (ins[2 * c][...].astype(F32) + ins[2 * c + 1][...].astype(F32)).astype(BF16)
            split(c)
    send_home()
    words[pl.ds(me, 1)] = words_ref[...][None]
    for c in events:
        go_on(c)
    for copy in home:
        copy.wait_recv()
    swaps = []
    for s in range(seqs):
        place = home_ref.at[exchanged(seq, s), core]
        swaps.append(begin(remote(place, place, home_send.at[seqs + s], home_receive.at[seqs + s], other_core)))
    for copy in word_copies:
        copy.wait_recv()
    total = words[0]
    for index in range(1, size):
        total = total + words[index]
    words_out[...] = total
    swap = remote(words_out.at[pl.ds(0, core_words)], other_words, word_send.at[0], word_receive.at[0], other_core)
    swap.start()
    swap.wait()
    words_out[pl.ds(0, core_words)] = total[:core_words] + other_words[...]
    for copy in swaps:
        copy.wait_recv()
    for copy in started:
        copy.wait_send()


def finish_call(chains, events, d_own, words, core_words, seqs, chips, number):
    size = chips * seqs
    rows, width = d_own.shape
    block = rows // seqs
    ins, specs, out, scratch, slots = [], [], [], [], []
    for masks, ready, (kept, other) in chains:
        pieces, share, columns = kept.shape
        ins += [kept, other]
        specs += [whole(kept.shape), whole(other.shape) if ready else anywhere(1)[0]]
        out.append(shape_of(share, columns, dtype=F32))
        scratch.append(pltpu.VMEM((pieces, share, columns), BF16))
        slots += [
            pltpu.VMEM((pieces >> (step + 1 if ready else step), share, columns), BF16) for step in range(len(masks))
        ]
    copies = len(slots)
    scratch += slots + [pltpu.VMEM((size, *words.shape), F32), pltpu.VMEM((core_words, 128), F32)]
    scratch += carrier_semaphores(copies) + carrier_semaphores(2 * seqs) + carrier_semaphores(size)
    scratch += [pltpu.SemaphoreType.DMA]
    home = shape_of(seqs, 2, block, width)
    out_specs = [whole(x.shape) for x in out] + anywhere(1) + [whole(words.shape)]
    return pl.pallas_call(
        functools.partial(finish_kernel, [(m, r, None) for m, r, _ in chains], events, seqs, chips, core_words),
        grid=(1,),
        in_specs=specs + anywhere(1) + [whole(words.shape)],
        out_specs=out_specs,
        out_shape=out + [home, shape_of(*words.shape, dtype=F32)],
        scratch_shapes=scratch,
        compiler_params=params_of(collective_id=number, has_side_effects=True),
        name="finish",
    )(*ins, d_own, words)


def swap_core(shard):
    return lax.ppermute(shard, "tp", [(0, 1), (1, 0)])


def swap_ctx(shard, mask):
    return lax.ppermute(shard, "ctx", [(c, c ^ mask) for c in range(lax.axis_size("ctx"))])


def next_section(shard, by):
    size = lax.axis_size("section")
    return lax.ppermute(shard, "section", [(s, s + by) for s in range(size) if 0 <= s + by < size])


def mask_order(masks):
    order = [0]
    for mask in reversed(masks):
        order = order + [value ^ mask for value in order]
    return order


def on_device(
    tokens,
    cotangent,
    block_order,
    first_gain,
    first_bias,
    second_gain,
    second_bias,
    joint_weight,
    joint_bias,
    output_weight,
    output_bias,
    up_weight,
    up_bias,
    down_weight,
    down_bias,
):
    section = lax.axis_index("section")
    sections = lax.axis_size("section")
    ctx = lax.axis_index("ctx")
    ctx_size = lax.axis_size("ctx")
    core = lax.axis_index("tp")
    seqs, local_len, width = tokens.shape
    block = local_len // 2
    chips = ctx_size // seqs
    seq, member = ctx // chips, ctx % chips
    rows = seqs * block
    chip_rows = 2 * rows
    length = chips * chip_rows
    seq_masks = [chips << b for b in range((seqs - 1).bit_length())]
    member_masks = [1 << b for b in range((chips - 1).bit_length())]

    k, u, a = jnp.meshgrid(jnp.arange(chips), jnp.arange(2), jnp.arange(seqs), indexing="ij")
    stored = (2 * ((seq ^ a) * chips + (member ^ k)) + (core ^ u)).reshape(-1)
    places = block_order[stored]
    spots = (places[:, None] * block + jnp.arange(block, dtype=jnp.int32)).reshape(-1)
    exponent = jnp.arange(ROT // 2, dtype=F32) * (2.0 / ROT)
    inverse = jnp.power(jnp.float32(ROTARY_BASE), -exponent)
    turns = spots.astype(F32)[:, None] * inverse[None, :]
    cosine, sine = jnp.cos(turns), jnp.sin(turns)
    rest = jnp.zeros((length, HEAD - ROT), F32)
    table = (
        jnp.tile(jnp.concatenate([cosine, cosine, rest + 1.0], 1), (1, 128 // HEAD)),
        jnp.tile(jnp.concatenate([sine, sine, rest], 1), (1, 128 // HEAD)),
    )

    tile = max(block, 128)
    tile_places = places[: chip_rows // block].reshape(-1, tile // block)
    lowest, highest = jnp.min(tile_places, 1), jnp.max(tile_places, 1)
    limits = jnp.stack([(lowest * block + 1) // KEY_TILE, (highest * block + block - 1) // KEY_TILE + 1], 1)

    gain_one, shift_one, gain_two, shift_two = first_gain, first_bias, second_gain, second_bias
    w_joint, b_joint = joint_weight[0], joint_bias[0]
    w_output, b_output = output_weight[0], output_bias
    w_up, b_up = up_weight[0], up_bias
    w_down, b_down = down_weight[0], down_bias
    gains = jnp.concatenate([gain_one, gain_two], 0)
    norms = jnp.concatenate([gain_one, shift_one, gain_two, shift_two], 0)
    shifts = jnp.concatenate([b_output, b_down], 0)

    def plane_parts(values):
        mine = lax.dynamic_slice_in_dim(values, core * block, block, 1)
        return [lax.dynamic_index_in_dim(mine, seq ^ shift, 0, keepdims=False) for shift in range(seqs)]

    def from_planes(values):
        parts = values.reshape(seqs, block, width)
        return [parts[s] if s == 0 else swap_ctx(parts[s], s * chips) for s in range(seqs)]

    def in_order(parts):
        parts = jnp.stack(parts)
        both = jnp.stack([parts, swap_core(parts)], 1)
        ordered = [
            lax.dynamic_index_in_dim(lax.dynamic_index_in_dim(both, s ^ seq, 0, False), v ^ core, 0, False)
            for s in range(seqs)
            for v in range(2)
        ]
        return jnp.stack(ordered).reshape(1, seqs, local_len, width)

    def paired(parts):
        count = len(parts) // 2
        return tuple(x[0] if count == 1 else jnp.concatenate(x, 0) for x in (parts[:count], parts[count:]))

    def forward(own, save, moves, moved, name, number):
        chip = (own, swap_core(own))
        moves = [("ctx", k) for k in range(1, chips)] + moves
        outs, arrived = front_call(
            chip, norms, w_joint, b_joint, table, w_up, b_up, w_down, save, moves, [own] * (chips - 1) + moved, name, number
        )
        normal, keys, values, queries, ffn0, ffn1, *kept_ffn = outs
        others, arrived = arrived[: chips - 1], arrived[chips - 1 :]
        key_parts, value_parts, normal_parts = [keys], [values], [normal]
        if chips > 1:
            rest = paired([x for other in others for x in (other, swap_core(other))])
            far_normal, far_keys, far_values = joint_call(
                rest, gain_one, shift_one, w_joint, b_joint, table, chip_rows
            )
            key_parts.append(far_keys)
            value_parts.append(far_values)
            normal_parts.append(far_normal)
        attn0, attn1, mixture, lse = attend_call(queries, key_parts, value_parts, places, limits, w_output, block)
        result, moments = merge_call(own, (attn0, swap_core(attn1)), (ffn0, swap_core(ffn1)), shifts)
        return result, moments, (normal_parts, queries, key_parts, value_parts, mixture, lse, *kept_ffn), arrived

    def attention_back(g_pair, kept, deps=()):
        normal_parts, queries, key_parts, value_parts, mixture, lse, second_in, active, slope = kept
        return attend_back_call(
            queries, g_pair, mixture, lse, key_parts, value_parts, places, limits, w_output, table, block, deps
        )

    def far_back(d_keys, d_values, deps=()):
        if chips == 1:
            return []
        far = joint_back_call([d_keys, d_values], chip_rows, length - chip_rows, w_joint, deps)
        if chips > 2:
            far = jnp.concatenate(far, 0).reshape(chips - 1, 2, rows, width)
            far = far[:, 0], far[:, 1]
        sums = (far[0].astype(F32) + swap_core(far[1]).astype(F32)).astype(BF16).reshape(chips - 1, rows, width)
        return [sums[k - 1] for k in range(1, chips)]

    others = [("ctx", k) for k in range(1, chips)]
    planes = [("ctx", s * chips) for s in range(1, seqs)]
    fused = chips == 2 and sections == 2 and seqs == SEQS and block % 128 == 0
    if fused:
        weights = (norms, w_joint, b_joint, table, w_up, b_up, w_down)
        token_rows, *kept, g_rows = gather_call(True, False, *weights, (tokens, cotangent), "gather0", 0)
        attn0, attn1, _, _ = attend_call(
            kept[6], [kept[4], kept[1]], [kept[5], kept[2]], places, limits, w_output, block
        )
        own, *kept = gather_call(
            False, True, *weights, (shifts, attn0, attn1, kept[7], kept[8], token_rows), "gather1", 1
        )
        far_normal, far_keys, far_values, normal, keys, values, queries, ffn0, ffn1, *kept_ffn = kept
        key_parts, value_parts, normal_parts = [keys, far_keys], [values, far_values], [normal, far_normal]
        attn0, attn1, mixture, lse = attend_call(queries, key_parts, value_parts, places, limits, w_output, block)
        kept = (normal_parts, queries, key_parts, value_parts, mixture, lse, *kept_ffn)
        slope = kept_ffn[2]
        g_pair = (g_rows, swap_core(g_rows))
        d_queries, d_keys, d_values, _ = attention_back(g_pair, kept)
        g_own, g_other, home, moments = hand_back_call(
            (d_queries, d_keys, d_values), w_joint, own, g_pair, slope, w_up, w_down, gains, shifts,
            (attn0, attn1), (ffn0, ffn1), "hand_back", 2,
        )
        section_out = home.reshape(1, seqs, local_len, width)
        moments = jnp.sum(moments[:3], axis=1)
        g_pair = (g_own, g_other)
    else:
        token_parts = plane_parts(tokens)
        token_rows = jnp.concatenate([token_parts[0]] + [swap_ctx(token_parts[s], s * chips) for s in range(1, seqs)], 0)
        g_parts = plane_parts(cotangent)
        own = token_rows
        for tick in range(sections):
            first = tick == 0
            result, moments, kept, arrived = forward(
                own, tick == sections - 1, planes if first else [], g_parts[1:] if first else [], "front" + str(tick), tick
            )
            if first:
                g_rows = jnp.concatenate([g_parts[0], *arrived], 0)
            if tick < sections - 1:
                own = jnp.where(section == 0, token_rows, next_section(result, 1))
        out_parts = from_planes(result)
        moments = jnp.sum(moments[:3], axis=1)
        slope = kept[-1]
        g_own = g_rows
        for tick in range(sections - 1):
            g_pair = (g_own, swap_core(g_own))
            d_queries, d_keys, d_values, _ = attention_back(g_pair, kept)
            sums = far_back(d_keys, d_values, tuple(out_parts) if tick == 0 else ())
            near, second, arrivals = rear_call(
                (d_queries, d_keys, d_values), w_joint, g_pair, slope, w_up, w_down, others, sums, "rear" + str(tick), sections + tick
            )
            firsts = [near[0], swap_core(near[1]), *arrivals]
            d_own, _ = norm_back_call(own, g_own, firsts, [second[0], swap_core(second[1])], gains)
            g_own = jnp.where(section == sections - 1, g_rows, next_section(d_own, -1))
        section_out = in_order(out_parts)
        g_pair = (g_own, swap_core(g_own))
    normal_parts, queries, key_parts, value_parts, mixture, lse, second_in, active, slope = kept

    local = w_output.shape[0]
    units = w_up.shape[1]

    def results(section_out, home, small, core_words, joint_total, output_total, up_total, down_total):
        both, ones = small[:core_words].reshape(-1), small[core_words:].reshape(-1)
        norm_total = both[: 5 * width].reshape(5, 1, width)
        root_means = jnp.sqrt(both[5 * width : 5 * width + 3] / (length * seqs * width))
        return (
            section_out,
            home.reshape(1, seqs, local_len, width),
            norm_total[0],
            norm_total[1],
            norm_total[2],
            norm_total[3],
            joint_total[None],
            ones[: 3 * local].reshape(1, 3, local),
            output_total[None],
            norm_total[4],
            up_total[None],
            ones[3 * local : 3 * local + units].reshape(1, units),
            down_total[None],
            norm_total[4],
            root_means[None],
        )

    late = tuple(member_masks + seq_masks)
    early = tuple(seq_masks + member_masks)
    late_owners = jnp.stack([ctx ^ m for m in mask_order(late)]).astype(jnp.int32)
    early_owners = jnp.stack([ctx ^ m for m in mask_order(early)]).astype(jnp.int32)
    share = width // ctx_size
    by_blocks = share % 128 == 0 and chips == 2

    def of_g(right, name, deps=()):
        if by_blocks:
            terms = [(g_pair[0], right, 0), (g_pair[1], right, 1)]
        else:
            terms = [(jnp.concatenate(g_pair, 0), right, 0)]
        return slope_call(late_owners, terms, name, (0, 1), deps)

    down = of_g(active, "down_slope")
    down_arrived = swap_ctx(down[1], late[0])
    output = of_g(mixture, "output_slope", (down[0],))
    second0, second1, d_hidden, up_sums = ffn_back_call(g_pair, slope, w_up, w_down, (output[0],))
    ups = [slope_call(early_owners, [(second_in, d_hidden, 0)], "up_slope", (0, 2))]
    ups.append(slope_call(early_owners, [(second_in, d_hidden, 0)], "up_slope", (1, 2), (ups[0][0],)))
    ups_arrived = [swap_ctx(part[1], early[0]) for part in ups]
    d_queries, d_keys, d_values, joint_sums = attention_back(g_pair, kept, (ups[1][0], output[0]))
    seconds = [second0, second1]

    def in_words(values):
        values = values.reshape(-1)
        return jnp.pad(values, (0, -values.size % 1024)).reshape(-1, 128)

    grads = (d_queries, d_keys, d_values)
    ones = in_words(jnp.concatenate([joint_sums[:3].reshape(-1), up_sums.reshape(-1)]))
    if by_blocks and len(late) == 3:
        both = in_words(jnp.concatenate([jnp.zeros((5 * width,), F32), moments]))
        pairs = [(part[0], there) for part, there in zip(ups, ups_arrived)]
        output_total, joint_total, down_total, up_total, home, small = tail_call(
            grads, w_joint, normal_parts, own, g_own, seconds, gains, jnp.concatenate([both, ones], 0), both.shape[0],
            output, (down[0], down_arrived), pairs, (late, early), seqs, 2 * sections,
        )
        return results(section_out, home, small, both.shape[0], joint_total, output_total, up_total, down_total)
    sums = far_back(d_keys, d_values, (down_arrived, *ups_arrived))

    def halved(pair, arrived):
        total = (pair[0].astype(F32) + arrived.astype(F32)).astype(BF16)
        return total[: total.shape[0] // 2], total[total.shape[0] // 2 :]

    down = halved(down, down_arrived)
    ups[0] = halved(ups[0], ups_arrived[0])
    near = joint_back_call(grads, 0, chip_rows, w_joint)
    down_arrived, ups_arrived[0] = swap_ctx(down[1], late[1]), swap_ctx(ups[0][1], early[1])
    arrivals = [swap_ctx(part, k + 1) for k, part in enumerate(sums)]
    joints = [slope_call(late_owners, [(normal_parts[0], d_queries, 0)], "query_slope")]
    for grad in grads[1:]:
        joints.append(slope_call(late_owners, [(part, grad, n) for n, part in enumerate(normal_parts)], "key_slope"))
    firsts = [near[0], swap_core(near[1]), *arrivals]
    d_own, norm_sums = norm_back_call(own, g_own, firsts, [second0, swap_core(second1)], gains)
    both = in_words(jnp.concatenate([norm_sums[:5].reshape(-1), moments]))
    chains = [
        (late, False, output),
        (late, False, joints[0]),
        (late, False, joints[1]),
        (late, False, joints[2]),
        (early[1:], True, (ups[1][0], ups_arrived[1])),
        (late[2:], True, (down[0], down_arrived)),
        (early[2:], True, (ups[0][0], ups_arrived[0])),
    ]
    events = [c for step in range(len(late)) for c, chain in enumerate(chains) if step < len(chain[0])]
    output_total, *joint_total, up_right, down_total, up_left, home, small = finish_call(
        chains, events, d_own, jnp.concatenate([both, ones], 0), both.shape[0], seqs, chips, 2 * sections + 1
    )
    joint_total = jnp.stack(joint_total)
    up_total = jnp.concatenate([up_left, up_right], 1)
    output_total, down_total = output_total.T, down_total.T
    return results(section_out, home, small, both.shape[0], joint_total, output_total, up_total, down_total)


def solution(mesh):
    in_specs = (
        P(None, "ctx", None),
        P(None, "ctx", None),
        P(),
        P("section", None),
        P("section", None),
        P("section", None),
        P("section", None),
        P("section", None, None, "tp"),
        P("section", None, "tp"),
        P("section", "tp", None),
        P("section", None),
        P("section", None, "tp"),
        P("section", "tp"),
        P("section", "tp", None),
        P("section", None),
    )
    out_specs = (
        P("section", None, "ctx", None),
        P("section", None, "ctx", None),
        P("section", None),
        P("section", None),
        P("section", None),
        P("section", None),
        P("section", None, "ctx", "tp"),
        P("section", None, "tp"),
        P("section", "tp", "ctx"),
        P("section", None),
        P("section", "ctx", "tp"),
        P("section", "tp"),
        P("section", "tp", "ctx"),
        P("section", None),
        P("section", None),
    )
    return jax.shard_map(
        on_device, mesh=mesh, in_specs=in_specs, out_specs=out_specs, check_vma=False
    )
```

```python
import functools

import jax
import jax.numpy as jnp
from jax import lax
from jax.experimental import pallas as pl
from jax.experimental.pallas import tpu as pltpu
from jax.sharding import PartitionSpec as P

HEAD = 64
ROT = 16
EPS = 1e-05
ROTARY_BASE = 10000.0
NEGATIVE = -1e30
SEQS = 4
STACK = 4
GROUP = STACK * HEAD
KEY_TILE = 512
HALF_TILE = KEY_TILE // 2
VMEM_LIMIT = 60 * 1024 * 1024
BF16 = jnp.bfloat16
F32 = jnp.float32


def dot(a, b):
    return jnp.dot(a, b, preferred_element_type=F32)


def dot_nt(a, b):
    return lax.dot_general(a, b, (((1,), (1,)), ((), ())), preferred_element_type=F32)


def params_of(**more):
    return pltpu.CompilerParams(vmem_limit_bytes=VMEM_LIMIT, **more)


def whole(shape):
    return pl.BlockSpec(shape, lambda *_: (0,) * len(shape))


def rows_of(tile, *rest):
    return pl.BlockSpec((tile, *rest), lambda r, *_: (r,) + (0,) * len(rest))


def halves_of(tile, count, *rest):
    return [
        pl.BlockSpec((tile, *rest), lambda r, *_: (jnp.minimum(r, count - 1),) + (0,) * len(rest)),
        pl.BlockSpec((tile, *rest), lambda r, *_: (jnp.maximum(r - count, 0),) + (0,) * len(rest)),
    ]


def pick(refs):
    return jnp.where(pl.program_id(0) < pl.num_programs(0) // 2, refs[0][...], refs[1][...])


def put(refs, value):
    first = pl.program_id(0) < pl.num_programs(0) // 2
    for ref, here in zip(refs, (first, jnp.logical_not(first))):

        @pl.when(here)
        def _():
            ref[...] = value


def waiting(kernel, inputs, deps):
    return lambda *refs: kernel(*refs[:inputs], *refs[inputs + len(deps) :])


def exchanged(position, mask):
    for bit in range(mask.bit_length()):
        if mask >> bit & 1:
            position = position + (1 << bit) - (2 << bit) * (position // (1 << bit) % 2)
    return position


def carrying(kernel, inputs, outputs, moves):
    count = len(moves)

    def body(*refs):
        sources = refs[inputs : inputs + count]
        outs = refs[inputs + count : inputs + count + outputs]
        targets = refs[inputs + count + outputs : inputs + 2 * count + outputs]
        *scratch, send, receive = refs[inputs + 2 * count + outputs :]
        partners = [{axis: exchanged(lax.axis_index(axis), mask)} for axis, mask in moves]
        copies = [
            pltpu.make_async_remote_copy(
                source, target, send.at[n], receive.at[n], device_id=partner, device_id_type=pl.DeviceIdType.MESH
            )
            for n, (source, target, partner) in enumerate(zip(sources, targets, partners))
        ]

        @pl.when(pl.program_id(0) == 0)
        def _():
            barrier = pltpu.get_barrier_semaphore()
            for partner in partners:
                pl.semaphore_signal(barrier, inc=1, device_id=partner, device_id_type=pl.DeviceIdType.MESH)
            pl.semaphore_wait(barrier, count)
            for copy in copies:
                copy.start()

        kernel(*refs[:inputs], *outs, *scratch)

        @pl.when(pl.program_id(0) == pl.num_programs(0) - 1)
        def _():
            for copy in copies:
                copy.wait()

    return body


def carrier_semaphores(count):
    return [pltpu.SemaphoreType.DMA((count,)), pltpu.SemaphoreType.DMA((count,))]


def anywhere(count):
    return [pl.BlockSpec(memory_space=pl.ANY)] * count


def cost(flops, size):
    return pl.CostEstimate(flops=int(flops), bytes_accessed=int(size), transcendentals=0)


def shape_of(*shape, dtype=BF16):
    return jax.ShapeDtypeStruct(shape, dtype)


def normalize(values):
    middle = jnp.mean(values, axis=-1, keepdims=True)
    centered = values - middle
    spread = jnp.mean(centered * centered, axis=-1, keepdims=True)
    inverse = lax.rsqrt(spread + EPS)
    return centered * inverse, inverse


def turn(values, cosine, sine):
    pieces = []
    for start in range(0, values.shape[1], 128):
        part = values[:, start : start + 128]
        ahead = pltpu.roll(part, 128 - ROT // 2, 1)
        behind = pltpu.roll(part, ROT // 2, 1)
        entry = lax.broadcasted_iota(jnp.int32, part.shape, 1) % HEAD
        pieces.append(part * cosine + jnp.where(entry < ROT // 2, -ahead, behind) * sine)
    return jnp.concatenate(pieces, axis=1)


def joint_kernel(h0_ref, h1_ref, gain_ref, shift_ref, w_ref, b_ref, cos_ref, sin_ref, n_ref, k_ref, v_ref):
    scaled, _ = normalize(pick((h0_ref, h1_ref)).astype(F32))
    low = (scaled * gain_ref[...] + shift_ref[...]).astype(BF16)
    n_ref[...] = low
    cosine, sine = cos_ref[...], sin_ref[...]
    keys = dot(low, w_ref[1]) + b_ref[1:2]
    values = dot(low, w_ref[2]) + b_ref[2:3]
    k_ref[...] = turn(keys, cosine, sine).astype(BF16)
    v_ref[...] = values.astype(BF16)


def joint_call(pair, gain, shift, w_joint, b_joint, table, offset, deps=()):
    rows, width = pair[0].shape
    local = w_joint.shape[2]
    tile = min(512, rows)
    first = offset // tile
    count = 2
    turns = pl.BlockSpec((tile, 128), lambda r: (first + r, 0))
    return pl.pallas_call(
        waiting(joint_kernel, 8, deps),
        grid=(2 * rows // tile,),
        in_specs=halves_of(tile, rows // tile, width)
        + [whole((1, width)), whole((1, width)), whole(w_joint.shape), whole(b_joint.shape), turns, turns]
        + anywhere(len(deps)),
        out_specs=[rows_of(tile, width)] + [rows_of(tile, local)] * count,
        out_shape=[shape_of(2 * rows, width)] + [shape_of(2 * rows, local)] * count,
        compiler_params=params_of(),
        cost_estimate=cost(4 * rows * width * local * count, 8 * rows * width + 2 * w_joint.size),
        name="joint_projection",
    )(*pair, gain, shift, w_joint, b_joint, *table, *deps)


def gelu_parts(x):
    return 0.5 + 0.5 * lax.erf(x * 0.5**0.5), jnp.exp(-0.5 * x * x)


def front_kernel(
    save, h0_ref, h1_ref, norms_ref, w_ref, b_ref, cos_ref, sin_ref, up_ref, up_b_ref, down_ref,
    n_ref, k_ref, v_ref, q_ref, part0_ref, part1_ref, *saved
):
    scaled, _ = normalize(pick((h0_ref, h1_ref)).astype(F32))
    low = (scaled * norms_ref[0:1] + norms_ref[1:2]).astype(BF16)
    n_ref[...] = low
    cosine, sine = cos_ref[...], sin_ref[...]
    keys = dot(low, w_ref[1]) + b_ref[1:2]
    values = dot(low, w_ref[2]) + b_ref[2:3]
    queries = dot(low, w_ref[0]) + b_ref[0:1]
    q_ref[...] = (turn(queries, cosine, sine) * HEAD ** (-0.5)).astype(BF16)
    k_ref[...] = turn(keys, cosine, sine).astype(BF16)
    v_ref[...] = values.astype(BF16)
    low = (scaled * norms_ref[2:3] + norms_ref[3:4]).astype(BF16)
    if save:
        saved[0][...] = low
    total = None
    for start in range(0, up_ref.shape[1], 512):
        cut = pl.ds(start, 512)
        hidden = dot(low, up_ref[:, cut]) + up_b_ref[:, cut]
        share, bell = gelu_parts(hidden)
        active = (hidden * share).astype(BF16)
        if save:
            saved[1][:, cut] = active
            saved[2][:, cut] = (share + hidden * bell * 0.3989422804014327).astype(BF16)
        term = dot(active, down_ref[cut, :])
        total = term if total is None else total + term
    put((part0_ref, part1_ref), total.astype(BF16))


def front_call(pair, norms, w_joint, b_joint, table, w_up, b_up, w_down, save, moves, moved, name, number):
    rows, width = pair[0].shape
    local = w_joint.shape[2]
    units = w_up.shape[1]
    tile = min(512, rows)
    out = [shape_of(2 * rows, width)] + [shape_of(2 * rows, local)] * 3 + [shape_of(rows, width)] * 2
    out_specs = [rows_of(tile, width)] + [rows_of(tile, local)] * 3 + halves_of(tile, rows // tile, width)
    if save:
        out += [shape_of(2 * rows, width)] + [shape_of(2 * rows, units)] * 2
        out_specs += [rows_of(tile, width), rows_of(tile, units), rows_of(tile, units)]
    ins = (norms, w_joint, b_joint, *table, w_up, b_up, w_down)
    turns = rows_of(tile, 128)
    specs = [turns if x is table[0] or x is table[1] else whole(x.shape) for x in ins]
    outs = pl.pallas_call(
        carrying(functools.partial(front_kernel, save), 2 + len(ins), len(out), moves),
        grid=(2 * rows // tile,),
        in_specs=halves_of(tile, rows // tile, width) + specs + anywhere(len(moves)),
        out_specs=out_specs + anywhere(len(moves)),
        out_shape=out + [shape_of(*x.shape) for x in moved],
        scratch_shapes=carrier_semaphores(len(moves)),
        compiler_params=params_of(collective_id=number, has_side_effects=True),
        cost_estimate=cost(4 * rows * width * (3 * local + 2 * units), 4 * w_up.size + 16 * rows * width),
        name=name,
    )(*pair, *ins, *moved)
    return outs[: len(out)], outs[len(out) :]


class Traffic:
    def __init__(self):
        self.started = []

    def send(self, source, target, first, second, device):
        copy = pltpu.make_async_remote_copy(
            source, target, first, second, device_id=device, device_id_type=pl.DeviceIdType.MESH
        )
        copy.start()
        self.started.append(copy)
        return copy

    def finish(self):
        for copy in self.started:
            copy.wait_send()


def greet(partners):
    barrier = pltpu.get_barrier_semaphore()
    for partner in partners:
        pl.semaphore_signal(barrier, inc=1, device_id=partner, device_id_type=pl.DeviceIdType.MESH)
    pl.semaphore_wait(barrier, len(partners))


def gather_kernel(first, save, seqs, *refs):
    refs = list(refs)
    take = lambda count: [refs.pop(0) for _ in range(count)]
    norms_ref, b_joint_ref, cos_ref, sin_ref, up_b_ref, w_in, up_in, down_in = take(8)
    if first:
        tokens_ref, cotangent_ref = take(2)
    else:
        shifts_ref, a0_in, a1_in, f0_in, f1_in, h_in = take(6)
    outs = take(13 if save else 10)
    own_out, far_outs, near_outs = outs[0], outs[1:4], outs[4:]
    if first:
        g_out = take(1)[0]
    own, other, far0, far1, w, up, down = take(7)
    far_stage = take(3)
    near_stage = take(len(near_outs))
    if not first:
        a0, a1, f0, f1, h, got, a_got, f_got = take(8)
    load, store, arrive_s, arrive_r, core_s, core_r, chip_s, chip_r, far_s, far_r, side_s, side_r = refs
    me, core, section = lax.axis_index("ctx"), lax.axis_index("tp"), lax.axis_index("section")
    rows, width = own.shape
    block = rows // seqs
    chips = 2
    seq = me // chips
    other_core, other_chip, twin = {"tp": 1 - core}, {"ctx": exchanged(me, 1)}, {"section": 1 - section}
    traffic = Traffic()

    def at(c):
        return pl.ds(c * block, block)

    copies = [pltpu.make_async_copy(a, b, load.at[n]) for n, (a, b) in enumerate(((w_in, w), (up_in, up), (down_in, down)))]
    if not first:
        extra = [
            pltpu.make_async_copy(a, b, load.at[3 + n])
            for n, (a, b) in enumerate(((a0_in, a0), (f0_in, f0), (h_in, h)))
        ]
        for copy in extra:
            copy.start()
    for copy in copies:
        copy.start()
    if first:
        planes = [{"ctx": exchanged(me, c * chips)} for c in range(1, seqs)]
        greet([other_core, other_chip] + planes)
        mine = pl.ds(pl.multiple_of(core * block, block), block)
        stay = [
            pltpu.make_async_copy(tokens_ref.at[seq, mine], own.at[at(0)], load.at[3]),
            pltpu.make_async_copy(cotangent_ref.at[seq, mine], g_out.at[at(0)], load.at[4]),
        ]
        for copy in stay:
            copy.start()
        arrivals = [None]
        for c in range(1, seqs):
            source = tokens_ref.at[exchanged(seq, c), mine]
            arrivals.append(traffic.send(source, own.at[at(c)], arrive_s.at[c], arrive_r.at[c], planes[c - 1]))
        sides = []
        for c in range(1, seqs):
            source = cotangent_ref.at[exchanged(seq, c), mine]
            sides.append(traffic.send(source, g_out.at[at(c)], side_s.at[c], side_r.at[c], planes[c - 1]))
    else:
        greet([other_core, other_chip, twin])
        swaps = [
            traffic.send(a1_in, a_got, side_s.at[0], side_r.at[0], other_core),
            traffic.send(f1_in, f_got, side_s.at[1], side_r.at[1], other_core),
        ]
        for copy in extra:
            copy.wait()
        for copy in swaps:
            copy.wait_recv()
        arrivals = []
        for c in range(seqs):
            cut = slice(c * block, (c + 1) * block)
            attention = a0[cut].astype(F32) + a_got[cut].astype(F32) + shifts_ref[0:1]
            feedforward = f0[cut].astype(F32) + f_got[cut].astype(F32) + shifts_ref[1:2]
            a1[cut] = (h[cut].astype(F32) + attention + feedforward).astype(BF16)
            arrivals.append(traffic.send(a1.at[at(c)], got.at[at(c)], arrive_s.at[c], arrive_r.at[c], twin))

    to_core, to_chip, to_far = [None] * seqs, [None] * seqs, [None] * seqs

    def arrive(c):
        if first and c == 0:
            stay[0].wait()
        else:
            arrivals[c].wait_recv()
        if not first:
            cut = slice(c * block, (c + 1) * block)
            own[cut] = jnp.where(section == 0, h[cut], got[cut])
        here = own.at[at(c)]
        to_core[c] = traffic.send(here, other.at[at(c)], core_s.at[c], core_r.at[c], other_core)
        to_chip[c] = traffic.send(here, far0.at[at(c)], chip_s.at[c], chip_r.at[c], other_chip)

    def arrive_far(c):
        to_chip[c].wait_recv()
        to_far[c] = traffic.send(far0.at[at(c)], far1.at[at(c)], far_s.at[c], far_r.at[c], other_core)

    n_st, k_st, v_st, q_st, part0_st, part1_st = near_stage[:6]
    half = block

    def near_rows(ref, part, value, base=0):
        ref[base + part * half : base + (part + 1) * half] = value

    def near_joint(part):
        cut = slice(part * half, (part + 1) * half)
        scaled, _ = normalize(jnp.concatenate([own[cut], other[cut]], 0).astype(F32))
        low = (scaled * norms_ref[0:1] + norms_ref[1:2]).astype(BF16)
        second = (scaled * norms_ref[2:3] + norms_ref[3:4]).astype(BF16)
        turns = [
            jnp.concatenate([ref[cut], ref[rows + part * half : rows + (part + 1) * half]], 0) for ref in (cos_ref, sin_ref)
        ]
        queries = turn(dot(low, w[0]) + b_joint_ref[0:1], *turns) * HEAD ** (-0.5)
        keys = turn(dot(low, w[1]) + b_joint_ref[1:2], *turns)
        values = dot(low, w[2]) + b_joint_ref[2:3]
        for ref, value in ((n_st, low), (q_st, queries), (k_st, keys), (v_st, values)):
            value = value.astype(BF16)
            near_rows(ref, part, value[:half])
            near_rows(ref, part, value[half:], rows)
        if save:
            near_rows(near_stage[6], part, second[:half])
            near_rows(near_stage[6], part, second[half:], rows)
        return second

    def near_ffn(part, low):
        total = None
        for start in range(0, up.shape[1], 512):
            cut = slice(start, start + 512)
            hidden = dot(low, up[:, cut]) + up_b_ref[:, cut]
            share, bell = gelu_parts(hidden)
            active = (hidden * share).astype(BF16)
            if save:
                slope = (share + hidden * bell * 0.3989422804014327).astype(BF16)
                for ref, value in ((near_stage[7], active), (near_stage[8], slope)):
                    ref[part * half : (part + 1) * half, cut] = value[:half]
                    ref[rows + part * half : rows + (part + 1) * half, cut] = value[half:]
            term = dot(active, down[cut, :])
            total = term if total is None else total + term
        near_rows(part0_st, part, total[:half].astype(BF16))
        near_rows(part1_st, part, total[half:].astype(BF16))

    def far_joint(u, ref):
        scaled, _ = normalize(ref[...].astype(F32))
        low = (scaled * norms_ref[0:1] + norms_ref[1:2]).astype(BF16)
        cut = slice(u * rows, (u + 1) * rows)
        turns = [table[2 * rows + u * rows : 2 * rows + (u + 1) * rows] for table in (cos_ref, sin_ref)]
        far_stage[0][cut] = low
        far_stage[1][cut] = turn(dot(low, w[1]) + b_joint_ref[1:2], *turns).astype(BF16)
        far_stage[2][cut] = (dot(low, w[2]) + b_joint_ref[2:3]).astype(BF16)

    for c in range(seqs):
        arrive(c)
        if c == 0:
            copies[0].wait()
        else:
            arrive_far(c - 1)
        to_core[c].wait_recv()
        low = near_joint(c)
        if c == 0:
            copies[1].wait()
            copies[2].wait()
        near_ffn(c, low)
    arrive_far(seqs - 1)
    stores = [pltpu.make_async_copy(own, own_out, store.at[0])]
    stores += [pltpu.make_async_copy(a, b, store.at[1 + n]) for n, (a, b) in enumerate(zip(near_stage, near_outs))]
    for copy in stores:
        copy.start()
    far_joint(0, far0)
    for c in range(seqs):
        to_far[c].wait_recv()
    far_joint(1, far1)
    base = 1 + len(near_outs)
    late = [pltpu.make_async_copy(a, b, store.at[base + n]) for n, (a, b) in enumerate(zip(far_stage, far_outs))]
    for copy in late:
        copy.start()
    if first:
        stay[1].wait()
        for copy in sides:
            copy.wait_recv()
    traffic.finish()
    for copy in stores + late:
        copy.wait()


def gather_call(first, save, norms, w_joint, b_joint, table, w_up, b_up, w_down, sources, name, number):
    rows = (sources[0].shape[0] * sources[0].shape[1] // 2) if first else sources[-1].shape[0]
    seqs = SEQS
    width, local, units = w_up.shape[0], w_joint.shape[2], w_up.shape[1]
    wide, narrow = (rows, width), (2 * rows, local)
    near = [(2 * rows, width), narrow, narrow, narrow, wide, wide]
    if save:
        near += [(2 * rows, width), (2 * rows, units), (2 * rows, units)]
    far = [(2 * rows, width), narrow, narrow]
    out = [wide, *far, *near] + ([wide] if first else [])
    ins = (norms, b_joint, *table, b_up)
    extra = [] if first else [whole(sources[0].shape)]
    scratch = [wide] * 4 + [w_joint.shape, w_up.shape, w_down.shape] + far + near + ([] if first else [wide] * 8)
    pair = carrier_semaphores(seqs)
    return pl.pallas_call(
        functools.partial(gather_kernel, first, save, seqs),
        grid=(1,),
        in_specs=[whole(x.shape) for x in ins] + anywhere(3) + extra + anywhere(len(sources) - len(extra)),
        out_specs=anywhere(len(out)),
        out_shape=[shape_of(*x) for x in out],
        scratch_shapes=[pltpu.VMEM(x, BF16) for x in scratch]
        + [pltpu.SemaphoreType.DMA((6,)), pltpu.SemaphoreType.DMA((len(out),))]
        + pair * 5,
        compiler_params=params_of(collective_id=number, has_side_effects=True),
        name=name,
    )(*ins, w_joint, w_up, w_down, *sources)


def ffn_back_kernel(g0_ref, g1_ref, slope_ref, up_ref, down_ref, part0_ref, part1_ref, hidden_ref, sums_ref):
    upstream = pick((g0_ref, g1_ref))
    units = up_ref.shape[1]

    @pl.when(pl.program_id(0) == 0)
    def _():
        sums_ref[...] = jnp.zeros_like(sums_ref)

    total = None
    for start in range(0, units, 512):
        cut = pl.ds(start, 512)
        d_active = dot_nt(upstream, down_ref[cut, :])
        d_hidden = (d_active * slope_ref[:, cut].astype(F32)).astype(BF16)
        hidden_ref[:, cut] = d_hidden
        sums_ref[:, cut] += jnp.sum(d_hidden.astype(F32), axis=0, keepdims=True)
        term = dot_nt(d_hidden, up_ref[:, cut])
        total = term if total is None else total + term
    put((part0_ref, part1_ref), total.astype(BF16))


def ffn_back_call(pair, slope, w_up, w_down, deps=()):
    rows, width = pair[0].shape
    units = w_up.shape[1]
    tile = min(512, rows)
    return pl.pallas_call(
        waiting(ffn_back_kernel, 5, deps),
        grid=(2 * rows // tile,),
        in_specs=halves_of(tile, rows // tile, width) + [rows_of(tile, units), whole(w_up.shape), whole(w_down.shape)]
        + anywhere(len(deps)),
        out_specs=halves_of(tile, rows // tile, width) + [rows_of(tile, units), whole((1, units))],
        out_shape=[shape_of(rows, width)] * 2 + [shape_of(2 * rows, units), shape_of(1, units, dtype=F32)],
        compiler_params=params_of(),
        cost_estimate=cost(8 * rows * width * units, 4 * w_up.size + 8 * rows * (width + units)),
        name="feed_forward_back",
    )(*pair, slope, w_up, w_down, *deps)


def start_sorted(places_ref, parts, targets, sem, block):
    copies = []
    for refs, target in zip(parts, targets):
        index = 0
        for ref in refs:
            for local in range(ref.shape[0] // block):
                place = pl.ds(pl.multiple_of(places_ref[index] * block, block), block)
                copies.append(pltpu.make_async_copy(ref.at[pl.ds(local * block, block)], target.at[place], sem))
                index += 1
    for copy in copies:
        copy.start()
    return copies


def transpose_into(source, target):
    rows, columns = source.shape

    def step(index, _):
        start = pl.multiple_of(index * 256, 256)
        for column in range(0, columns, 256):
            target[column : column + 256, pl.ds(start, 256)] = source[pl.ds(start, 256), column : column + 256].T
        return 0

    lax.fori_loop(0, rows // 256, step, 0)


def stacked(values):
    owner = lax.broadcasted_iota(jnp.int32, values.shape, 1) // HEAD
    zero = jnp.zeros_like(values)
    return jnp.concatenate([jnp.where(owner == a, values, zero) for a in range(STACK)], axis=0)


def spots_of(places_ref, step, tile, block, shape, axis):
    at = lax.broadcasted_iota(jnp.int32, shape, axis) % tile
    count = tile // block
    spot = at + places_ref[step * count] * block
    for s in range(1, count):
        spot = jnp.where(at >= s * block, at - s * block + places_ref[step * count + s] * block, spot)
    return spot


def attend_kernel(block, tile, remote, places_ref, limits_ref, q_ref, wo_ref, *refs):
    key_refs, value_refs = refs[: 1 + remote], refs[1 + remote : 2 + 2 * remote]
    part0_ref, part1_ref, mix_ref, lse_ref, keys, values, scores_ref, sem = refs[2 + 2 * remote :]
    groups = q_ref.shape[1] // GROUP
    half = part0_ref.shape[0]
    rows = STACK * tile
    lanes = [slice(g * GROUP, (g + 1) * GROUP) for g in range(groups)]
    for copy in start_sorted(places_ref, (key_refs, value_refs), (keys, values), sem, block):
        copy.wait()

    def tile_step(step, _):
        mine = pl.ds(pl.multiple_of(step * tile, tile), tile)
        heads = [stacked(q_ref[mine, lane]) for lane in lanes]
        spots = spots_of(places_ref, step, tile, block, (rows, 128), 0)

        def attend_to(count):
            length = count * HALF_TILE
            open_end = length - HALF_TILE if tile == block else 0
            spans = [(start, min(KEY_TILE, length - start)) for start in range(0, length, KEY_TILE)]
            tops = []
            for g, lane in enumerate(lanes):
                top = None
                for start, extent in spans:
                    scores = dot_nt(heads[g], keys[start : start + extent, lane])
                    for column in range(0, extent, 128):
                        piece = scores[:, column : column + 128]
                        if start + column >= open_end:
                            spot = start + column + lax.broadcasted_iota(jnp.int32, piece.shape, 1)
                            piece = jnp.where(spot <= spots, piece, NEGATIVE)
                        scores_ref[g, :, start + column : start + column + 128] = piece
                        top = piece if top is None else jnp.maximum(top, piece)
                tops.append(jnp.broadcast_to(jnp.max(top, axis=1, keepdims=True), (rows, 128)))
            for g, lane in enumerate(lanes):
                mass, total = None, None
                for start, extent in spans:
                    raised = []
                    for column in range(start, start + extent, 128):
                        piece = jnp.exp(scores_ref[g, :, column : column + 128] - tops[g])
                        mass = piece if mass is None else mass + piece
                        raised.append(piece.astype(BF16))
                    term = dot(jnp.concatenate(raised, axis=1), values[start : start + extent, lane])
                    total = term if total is None else total + term
                mass = jnp.broadcast_to(jnp.sum(mass, axis=1, keepdims=True), (rows, 128))
                total = total * jnp.concatenate([1.0 / mass] * (GROUP // 128), axis=1)
                owner = lax.broadcasted_iota(jnp.int32, (tile, GROUP), 1) // HEAD
                mixture = total[:tile]
                for a in range(1, STACK):
                    mixture = jnp.where(owner == a, total[a * tile : (a + 1) * tile], mixture)
                mix_ref[mine, lane] = mixture.astype(BF16)
                lse = tops[g] + jnp.log(mass)
                for a in range(STACK):
                    lse_ref[step, g : g + 1, a * tile : (a + 1) * tile] = lse[a * tile : (a + 1) * tile].T[0:1]

        for count in range(1, keys.shape[0] // HALF_TILE + 1):
            pl.when(limits_ref[step, 1] == count)(functools.partial(attend_to, count))
        return 0

    lax.fori_loop(0, q_ref.shape[0] // tile, tile_step, 0)
    part0_ref[...] = dot(mix_ref[:half], wo_ref[...]).astype(BF16)
    part1_ref[...] = dot(mix_ref[half:], wo_ref[...]).astype(BF16)


def attend_call(queries, key_parts, value_parts, places, limits, w_output, block, deps=()):
    rows, local = queries.shape
    width = w_output.shape[1]
    tile = rows // limits.shape[0]
    length = sum(part.shape[0] for part in key_parts)
    groups = local // GROUP
    outs = [(rows // 2, width), (rows // 2, width), (rows, local), (rows // tile, groups, STACK * tile)]
    return pl.pallas_call(
        waiting(functools.partial(attend_kernel, block, tile, len(key_parts) - 1), 4 + 2 * len(key_parts), deps),
        grid_spec=pltpu.PrefetchScalarGridSpec(
            num_scalar_prefetch=2,
            grid=(1,),
            in_specs=[whole((rows, local)), whole(w_output.shape)] + anywhere(2 * len(key_parts) + len(deps)),
            out_specs=[whole(shape) for shape in outs],
            scratch_shapes=[
                pltpu.VMEM((length, local), BF16),
                pltpu.VMEM((length, local), BF16),
                pltpu.VMEM((groups, STACK * tile, length), F32),
                pltpu.SemaphoreType.DMA,
            ],
        ),
        out_shape=[shape_of(*shape) for shape in outs[:3]] + [shape_of(*outs[3], dtype=F32)],
        compiler_params=params_of(),
        cost_estimate=cost(12 * rows * length * local, 2 * length * local * 4),
        name="attend",
    )(places, limits, queries, w_output, *key_parts, *value_parts, *deps)


def attend_back_kernel(
    block, tile, remote, places_ref, limits_ref, q_ref, g0_ref, g1_ref, mix_ref, lse_ref, wo_ref, cos_ref, sin_ref, *refs
):
    key_refs, value_refs = refs[: 1 + remote], refs[1 + remote : 2 + 2 * remote]
    (dq_ref, dk_ref, dv_ref, sums_ref, keys, values, keys_t, d_keys, d_values, d_mixture, inner, total, d_queries, sem) = refs[
        2 + 2 * remote :
    ]
    groups = q_ref.shape[1] // GROUP
    rows = q_ref.shape[0]
    half = g0_ref.shape[0]
    lanes = [slice(g * GROUP, (g + 1) * GROUP) for g in range(groups)]
    copies = start_sorted(places_ref, (key_refs, value_refs), (keys, values), sem, block)
    d_keys[...] = jnp.zeros_like(d_keys)
    d_values[...] = jnp.zeros_like(d_values)
    head_of = lax.broadcasted_iota(jnp.int32, (8, GROUP), 1) // HEAD
    picker = jnp.where(lax.broadcasted_iota(jnp.int32, (8, GROUP), 0) == head_of, 1.0, 0.0).astype(BF16)
    for index, ref in enumerate((g0_ref, g1_ref)):
        cut = pl.ds(index * half, half)
        low = dot_nt(ref[...], wo_ref[...]).astype(BF16)
        d_mixture[cut, :] = low
        product = low.astype(F32) * mix_ref[cut, :].astype(F32)
        high = product.astype(BF16)
        rest = (product - high.astype(F32)).astype(BF16)
        for g, lane in enumerate(lanes):
            inner[g * 8 : (g + 1) * 8, cut] = dot_nt(picker, high[:, lane]) + dot_nt(picker, rest[:, lane])
    for copy in copies:
        copy.wait()
    transpose_into(keys, keys_t)

    def query_step(step, _):
        mine = pl.ds(pl.multiple_of(step * tile, tile), tile)
        spots = spots_of(places_ref, step, tile, block, (1, STACK * tile), 1)
        heads = [stacked(q_ref[mine, lane]) for lane in lanes]
        sides = [stacked(d_mixture[mine, lane]) for lane in lanes]
        sums = [
            jnp.concatenate([inner[g * 8 + a : g * 8 + a + 1, mine] for a in range(STACK)], axis=1) for g in range(groups)
        ]
        lse = [lse_ref[step, g : g + 1, :] for g in range(groups)]
        total[...] = jnp.zeros_like(total)

        def key_step(masked, extent, index, carry):
            start = pl.multiple_of(index * KEY_TILE, KEY_TILE)
            cut = pl.ds(start, extent)
            for g, lane in enumerate(lanes):
                scores = dot_nt(keys[cut, lane], heads[g])
                if masked:
                    spot = start + lax.broadcasted_iota(jnp.int32, scores.shape, 0)
                    scores = jnp.where(spot <= spots, scores, NEGATIVE)
                weights = jnp.exp(scores - lse[g])
                d_weights = dot_nt(values[cut, lane], sides[g])
                d_scores = (weights * (d_weights - sums[g])).astype(BF16)
                d_values[cut, lane] += dot(weights.astype(BF16), sides[g])
                d_keys[cut, lane] += dot(d_scores, heads[g])
                total[lane, :] += dot(keys_t[lane, cut], d_scores)
            return carry

        whole_tiles = limits_ref[step, 1] // 2
        lax.fori_loop(0, limits_ref[step, 0], functools.partial(key_step, False, KEY_TILE), 0)
        lax.fori_loop(limits_ref[step, 0], whole_tiles, functools.partial(key_step, True, KEY_TILE), 0)

        @pl.when(limits_ref[step, 1] % 2 == 1)
        def _():
            key_step(True, HALF_TILE, whole_tiles, 0)

        for lane in lanes:
            picked = [total[lane, :][a * HEAD : (a + 1) * HEAD, a * tile : (a + 1) * tile] for a in range(STACK)]
            d_queries[mine, lane] = jnp.concatenate(picked, axis=0).T
        return 0

    lax.fori_loop(0, rows // tile, query_step, 0)
    turned = turn(d_queries[...] * HEAD ** (-0.5), cos_ref[:rows], -sin_ref[:rows]).astype(BF16)
    dq_ref[...] = turned
    sums_ref[...] = jnp.zeros_like(sums_ref)
    sums_ref[0:1, :] = jnp.sum(turned.astype(F32), axis=0, keepdims=True)

    def block_step(index, _):
        place = pl.ds(pl.multiple_of(places_ref[index] * block, block), block)
        mine = pl.ds(pl.multiple_of(index * block, block), block)
        turned = turn(d_keys[place, :], cos_ref[mine, :], -sin_ref[mine, :]).astype(BF16)
        dk_ref[mine, :] = turned
        low = d_values[place, :].astype(BF16)
        dv_ref[mine, :] = low
        sums_ref[1:2, :] += jnp.sum(turned.astype(F32), axis=0, keepdims=True)
        sums_ref[2:3, :] += jnp.sum(low.astype(F32), axis=0, keepdims=True)
        return 0

    lax.fori_loop(0, dk_ref.shape[0] // block, block_step, 0)


def attend_back_call(
    queries, g_pair, mixture, lse, key_parts, value_parts, places, limits, w_output, table, block, deps=()
):
    rows, local = queries.shape
    width = w_output.shape[1]
    tile = rows // limits.shape[0]
    length = sum(part.shape[0] for part in key_parts)
    groups = local // GROUP
    ins = (queries, *g_pair, mixture, lse, w_output, *table)
    return pl.pallas_call(
        waiting(
            functools.partial(attend_back_kernel, block, tile, len(key_parts) - 1), 2 + len(ins) + 2 * len(key_parts), deps
        ),
        grid_spec=pltpu.PrefetchScalarGridSpec(
            num_scalar_prefetch=2,
            grid=(1,),
            in_specs=[whole(x.shape) for x in ins] + anywhere(2 * len(key_parts) + len(deps)),
            out_specs=[whole((rows, local)), whole((length, local)), whole((length, local)), whole((8, local))],
            scratch_shapes=[
                pltpu.VMEM((length, local), BF16),
                pltpu.VMEM((length, local), BF16),
                pltpu.VMEM((local, length), BF16),
                pltpu.VMEM((length, local), F32),
                pltpu.VMEM((length, local), F32),
                pltpu.VMEM((rows, local), BF16),
                pltpu.VMEM((8 * groups, rows), F32),
                pltpu.VMEM((local, STACK * tile), F32),
                pltpu.VMEM((rows, local), F32),
                pltpu.SemaphoreType.DMA,
            ],
        ),
        out_shape=[shape_of(rows, local), shape_of(length, local), shape_of(length, local), shape_of(8, local, dtype=F32)],
        compiler_params=params_of(),
        cost_estimate=cost(24 * rows * length * local, 2 * length * local * 8),
        name="attend_back",
    )(places, limits, *ins, *key_parts, *value_parts, *deps)


def joint_back_kernel(count, *refs):
    w_ref = refs[count]
    total = None
    for index in range(count):
        term = dot_nt(refs[index][...], w_ref[3 - count + index])
        total = term if total is None else total + term
    put(refs[count + 1 :], total.astype(BF16))


def joint_back_call(grads, offset, rows, w_joint, deps=()):
    width, local = w_joint.shape[1:]
    half = rows // 2
    tile = min(512, half)
    first = offset // tile
    return pl.pallas_call(
        waiting(functools.partial(joint_back_kernel, len(grads)), len(grads) + 1, deps),
        grid=(rows // tile,),
        in_specs=[pl.BlockSpec((tile, local), lambda r: (first + r, 0))] * len(grads)
        + [whole(w_joint.shape)]
        + anywhere(len(deps)),
        out_specs=halves_of(tile, half // tile, width),
        out_shape=[shape_of(half, width)] * 2,
        compiler_params=params_of(),
        cost_estimate=cost(2 * rows * width * local * len(grads), 2 * rows * (width + 3 * local) + 2 * w_joint.size),
        name="joint_projection_back",
    )(*grads, w_joint, *deps)


def rear_kernel(q_ref, k_ref, v_ref, w_ref, g0_ref, g1_ref, slope_ref, up_ref, down_ref, first0_ref, first1_ref, part0_ref, part1_ref):
    total = dot_nt(q_ref[...], w_ref[0]) + dot_nt(k_ref[...], w_ref[1]) + dot_nt(v_ref[...], w_ref[2])
    put((first0_ref, first1_ref), total.astype(BF16))
    upstream = pick((g0_ref, g1_ref))
    total = None
    for start in range(0, up_ref.shape[1], 512):
        cut = pl.ds(start, 512)
        d_active = dot_nt(upstream, down_ref[cut, :])
        d_hidden = (d_active * slope_ref[:, cut].astype(F32)).astype(BF16)
        term = dot_nt(d_hidden, up_ref[:, cut])
        total = term if total is None else total + term
    put((part0_ref, part1_ref), total.astype(BF16))


def rear_call(grads, w_joint, pair, slope, w_up, w_down, moves, moved, name, number):
    rows, width = pair[0].shape
    local = w_joint.shape[2]
    units = w_up.shape[1]
    tile = min(512, rows)
    halves = halves_of(tile, rows // tile, width)
    outs = pl.pallas_call(
        carrying(rear_kernel, 9, 4, moves),
        grid=(2 * rows // tile,),
        in_specs=[rows_of(tile, local)] * 3
        + [whole(w_joint.shape)]
        + halves
        + [rows_of(tile, units), whole(w_up.shape), whole(w_down.shape)]
        + anywhere(len(moves)),
        out_specs=halves + halves + anywhere(len(moves)),
        out_shape=[shape_of(rows, width)] * 4 + [shape_of(*x.shape) for x in moved],
        scratch_shapes=carrier_semaphores(len(moves)),
        compiler_params=params_of(collective_id=number, has_side_effects=True),
        cost_estimate=cost(4 * rows * width * (3 * local + 2 * units), 4 * w_up.size + 16 * rows * width),
        name=name,
    )(*grads, w_joint, *pair, slope, w_up, w_down, *moved)
    return outs[:2], outs[2:4], outs[4:]


def norm_back_kernel(firsts, h_ref, g_ref, gains_ref, *refs):
    first_refs, second_refs, (out_ref, sums_ref) = refs[:firsts], refs[firsts:-2], refs[-2:]

    @pl.when(pl.program_id(0) == 0)
    def _():
        sums_ref[...] = jnp.zeros_like(sums_ref)

    scaled, inverse = normalize(h_ref[...].astype(F32))
    upstream = g_ref[...].astype(F32)
    d_first = sum(ref[...].astype(F32) for ref in first_refs)
    d_second = sum(ref[...].astype(F32) for ref in second_refs)
    for row, term in enumerate((d_first * scaled, d_first, d_second * scaled, d_second, upstream)):
        sums_ref[row : row + 1, :] += jnp.sum(term, axis=0, keepdims=True)
    d_scaled = d_first * gains_ref[0:1] + d_second * gains_ref[1:2]
    middle = jnp.mean(d_scaled, axis=-1, keepdims=True)
    along = jnp.mean(d_scaled * scaled, axis=-1, keepdims=True)
    out_ref[...] = (upstream + inverse * (d_scaled - middle - scaled * along)).astype(BF16)


def norm_back_call(h, g, firsts, seconds, gains, deps=()):
    rows, width = h.shape
    tile = min(128, rows)
    one = rows_of(tile, width)
    return pl.pallas_call(
        waiting(functools.partial(norm_back_kernel, len(firsts)), 3 + len(firsts) + len(seconds), deps),
        grid=(rows // tile,),
        in_specs=[one, one, whole(gains.shape)] + [one] * (len(firsts) + len(seconds)) + anywhere(len(deps)),
        out_specs=[one, whole((8, width))],
        out_shape=[shape_of(rows, width), shape_of(8, width, dtype=F32)],
        compiler_params=params_of(),
        cost_estimate=cost(20 * rows * width, 2 * rows * width * 8),
        name="norm_back",
    )(h, g, gains, *firsts, *seconds, *deps)


def merge_kernel(h_ref, a0_ref, a1_ref, f0_ref, f1_ref, shifts_ref, out_ref, sums_ref):
    @pl.when(pl.program_id(0) == 0)
    def _():
        sums_ref[...] = jnp.zeros_like(sums_ref)

    state = h_ref[...].astype(F32)
    attention = a0_ref[...].astype(F32) + a1_ref[...].astype(F32) + shifts_ref[0:1]
    feedforward = f0_ref[...].astype(F32) + f1_ref[...].astype(F32) + shifts_ref[1:2]
    out_ref[...] = (state + attention + feedforward).astype(BF16)
    for row, term in enumerate((state, attention, feedforward)):
        sums_ref[row : row + 1, :] += jnp.sum(term * term, axis=0, keepdims=True)


def merge_call(h, attn_pair, ffn_pair, shifts, deps=()):
    rows, width = h.shape
    tile = min(128, rows)
    one = rows_of(tile, width)
    return pl.pallas_call(
        waiting(merge_kernel, 6, deps),
        grid=(rows // tile,),
        in_specs=[one] * 5 + [whole(shifts.shape)] + anywhere(len(deps)),
        out_specs=[one, whole((8, width))],
        out_shape=[shape_of(rows, width), shape_of(8, width, dtype=F32)],
        compiler_params=params_of(),
        cost_estimate=cost(10 * rows * width, 2 * rows * width * 6),
        name="merge",
    )(h, *attn_pair, *ffn_pair, shifts, *deps)


def tn(a, b):
    return lax.dot_general(a, b, (((0,), (0,)), ((), ())), preferred_element_type=F32)


def slope_kernel(count, terms, owners_ref, *refs):
    lefts = [jnp.concatenate([ref[...] for ref in refs[t * count : (t + 1) * count]], axis=1) for t in range(terms)]
    rights = refs[terms * count : terms * (count + 1)]
    outs = refs[terms * (count + 1) :]
    share = lefts[0].shape[1] // count
    total = sum(tn(left, right[...]) for left, right in zip(lefts, rights)).astype(BF16)
    first = pl.program_id(0) < pl.num_programs(0) // 2
    for ref, here in zip(outs, (first, jnp.logical_not(first))):

        @pl.when(here)
        def _():
            for index in range(count):
                ref[index] = total[index * share : (index + 1) * share]


def slope_call(owners, terms, name, cut=(0, 1), deps=()):
    total = owners.shape[0]
    share = terms[0][0].shape[1] // total
    columns = terms[0][1].shape[1] // cut[1]
    count = 4
    if share % 128 or total % (2 * count):
        pieces = 0.0
        row = 0
        for left, right, _ in terms:
            left_ordered = jnp.take(left.reshape(left.shape[0], total, share), owners, axis=1).reshape(left.shape)
            part = right[row : row + left.shape[0], cut[0] * columns : (cut[0] + 1) * columns]
            row += left.shape[0]
            pieces = pieces + tn(left_ordered, part)
        pieces = pieces.astype(BF16).reshape(total, share, columns)
        return pieces[: total // 2], pieces[total // 2 :]
    steps = total // count
    ins, specs = [], []
    for left, _, _ in terms:
        for index in range(count):
            ins.append(left)
            specs.append(
                pl.BlockSpec((left.shape[0], share), functools.partial(lambda i, r, o: (0, o[count * r + i]), index))
            )
    for left, right, row in terms:
        ins.append(right)
        specs.append(
            pl.BlockSpec((left.shape[0], columns), functools.partial(lambda i, r, o: (i, cut[0]), row))
        )
    return pl.pallas_call(
        waiting(functools.partial(slope_kernel, count, len(terms)), 1 + len(ins), deps),
        grid_spec=pltpu.PrefetchScalarGridSpec(
            num_scalar_prefetch=1,
            grid=(steps,),
            in_specs=specs + anywhere(len(deps)),
            out_specs=halves_of(count, steps // 2, share, columns),
        ),
        out_shape=[shape_of(total // 2, share, columns)] * 2,
        compiler_params=params_of(),
        cost_estimate=cost(
            sum(2 * a.size * columns for a, _, _ in terms),
            sum(2 * (a.size + a.shape[0] * columns) for a, _, _ in terms) + 2 * total * share * columns,
        ),
        name=name,
    )(owners, *ins, *deps)


class Sums:
    def __init__(self, masks, slots, send, receive, remote, totals):
        self.masks, self.slots, self.send, self.receive = masks, slots, send, receive
        self.remote, self.totals = remote, totals
        self.steps = [0] * len(masks)
        self.running = [None] * len(masks)
        self.kept = [None] * len(masks)
        self.first = [sum(len(m) for m in masks[:c]) for c in range(len(masks))]

    def launch(self, c, kept, sent):
        step = self.steps[c]
        number = self.first[c] + step
        self.kept[c] = kept
        self.running[c] = self.remote(
            sent, self.slots[c][step], self.send.at[number], self.receive.at[number], self.masks[c][step]
        )

    def halve(self, c, pieces, count):
        self.launch(c, pieces, pieces.at[pl.ds(count // 2, count // 2)])

    def go_on(self, c):
        self.running[c].wait_recv()
        slot = self.slots[c][self.steps[c]]
        count = slot.shape[0]
        total = self.kept[c][:count].astype(F32) + slot[...].astype(F32)
        self.steps[c] += 1
        if self.steps[c] == len(self.masks[c]):
            self.totals[c](total[0])
            return
        self.kept[c][:count] = total.astype(BF16)
        self.halve(c, self.kept[c], count)


def ffn_slopes_kernel(late, early, *refs):
    refs = list(refs)
    take = lambda count: [refs.pop(0) for _ in range(count)]
    sources, outs, (sums_ref,) = take(8), take(8), take(1)
    held = take(8)
    g0, g1, active, mixture, down, slope, up, second = held
    d, o, u, hidden, second0, second1, d_z, o_y = take(8)
    load, store, side_s, side_r = refs
    me = lax.axis_index("ctx")
    rows, width = g0.shape
    units = up.shape[1]
    size = 1 << len(late)
    half, quarter = size // 2, size // 4
    share = width // size
    count = 4
    traffic = Traffic()
    loads = [pltpu.make_async_copy(a, b, load.at[n]) for n, (a, b) in enumerate(zip(sources, held))]
    for copy in loads:
        copy.start()
    chip, plane = {"ctx": exchanged(me, late[0])}, {"ctx": exchanged(me, early[0])}
    greet([chip, plane])

    def pieces(left, right, target, cut, masks):
        owners = mask_order(masks)
        for start in range(0, size, count):
            spots = [pl.ds(pl.multiple_of(exchanged(me, m) * share, share), share) for m in owners[start : start + count]]
            total = tn(jnp.concatenate([left(spot) for spot in spots], axis=1), right).astype(BF16)
            for index in range(count):
                target[start + index, :, cut] = total[index * share : (index + 1) * share]

    def of_g(spot):
        return jnp.concatenate([g0[:, spot], g1[:, spot]], axis=0)

    def back(part, ref, target):
        upstream = ref[...]
        mine = slice(part * rows, (part + 1) * rows)
        total = None
        for start in range(0, units, 512):
            cut = slice(start, start + 512)
            d_hidden = (dot_nt(upstream, down[cut, :]) * slope[mine, cut].astype(F32)).astype(BF16)
            hidden[mine, cut] = d_hidden
            short = jnp.sum(d_hidden.astype(F32), axis=0, keepdims=True)
            sums_ref[:, cut] = short if part == 0 else sums_ref[:, cut] + short
            term = dot_nt(d_hidden, up[:, cut])
            total = term if total is None else total + term
        target[...] = total.astype(BF16)

    for n in (0, 1, 2):
        loads[n].wait()
    cuts = [slice(0, units // 2), slice(units // 2, units)]
    on_the_way = []
    for n, cut in enumerate(cuts):
        pieces(of_g, active[:, cut], d, cut, early)
        on_the_way.append(
            traffic.send(
                d.at[pl.ds(half, half), :, cut], d_z.at[:, :, cut], side_s.at[n], side_r.at[n], plane
            )
        )
    for n in range(3, 8):
        loads[n].wait()
    pieces(of_g, mixture[...], o, slice(0, mixture.shape[1]), late)
    side = traffic.send(o.at[pl.ds(half, half)], o_y, side_s.at[2], side_r.at[2], chip)
    back(0, g0, second0)
    back(1, g1, second1)
    side.wait_recv()
    for index in range(half):
        o[index] = (o[index].astype(F32) + o_y[index].astype(F32)).astype(BF16)
    for cut in cuts:
        pieces(lambda spot: second[:, spot], hidden[:, cut], u, cut, late)
    stores = [o.at[pl.ds(0, quarter)], o.at[pl.ds(quarter, quarter)], u.at[pl.ds(0, half)], u.at[pl.ds(half, half)]]
    stores += [second0, second1]
    copies = [pltpu.make_async_copy(a, b, store.at[n]) for n, (a, b) in enumerate(zip(stores, outs))]
    for copy in copies:
        copy.start()
    for copy, cut in zip(on_the_way, cuts):
        copy.wait_recv()
        for index in range(half):
            d[index, :, cut] = (d[index, :, cut].astype(F32) + d_z[index, :, cut].astype(F32)).astype(BF16)
    stores = [d.at[pl.ds(0, quarter)], d.at[pl.ds(quarter, quarter)]]
    more = [pltpu.make_async_copy(a, b, store.at[6 + n]) for n, (a, b) in enumerate(zip(stores, outs[6:]))]
    for copy in more:
        copy.start()
    traffic.finish()
    for copy in copies + more:
        copy.wait()


def ffn_slopes_call(g_pair, active, mixture, w_down, slope, w_up, second_in, late, early, number):
    ins = (*g_pair, active, mixture, w_down, slope, w_up, second_in)
    rows, width = g_pair[0].shape
    units, local = w_up.shape[1], mixture.shape[1]
    size = 1 << len(late)
    half, quarter, share = size // 2, size // 4, width // size
    part = (rows, width)
    out = [(quarter, share, local)] * 2 + [(half, share, units)] * 2 + [part] * 2 + [(quarter, share, units)] * 2
    scratch = [x.shape for x in ins] + [(size, share, units), (size, share, local), (size, share, units)]
    scratch += [(2 * rows, units), part, part, (half, share, units), (half, share, local)]
    return pl.pallas_call(
        functools.partial(ffn_slopes_kernel, late, early),
        grid=(1,),
        in_specs=anywhere(len(ins)),
        out_specs=anywhere(len(out)) + [whole((1, units))],
        out_shape=[shape_of(*x) for x in out] + [shape_of(1, units, dtype=F32)],
        scratch_shapes=[pltpu.VMEM(x, BF16) for x in scratch]
        + [pltpu.SemaphoreType.DMA((8,)), pltpu.SemaphoreType.DMA((8,))]
        + carrier_semaphores(3),
        compiler_params=params_of(collective_id=number, has_side_effects=True),
        name="ffn_slopes",
    )(*ins)


def hand_back_kernel(seqs, *refs):
    refs = list(refs)
    take = lambda count: [refs.pop(0) for _ in range(count)]
    gains_ref, shifts_ref = take(2)
    sources = take(12)
    a1_in, f1_in = take(2)
    g0_out, g1_out, home_ref, moments_ref = take(4)
    targets = take(12)
    dk, dv, w, dq, g1, g0, down, up, slope, a0, f0, h = targets
    far1, far1_got, sums, arrived, near0, near1, near1_got = take(7)
    second0, second1, second1_got, d_own, got, fresh, fresh_other, a_got, f_got, result = take(10)
    load, side_s, side_r, chip_s, chip_r, core_s, core_r, twin_s, twin_r, new_s, new_r, home_s, home_r, swap_s, swap_r = refs
    me, core, section = lax.axis_index("ctx"), lax.axis_index("tp"), lax.axis_index("section")
    rows, width = far1.shape
    block = rows // seqs
    chips = 2
    seq = me // chips
    chip_rows = 2 * rows
    other_core, other_chip, twin = {"tp": 1 - core}, {"ctx": exchanged(me, 1)}, {"section": 1 - section}
    planes = [{"ctx": exchanged(me, c * chips)} for c in range(1, seqs)]
    traffic = Traffic()

    def at(c):
        return pl.ds(c * block, block)

    def span(c):
        return slice(c * block, (c + 1) * block)

    loads = [pltpu.make_async_copy(a, b, load.at[n]) for n, (a, b) in enumerate(zip(sources, targets))]
    for copy in loads:
        copy.start()
    greet([other_core, other_chip, twin] + planes)
    out_swaps = [
        traffic.send(a1_in, a_got, side_s.at[0], side_r.at[0], other_core),
        traffic.send(f1_in, f_got, side_s.at[1], side_r.at[1], other_core),
    ]
    for n in (0, 1, 2):
        loads[n].wait()

    def from_far(start):
        cut = slice(start, start + rows)
        return dot_nt(dk[cut], w[1]) + dot_nt(dv[cut], w[2])

    far1[...] = from_far(chip_rows + rows).astype(BF16)
    swap = traffic.send(far1, far1_got, side_s.at[2], side_r.at[2], other_core)
    mine = from_far(chip_rows)
    swap.wait_recv()
    sums[...] = (mine + far1_got[...].astype(F32)).astype(BF16)
    arrivals = [
        traffic.send(sums.at[at(c)], arrived.at[at(c)], chip_s.at[c], chip_r.at[c], other_chip) for c in range(seqs)
    ]
    for n in range(3, 12):
        loads[n].wait()

    def from_near(cut):
        return sum(dot_nt(grad[cut], w[t]) for t, grad in enumerate((dq, dk, dv)))

    near1[...] = from_near(slice(rows, chip_rows)).astype(BF16)
    near_swap = traffic.send(near1, near1_got, side_s.at[3], side_r.at[3], other_core)
    near0[...] = from_near(slice(0, rows)).astype(BF16)
    for copy in out_swaps:
        copy.wait_recv()
    moments_ref[...] = jnp.zeros_like(moments_ref)
    home = []
    for c in range(seqs):
        cut = span(c)
        state = h[cut].astype(F32)
        attention = a0[cut].astype(F32) + a_got[cut].astype(F32) + shifts_ref[0:1]
        feedforward = f0[cut].astype(F32) + f_got[cut].astype(F32) + shifts_ref[1:2]
        result[cut] = (state + attention + feedforward).astype(BF16)
        for row, term in enumerate((state, attention, feedforward)):
            moments_ref[row : row + 1, :] += jnp.sum(term * term, axis=0, keepdims=True)
        place = home_ref.at[seq, core]
        if c == 0:
            stay = pltpu.make_async_copy(result.at[at(0)], place, load.at[12])
            stay.start()
        else:
            home.append(traffic.send(result.at[at(c)], place, home_s.at[c], home_r.at[c], planes[c - 1]))
    near_swap.wait_recv()
    handed = []
    for c in range(seqs):
        cut = span(c)
        upstream = jnp.concatenate([g0[cut], g1[cut]], 0)
        slopes = [slice(part * rows + c * block, part * rows + (c + 1) * block) for part in range(2)]
        total = None
        for start in range(0, up.shape[1], 512):
            unit = slice(start, start + 512)
            d_active = dot_nt(upstream, down[unit, :])
            bend = jnp.concatenate([slope[rows_cut, unit] for rows_cut in slopes], 0).astype(F32)
            term = dot_nt((d_active * bend).astype(BF16), up[:, unit])
            total = term if total is None else total + term
        second1[cut] = total[block:].astype(BF16)
        swap = traffic.send(second1.at[at(c)], second1_got.at[at(c)], core_s.at[c], core_r.at[c], other_core)
        arrivals[c].wait_recv()
        scaled, inverse = normalize(h[cut].astype(F32))
        d_first = near0[cut].astype(F32) + near1_got[cut].astype(F32) + arrived[cut].astype(F32)
        swap.wait_recv()
        d_second = total[:block] + second1_got[cut].astype(F32)
        d_scaled = d_first * gains_ref[0:1] + d_second * gains_ref[1:2]
        middle = jnp.mean(d_scaled, axis=-1, keepdims=True)
        along = jnp.mean(d_scaled * scaled, axis=-1, keepdims=True)
        d_own[cut] = (g0[cut].astype(F32) + inverse * (d_scaled - middle - scaled * along)).astype(BF16)
        handed.append(traffic.send(d_own.at[at(c)], got.at[at(c)], twin_s.at[c], twin_r.at[c], twin))
    stay.wait()
    swaps = []
    for s in range(seqs):
        if s:
            home[s - 1].wait_recv()
        place = home_ref.at[exchanged(seq, s), core]
        swaps.append(traffic.send(place, place, swap_s.at[s], swap_r.at[s], other_core))
    news = []
    for c in range(seqs):
        handed[c].wait_recv()
        cut = span(c)
        fresh[cut] = jnp.where(section == 1, g0[cut], got[cut])
        news.append(traffic.send(fresh.at[at(c)], fresh_other.at[at(c)], new_s.at[c], new_r.at[c], other_core))
    first = pltpu.make_async_copy(fresh, g0_out, load.at[0])
    first.start()
    for copy in news:
        copy.wait_recv()
    last = pltpu.make_async_copy(fresh_other, g1_out, load.at[1])
    last.start()
    for copy in swaps:
        copy.wait_recv()
    traffic.finish()
    first.wait()
    last.wait()


def hand_back_call(grads, w_joint, h, g_pair, slope, w_up, w_down, gains, shifts, attn, ffn, name, number):
    d_queries, d_keys, d_values = grads
    rows, width = h.shape
    seqs = SEQS
    wide = (rows, width)
    sources = (d_keys, d_values, w_joint, d_queries, g_pair[1], g_pair[0], w_down, w_up, slope, attn[0], ffn[0], h)
    home = (seqs, 2, rows // seqs, width)
    scratch = [x.shape for x in sources] + [wide] * 17
    quads = carrier_semaphores(seqs)
    return pl.pallas_call(
        functools.partial(hand_back_kernel, seqs),
        grid=(1,),
        in_specs=[whole(gains.shape), whole(shifts.shape)] + anywhere(14),
        out_specs=anywhere(3) + [whole((8, width))],
        out_shape=[shape_of(*wide), shape_of(*wide), shape_of(*home), shape_of(8, width, dtype=F32)],
        scratch_shapes=[pltpu.VMEM(x, BF16) for x in scratch] + [pltpu.SemaphoreType.DMA((14,))] + quads * 7,
        compiler_params=params_of(collective_id=number, has_side_effects=True),
        name=name,
    )(gains, shifts, *sources, attn[1], ffn[1])


def tail_kernel(late, early, *refs):
    (dq_in, dk_in, dv_in, w_in, near_in, far_in, h_in, g_in, second0_in, second1_in, gains_ref, words_in, o0_in, o1_in,
     u0_in, u1_in, d0_in, d1_in) = refs[:18]
    o_out, joint_out, down_out, up_out, home_ref, words_out = refs[18:24]
    (dq, dk, dv, w, near, far, h, g, second0, second1, o0, u0, u1, d0, d1, jq, jk, jv,
     far1, far1_got, sums, arrived, near0, near1, near1_got, d_own, words, other_words) = refs[24:52]
    slots = refs[52:66]
    load, chain_send, chain_receive, side_send, side_receive, word_send, word_receive, part_send, part_receive = refs[66:]
    me, core = lax.axis_index("ctx"), lax.axis_index("tp")
    size = words.shape[0]
    rows, width = h.shape
    seqs, _, block, _ = home_ref.shape
    chips = size // seqs
    seq = me // chips
    chip_rows = 2 * rows
    other_core = {"tp": 1 - core}
    started = []

    def at_ctx(mask):
        return {"ctx": exchanged(me, mask)}

    def send(source, target, first, second, device):
        copy = pltpu.make_async_remote_copy(
            source, target, first, second, device_id=device, device_id_type=pl.DeviceIdType.MESH
        )
        copy.start()
        started.append(copy)
        return copy

    def to_core(source, target, number):
        return send(source, target, side_send.at[number], side_receive.at[number], other_core)

    loads = {}

    def start_loads(first, items):
        for number, (name, source, target) in enumerate(items):
            loads[name] = pltpu.make_async_copy(source, target, load.at[first + number])
            loads[name].start()

    upper, lower = pl.ds(chip_rows, chip_rows), pl.ds(0, chip_rows)
    start_loads(0, (("dk", dk_in.at[upper], dk.at[upper]), ("dv", dv_in.at[upper], dv.at[upper]), ("w", w_in, w)))
    barrier = pltpu.get_barrier_semaphore()
    for mask in range(1, size):
        pl.semaphore_signal(barrier, inc=1, device_id=at_ctx(mask), device_id_type=pl.DeviceIdType.MESH)
    pl.semaphore_signal(barrier, inc=1, device_id=other_core, device_id_type=pl.DeviceIdType.MESH)
    pl.semaphore_wait(barrier, size)

    for name in ("dk", "dv", "w"):
        loads[name].wait()
    start_loads(
        3,
        (
            ("u0", u0_in, u0), ("u1", u1_in, u1), ("dq", dq_in, dq), ("dk", dk_in.at[lower], dk.at[lower]),
            ("dv", dv_in.at[lower], dv.at[lower]), ("h", h_in, h), ("g", g_in, g), ("second0", second0_in, second0),
            ("near", near_in, near), ("far", far_in, far), ("o0", o0_in, o0), ("d0", d0_in, d0), ("d1", d1_in, d1),
        ),
    )
    units = up_out.shape[1]

    def put_output(total):
        o_out[...] = total.T

    def put_down(total):
        down_out[...] = total.T

    def put_joint(t):
        def write(total):
            joint_out[t] = total

        return write

    def put_up(total):
        up_out[...] = total

    chains = [late[1:], late, late, late, late[1:], early[2:]]
    parts, used = [], 0
    for chain in chains:
        parts.append(slots[used : used + len(chain)])
        used += len(chain)
    totals = [put_output, put_joint(0), put_joint(1), put_joint(2), put_up, put_down]
    run = Sums(
        chains, parts, chain_send, chain_receive,
        lambda source, target, first, second, mask: send(source, target, first, second, at_ctx(mask)), totals,
    )
    run.launch(0, o0, o1_in)
    second_swap = to_core(second1_in, second1, 0)

    def ready(c, kept, other, names):
        for name in names:
            loads[name].wait()
        for index in range(kept.shape[0]):
            kept[index] = (kept[index].astype(F32) + other[index].astype(F32)).astype(BF16)
        run.halve(c, kept, kept.shape[0])

    def from_far(start):
        cut = slice(start, start + rows)
        return dot_nt(dk[cut], w[1]) + dot_nt(dv[cut], w[2])

    far1[...] = from_far(chip_rows + rows).astype(BF16)
    swap = to_core(far1, far1_got, 1)
    mine = from_far(chip_rows)
    swap.wait_recv()
    sums[...] = (mine + far1_got[...].astype(F32)).astype(BF16)
    blocks = [*range(seqs // 2, seqs), *range(seqs // 2 - 1, -1, -1)]
    arrivals = {}
    for s in blocks:
        cut = pl.ds(s * block, block)
        arrivals[s] = send(sums.at[cut], arrived.at[cut], part_send.at[s], part_receive.at[s], at_ctx(1))
    ready(4, u0, u1, ("u0", "u1"))
    for name in ("dq", "dk", "dv", "h", "g", "second0"):
        loads[name].wait()
    loads["near"].wait()
    loads["far"].wait()
    loads["o0"].wait()

    def from_near(cut):
        return sum(dot_nt(grad[cut], w[t]) for t, grad in enumerate((dq, dk, dv)))

    near1[...] = from_near(slice(rows, chip_rows)).astype(BF16)
    near_swap = to_core(near1, near1_got, 3)
    near0[...] = from_near(slice(0, rows)).astype(BF16)
    second_swap.wait_recv()
    near_swap.wait_recv()
    gradients = [jnp.zeros((1, width), F32) for _ in range(5)]
    home = {}

    def norm_back(s):
        cut = slice(s * block, (s + 1) * block)
        scaled, inverse = normalize(h[cut].astype(F32))
        upstream = g[cut].astype(F32)
        arrivals[s].wait_recv()
        d_first = near0[cut].astype(F32) + near1_got[cut].astype(F32) + arrived[cut].astype(F32)
        d_second = second0[cut].astype(F32) + second1[cut].astype(F32)
        for row, term in enumerate((d_first * scaled, d_first, d_second * scaled, d_second, upstream)):
            gradients[row] = gradients[row] + jnp.sum(term, axis=0, keepdims=True)
        d_scaled = d_first * gains_ref[0:1] + d_second * gains_ref[1:2]
        middle = jnp.mean(d_scaled, axis=-1, keepdims=True)
        along = jnp.mean(d_scaled * scaled, axis=-1, keepdims=True)
        d_own[cut] = (upstream + inverse * (d_scaled - middle - scaled * along)).astype(BF16)
        source, place = d_own.at[pl.ds(s * block, block)], home_ref.at[seq, core]
        if s == 0:
            home[s] = pltpu.make_async_copy(source, place, load.at[16])
            home[s].start()
        else:
            home[s] = send(source, place, side_send.at[4 + s], side_receive.at[4 + s], at_ctx(s * chips))

    share = width // size
    count = 4
    owners = mask_order(late)

    def joint_slope(t, target, grad):
        for start in range(0, size, count):
            spots = [pl.ds(pl.multiple_of(exchanged(me, m) * share, share), share) for m in owners[start : start + count]]
            total = tn(jnp.concatenate([near[:, spot] for spot in spots], axis=1), grad[:chip_rows])
            if t:
                total = total + tn(jnp.concatenate([far[:, spot] for spot in spots], axis=1), grad[chip_rows:])
            low = total.astype(BF16)
            for index in range(count):
                target[start + index] = low[index * share : (index + 1) * share]
        run.halve(1 + t, target, size)

    joint_slope(0, jq, dq)
    norm_back(blocks[0])
    joint_slope(1, jk, dk)
    norm_back(blocks[1])
    joint_slope(2, jv, dv)
    run.go_on(4)
    run.go_on(0)
    for s in blocks[2:]:
        norm_back(s)
    ready(5, d0, d1, ("d0", "d1"))
    lines = width // 128
    words_out[...] = words_in[...]
    for row in range(5):
        for line in range(lines):
            words_out[row * lines + line : row * lines + line + 1] = gradients[row][:, line * 128 : (line + 1) * 128]
    words[pl.ds(me, 1)] = words_out[...][None]
    word_copies = [
        send(words.at[me], words.at[me], word_send.at[mask], word_receive.at[mask], at_ctx(mask))
        for mask in range(1, size)
    ]
    for c in (0, 1, 4, 1, 2, 2):
        run.go_on(c)
    swaps = []
    for s in range(seqs):
        if s:
            home[s].wait_recv()
        else:
            home[s].wait()
        place = home_ref.at[exchanged(seq, s), core]
        swaps.append(to_core(place, place, 4 + seqs + s))
    run.go_on(3)
    run.go_on(3)
    for copy in word_copies:
        copy.wait_recv()
    total = words[0]
    for index in range(1, size):
        total = total + words[index]
    core_words = other_words.shape[0]
    for copy in word_copies:
        copy.wait_send()
    words_out[...] = total
    swap = to_core(words_out.at[pl.ds(0, core_words)], other_words, 4)
    swap.wait_recv()
    swap.wait_send()
    words_out[pl.ds(0, core_words)] = total[:core_words] + other_words[...]
    for c in (1, 2, 5, 3):
        run.go_on(c)
    for copy in swaps:
        copy.wait_recv()
    for copy in started:
        if copy is not swap and not any(copy is x for x in word_copies):
            copy.wait_send()


def tail_call(grads, w_joint, normals, h, g, seconds, gains, words, core_words, output, up, down, late, early, seqs, number):
    rows, width = h.shape
    chip_rows, local = grads[0].shape
    size = 1 << len(late)
    units = up[0].shape[2]
    share = width // size
    ins = (*grads, w_joint, *normals, h, g, *seconds, gains, words, *output, *up, *down)
    specs = anywhere(len(ins))
    specs[10], specs[11] = whole(gains.shape), whole(words.shape)
    out = [
        shape_of(local, share, dtype=F32),
        shape_of(3, share, local, dtype=F32),
        shape_of(units, share, dtype=F32),
        shape_of(share, units, dtype=F32),
        shape_of(seqs, 2, rows // seqs, width),
        shape_of(*words.shape, dtype=F32),
    ]
    half = size // 2
    wide = (rows, width)
    scratch = [x.shape for x in (*grads, w_joint, *normals)] + [wide] * 4 + [output[0].shape]
    scratch += [x.shape for x in (*up, *down)] + [(size, share, local)] * 3 + [wide] * 8
    scratch = [pltpu.VMEM(shape, BF16) for shape in scratch]
    scratch += [pltpu.VMEM((size, *words.shape), F32), pltpu.VMEM((core_words, 128), F32)]
    for chain, columns, pieces in (
        (late[1:], local, half // 2), (late, local, half), (late, local, half), (late, local, half),
        (late[1:], units, half // 2), (early[2:], units, half // 4),
    ):
        scratch += [pltpu.VMEM((pieces >> step, share, columns), BF16) for step in range(len(chain))]
    scratch += [pltpu.SemaphoreType.DMA((17,))] + carrier_semaphores(14)
    scratch += carrier_semaphores(4 + 2 * seqs) + carrier_semaphores(size) + carrier_semaphores(seqs)
    return pl.pallas_call(
        functools.partial(tail_kernel, late, early),
        grid=(1,),
        in_specs=specs,
        out_specs=[pl.BlockSpec(memory_space=pl.ANY) if n == 4 else whole(x.shape) for n, x in enumerate(out)],
        out_shape=out,
        scratch_shapes=scratch,
        compiler_params=params_of(collective_id=number, has_side_effects=True),
        name="tail",
    )(*ins)


def finish_kernel(chains, events, seqs, chips, core_words, *refs):
    count = len(chains)
    ins, refs = refs[: 2 * count], refs[2 * count :]
    d_own_ref, words_ref = refs[:2]
    totals, home_ref, words_out = refs[2 : 2 + count], refs[2 + count], refs[3 + count]
    refs = list(refs[4 + count :])
    current = [refs.pop(0) for _ in chains]
    slots = [[refs.pop(0) for _ in chain[0]] for chain in chains]
    words, other_words, chain_send, chain_receive, home_send, home_receive, word_send, word_receive, local = refs
    me, core = lax.axis_index("ctx"), lax.axis_index("tp")
    size = words.shape[0]
    seq = me // chips
    block = home_ref.shape[2]

    def at_ctx(mask):
        return {"ctx": exchanged(me, mask)}

    other_core = {"tp": 1 - core}

    def remote(source, target, send, receive, device):
        return pltpu.make_async_remote_copy(
            source, target, send, receive, device_id=device, device_id_type=pl.DeviceIdType.MESH
        )

    barrier = pltpu.get_barrier_semaphore()
    for mask in range(1, size):
        pl.semaphore_signal(barrier, inc=1, device_id=at_ctx(mask), device_id_type=pl.DeviceIdType.MESH)
    pl.semaphore_signal(barrier, inc=1, device_id=other_core, device_id_type=pl.DeviceIdType.MESH)
    pl.semaphore_wait(barrier, size)

    started = []

    def begin(copy):
        copy.start()
        started.append(copy)
        return copy

    word_copies = [
        begin(remote(words_ref, words.at[me], word_send.at[mask], word_receive.at[mask], at_ctx(mask)))
        for mask in range(1, size)
    ]
    steps = [0] * count
    running = [None] * count
    number = [sum(len(chain[0]) for chain in chains[:c]) for c in range(count)]

    def launch(c, source):
        masks = chains[c][0]
        step = steps[c]
        n = number[c] + step
        running[c] = begin(
            remote(source, slots[c][step], chain_send.at[n], chain_receive.at[n], at_ctx(masks[step]))
        )

    def split(c):
        pieces = current[c].shape[0] >> (steps[c] + (0 if chains[c][1] else -1))
        launch(c, current[c].at[pl.ds(pieces // 2, pieces // 2)])

    home = []

    def send_home():
        copy = pltpu.make_async_copy(d_own_ref.at[pl.ds(0, block)], home_ref.at[seq, core], local)
        copy.start()
        for s in range(1, seqs):
            home.append(
                begin(
                    remote(
                        d_own_ref.at[pl.ds(s * block, block)], home_ref.at[seq, core],
                        home_send.at[s], home_receive.at[s], at_ctx(s * chips),
                    )
                )
            )
        copy.wait()

    def go_on(c):
        masks, ready = chains[c][:2]
        running[c].wait_recv()
        slot = slots[c][steps[c]]
        pieces = slot.shape[0]
        kept = ins[2 * c] if steps[c] == 0 and not ready else current[c]
        total = kept[:pieces].astype(F32) + slot[...].astype(F32)
        steps[c] += 1
        if steps[c] == len(masks):
            totals[c][...] = total[0]
            return
        current[c][:pieces] = total.astype(BF16)
        split(c)

    for c, (masks, ready, _) in enumerate(chains):
        if not ready:
            launch(c, ins[2 * c + 1])
    for c, (masks, ready, _) in enumerate(chains):
        if ready:
            current[c][...] = (ins[2 * c][...].astype(F32) + ins[2 * c + 1][...].astype(F32)).astype(BF16)
            split(c)
    send_home()
    words[pl.ds(me, 1)] = words_ref[...][None]
    for c in events:
        go_on(c)
    for copy in home:
        copy.wait_recv()
    swaps = []
    for s in range(seqs):
        place = home_ref.at[exchanged(seq, s), core]
        swaps.append(begin(remote(place, place, home_send.at[seqs + s], home_receive.at[seqs + s], other_core)))
    for copy in word_copies:
        copy.wait_recv()
    total = words[0]
    for index in range(1, size):
        total = total + words[index]
    words_out[...] = total
    swap = remote(words_out.at[pl.ds(0, core_words)], other_words, word_send.at[0], word_receive.at[0], other_core)
    swap.start()
    swap.wait()
    words_out[pl.ds(0, core_words)] = total[:core_words] + other_words[...]
    for copy in swaps:
        copy.wait_recv()
    for copy in started:
        copy.wait_send()


def finish_call(chains, events, d_own, words, core_words, seqs, chips, number):
    size = chips * seqs
    rows, width = d_own.shape
    block = rows // seqs
    ins, specs, out, scratch, slots = [], [], [], [], []
    for masks, ready, (kept, other) in chains:
        pieces, share, columns = kept.shape
        ins += [kept, other]
        specs += [whole(kept.shape), whole(other.shape) if ready else anywhere(1)[0]]
        out.append(shape_of(share, columns, dtype=F32))
        scratch.append(pltpu.VMEM((pieces, share, columns), BF16))
        slots += [
            pltpu.VMEM((pieces >> (step + 1 if ready else step), share, columns), BF16) for step in range(len(masks))
        ]
    copies = len(slots)
    scratch += slots + [pltpu.VMEM((size, *words.shape), F32), pltpu.VMEM((core_words, 128), F32)]
    scratch += carrier_semaphores(copies) + carrier_semaphores(2 * seqs) + carrier_semaphores(size)
    scratch += [pltpu.SemaphoreType.DMA]
    home = shape_of(seqs, 2, block, width)
    out_specs = [whole(x.shape) for x in out] + anywhere(1) + [whole(words.shape)]
    return pl.pallas_call(
        functools.partial(finish_kernel, [(m, r, None) for m, r, _ in chains], events, seqs, chips, core_words),
        grid=(1,),
        in_specs=specs + anywhere(1) + [whole(words.shape)],
        out_specs=out_specs,
        out_shape=out + [home, shape_of(*words.shape, dtype=F32)],
        scratch_shapes=scratch,
        compiler_params=params_of(collective_id=number, has_side_effects=True),
        name="finish",
    )(*ins, d_own, words)


def swap_core(shard):
    return lax.ppermute(shard, "tp", [(0, 1), (1, 0)])


def swap_ctx(shard, mask):
    return lax.ppermute(shard, "ctx", [(c, c ^ mask) for c in range(lax.axis_size("ctx"))])


def next_section(shard, by):
    size = lax.axis_size("section")
    return lax.ppermute(shard, "section", [(s, s + by) for s in range(size) if 0 <= s + by < size])


def mask_order(masks):
    order = [0]
    for mask in reversed(masks):
        order = order + [value ^ mask for value in order]
    return order


def on_device(
    tokens,
    cotangent,
    block_order,
    first_gain,
    first_bias,
    second_gain,
    second_bias,
    joint_weight,
    joint_bias,
    output_weight,
    output_bias,
    up_weight,
    up_bias,
    down_weight,
    down_bias,
):
    section = lax.axis_index("section")
    sections = lax.axis_size("section")
    ctx = lax.axis_index("ctx")
    ctx_size = lax.axis_size("ctx")
    core = lax.axis_index("tp")
    seqs, local_len, width = tokens.shape
    block = local_len // 2
    chips = ctx_size // seqs
    seq, member = ctx // chips, ctx % chips
    rows = seqs * block
    chip_rows = 2 * rows
    length = chips * chip_rows
    seq_masks = [chips << b for b in range((seqs - 1).bit_length())]
    member_masks = [1 << b for b in range((chips - 1).bit_length())]

    k, u, a = jnp.meshgrid(jnp.arange(chips), jnp.arange(2), jnp.arange(seqs), indexing="ij")
    stored = (2 * ((seq ^ a) * chips + (member ^ k)) + (core ^ u)).reshape(-1)
    places = block_order[stored]
    spots = (places[:, None] * block + jnp.arange(block, dtype=jnp.int32)).reshape(-1)
    exponent = jnp.arange(ROT // 2, dtype=F32) * (2.0 / ROT)
    inverse = jnp.power(jnp.float32(ROTARY_BASE), -exponent)
    turns = spots.astype(F32)[:, None] * inverse[None, :]
    cosine, sine = jnp.cos(turns), jnp.sin(turns)
    rest = jnp.zeros((length, HEAD - ROT), F32)
    table = (
        jnp.tile(jnp.concatenate([cosine, cosine, rest + 1.0], 1), (1, 128 // HEAD)),
        jnp.tile(jnp.concatenate([sine, sine, rest], 1), (1, 128 // HEAD)),
    )

    tile = max(block, 128)
    tile_places = places[: chip_rows // block].reshape(-1, tile // block)
    lowest, highest = jnp.min(tile_places, 1), jnp.max(tile_places, 1)
    limits = jnp.stack([(lowest * block + 1) // KEY_TILE, (highest * block + block - 1) // HALF_TILE + 1], 1)

    gain_one, shift_one, gain_two, shift_two = first_gain, first_bias, second_gain, second_bias
    w_joint, b_joint = joint_weight[0], joint_bias[0]
    w_output, b_output = output_weight[0], output_bias
    w_up, b_up = up_weight[0], up_bias
    w_down, b_down = down_weight[0], down_bias
    gains = jnp.concatenate([gain_one, gain_two], 0)
    norms = jnp.concatenate([gain_one, shift_one, gain_two, shift_two], 0)
    shifts = jnp.concatenate([b_output, b_down], 0)

    def plane_parts(values):
        mine = lax.dynamic_slice_in_dim(values, core * block, block, 1)
        return [lax.dynamic_index_in_dim(mine, seq ^ shift, 0, keepdims=False) for shift in range(seqs)]

    def from_planes(values):
        parts = values.reshape(seqs, block, width)
        return [parts[s] if s == 0 else swap_ctx(parts[s], s * chips) for s in range(seqs)]

    def in_order(parts):
        parts = jnp.stack(parts)
        both = jnp.stack([parts, swap_core(parts)], 1)
        ordered = [
            lax.dynamic_index_in_dim(lax.dynamic_index_in_dim(both, s ^ seq, 0, False), v ^ core, 0, False)
            for s in range(seqs)
            for v in range(2)
        ]
        return jnp.stack(ordered).reshape(1, seqs, local_len, width)

    def paired(parts):
        count = len(parts) // 2
        return tuple(x[0] if count == 1 else jnp.concatenate(x, 0) for x in (parts[:count], parts[count:]))

    def forward(own, save, moves, moved, name, number):
        chip = (own, swap_core(own))
        moves = [("ctx", k) for k in range(1, chips)] + moves
        outs, arrived = front_call(
            chip, norms, w_joint, b_joint, table, w_up, b_up, w_down, save, moves, [own] * (chips - 1) + moved, name, number
        )
        normal, keys, values, queries, ffn0, ffn1, *kept_ffn = outs
        others, arrived = arrived[: chips - 1], arrived[chips - 1 :]
        key_parts, value_parts, normal_parts = [keys], [values], [normal]
        if chips > 1:
            rest = paired([x for other in others for x in (other, swap_core(other))])
            far_normal, far_keys, far_values = joint_call(
                rest, gain_one, shift_one, w_joint, b_joint, table, chip_rows
            )
            key_parts.append(far_keys)
            value_parts.append(far_values)
            normal_parts.append(far_normal)
        attn0, attn1, mixture, lse = attend_call(queries, key_parts, value_parts, places, limits, w_output, block)
        result, moments = merge_call(own, (attn0, swap_core(attn1)), (ffn0, swap_core(ffn1)), shifts)
        return result, moments, (normal_parts, queries, key_parts, value_parts, mixture, lse, *kept_ffn), arrived

    def attention_back(g_pair, kept, deps=()):
        normal_parts, queries, key_parts, value_parts, mixture, lse, second_in, active, slope = kept
        return attend_back_call(
            queries, g_pair, mixture, lse, key_parts, value_parts, places, limits, w_output, table, block, deps
        )

    def far_back(d_keys, d_values, deps=()):
        if chips == 1:
            return []
        far = joint_back_call([d_keys, d_values], chip_rows, length - chip_rows, w_joint, deps)
        if chips > 2:
            far = jnp.concatenate(far, 0).reshape(chips - 1, 2, rows, width)
            far = far[:, 0], far[:, 1]
        sums = (far[0].astype(F32) + swap_core(far[1]).astype(F32)).astype(BF16).reshape(chips - 1, rows, width)
        return [sums[k - 1] for k in range(1, chips)]

    others = [("ctx", k) for k in range(1, chips)]
    planes = [("ctx", s * chips) for s in range(1, seqs)]
    fused = chips == 2 and sections == 2 and seqs == SEQS and block % 128 == 0
    if fused:
        weights = (norms, w_joint, b_joint, table, w_up, b_up, w_down)
        token_rows, *kept, g_rows = gather_call(True, False, *weights, (tokens, cotangent), "gather0", 0)
        attn0, attn1, _, _ = attend_call(
            kept[6], [kept[4], kept[1]], [kept[5], kept[2]], places, limits, w_output, block
        )
        own, *kept = gather_call(
            False, True, *weights, (shifts, attn0, attn1, kept[7], kept[8], token_rows), "gather1", 1
        )
        far_normal, far_keys, far_values, normal, keys, values, queries, ffn0, ffn1, *kept_ffn = kept
        key_parts, value_parts, normal_parts = [keys, far_keys], [values, far_values], [normal, far_normal]
        attn0, attn1, mixture, lse = attend_call(queries, key_parts, value_parts, places, limits, w_output, block)
        kept = (normal_parts, queries, key_parts, value_parts, mixture, lse, *kept_ffn)
        slope = kept_ffn[2]
        g_pair = (g_rows, swap_core(g_rows))
        d_queries, d_keys, d_values, _ = attention_back(g_pair, kept)
        g_own, g_other, home, moments = hand_back_call(
            (d_queries, d_keys, d_values), w_joint, own, g_pair, slope, w_up, w_down, gains, shifts,
            (attn0, attn1), (ffn0, ffn1), "hand_back", 2,
        )
        section_out = home.reshape(1, seqs, local_len, width)
        moments = jnp.sum(moments[:3], axis=1)
        g_pair = (g_own, g_other)
    else:
        token_parts = plane_parts(tokens)
        token_rows = jnp.concatenate([token_parts[0]] + [swap_ctx(token_parts[s], s * chips) for s in range(1, seqs)], 0)
        g_parts = plane_parts(cotangent)
        own = token_rows
        for tick in range(sections):
            first = tick == 0
            result, moments, kept, arrived = forward(
                own, tick == sections - 1, planes if first else [], g_parts[1:] if first else [], "front" + str(tick), tick
            )
            if first:
                g_rows = jnp.concatenate([g_parts[0], *arrived], 0)
            if tick < sections - 1:
                own = jnp.where(section == 0, token_rows, next_section(result, 1))
        out_parts = from_planes(result)
        moments = jnp.sum(moments[:3], axis=1)
        slope = kept[-1]
        g_own = g_rows
        for tick in range(sections - 1):
            g_pair = (g_own, swap_core(g_own))
            d_queries, d_keys, d_values, _ = attention_back(g_pair, kept)
            sums = far_back(d_keys, d_values, tuple(out_parts) if tick == 0 else ())
            near, second, arrivals = rear_call(
                (d_queries, d_keys, d_values), w_joint, g_pair, slope, w_up, w_down, others, sums, "rear" + str(tick), sections + tick
            )
            firsts = [near[0], swap_core(near[1]), *arrivals]
            d_own, _ = norm_back_call(own, g_own, firsts, [second[0], swap_core(second[1])], gains)
            g_own = jnp.where(section == sections - 1, g_rows, next_section(d_own, -1))
        section_out = in_order(out_parts)
        g_pair = (g_own, swap_core(g_own))
    normal_parts, queries, key_parts, value_parts, mixture, lse, second_in, active, slope = kept

    local = w_output.shape[0]
    units = w_up.shape[1]

    def results(section_out, home, small, core_words, joint_total, output_total, up_total, down_total):
        both, ones = small[:core_words].reshape(-1), small[core_words:].reshape(-1)
        norm_total = both[: 5 * width].reshape(5, 1, width)
        root_means = jnp.sqrt(both[5 * width : 5 * width + 3] / (length * seqs * width))
        return (
            section_out,
            home.reshape(1, seqs, local_len, width),
            norm_total[0],
            norm_total[1],
            norm_total[2],
            norm_total[3],
            joint_total[None],
            ones[: 3 * local].reshape(1, 3, local),
            output_total[None],
            norm_total[4],
            up_total[None],
            ones[3 * local : 3 * local + units].reshape(1, units),
            down_total[None],
            norm_total[4],
            root_means[None],
        )

    late = tuple(member_masks + seq_masks)
    early = tuple(seq_masks + member_masks)
    late_owners = jnp.stack([ctx ^ m for m in mask_order(late)]).astype(jnp.int32)
    early_owners = jnp.stack([ctx ^ m for m in mask_order(early)]).astype(jnp.int32)
    share = width // ctx_size
    by_blocks = share % 128 == 0 and chips == 2

    def of_g(right, name, deps=()):
        if by_blocks:
            terms = [(g_pair[0], right, 0), (g_pair[1], right, 1)]
        else:
            terms = [(jnp.concatenate(g_pair, 0), right, 0)]
        return slope_call(late_owners, terms, name, (0, 1), deps)

    def in_words(values):
        values = values.reshape(-1)
        return jnp.pad(values, (0, -values.size % 1024)).reshape(-1, 128)

    if fused:
        *parts, up_sums = ffn_slopes_call(
            g_pair, active, mixture, w_down, slope, w_up, second_in, late, early, 2 * sections
        )
        o_kept, o_sent, u_kept, u_sent, second0, second1, down_kept, down_sent = parts
        up_arrived = swap_ctx(u_sent, late[0])
        down_arrived = swap_ctx(down_sent, early[1])
        *grads, joint_sums = attention_back(g_pair, kept, (u_kept,))
        both = in_words(jnp.concatenate([jnp.zeros((5 * width,), F32), moments]))
        ones = in_words(jnp.concatenate([joint_sums[:3].reshape(-1), up_sums.reshape(-1)]))
        output_total, joint_total, down_total, up_total, home, small = tail_call(
            grads, w_joint, normal_parts, own, g_own, [second0, second1], gains, jnp.concatenate([both, ones], 0),
            both.shape[0], (o_kept, o_sent), (u_kept, up_arrived), (down_kept, down_arrived), late, early, seqs,
            2 * sections + 1,
        )
        return results(section_out, home, small, both.shape[0], joint_total, output_total, up_total, down_total)
    down = of_g(active, "down_slope")
    down_arrived = swap_ctx(down[1], late[0])
    output = of_g(mixture, "output_slope", (down[0],))
    second0, second1, d_hidden, up_sums = ffn_back_call(g_pair, slope, w_up, w_down, (output[0],))
    ups = [slope_call(early_owners, [(second_in, d_hidden, 0)], "up_slope", (0, 2))]
    ups.append(slope_call(early_owners, [(second_in, d_hidden, 0)], "up_slope", (1, 2), (ups[0][0],)))
    ups_arrived = [swap_ctx(part[1], early[0]) for part in ups]
    d_queries, d_keys, d_values, joint_sums = attention_back(g_pair, kept, (ups[1][0], output[0]))
    grads = (d_queries, d_keys, d_values)
    ones = in_words(jnp.concatenate([joint_sums[:3].reshape(-1), up_sums.reshape(-1)]))
    sums = far_back(d_keys, d_values, (down_arrived, *ups_arrived))

    def halved(pair, arrived):
        total = (pair[0].astype(F32) + arrived.astype(F32)).astype(BF16)
        return total[: total.shape[0] // 2], total[total.shape[0] // 2 :]

    down = halved(down, down_arrived)
    ups[0] = halved(ups[0], ups_arrived[0])
    near = joint_back_call(grads, 0, chip_rows, w_joint)
    down_arrived, ups_arrived[0] = swap_ctx(down[1], late[1]), swap_ctx(ups[0][1], early[1])
    arrivals = [swap_ctx(part, k + 1) for k, part in enumerate(sums)]
    joints = [slope_call(late_owners, [(normal_parts[0], d_queries, 0)], "query_slope")]
    for grad in grads[1:]:
        joints.append(slope_call(late_owners, [(part, grad, n) for n, part in enumerate(normal_parts)], "key_slope"))
    firsts = [near[0], swap_core(near[1]), *arrivals]
    d_own, norm_sums = norm_back_call(own, g_own, firsts, [second0, swap_core(second1)], gains)
    both = in_words(jnp.concatenate([norm_sums[:5].reshape(-1), moments]))
    chains = [
        (late, False, output),
        (late, False, joints[0]),
        (late, False, joints[1]),
        (late, False, joints[2]),
        (early[1:], True, (ups[1][0], ups_arrived[1])),
        (late[2:], True, (down[0], down_arrived)),
        (early[2:], True, (ups[0][0], ups_arrived[0])),
    ]
    events = [c for step in range(len(late)) for c, chain in enumerate(chains) if step < len(chain[0])]
    output_total, *joint_total, up_right, down_total, up_left, home, small = finish_call(
        chains, events, d_own, jnp.concatenate([both, ones], 0), both.shape[0], seqs, chips, 2 * sections + 1
    )
    joint_total = jnp.stack(joint_total)
    up_total = jnp.concatenate([up_left, up_right], 1)
    output_total, down_total = output_total.T, down_total.T
    return results(section_out, home, small, both.shape[0], joint_total, output_total, up_total, down_total)


def solution(mesh):
    in_specs = (
        P(None, "ctx", None),
        P(None, "ctx", None),
        P(),
        P("section", None),
        P("section", None),
        P("section", None),
        P("section", None),
        P("section", None, None, "tp"),
        P("section", None, "tp"),
        P("section", "tp", None),
        P("section", None),
        P("section", None, "tp"),
        P("section", "tp"),
        P("section", "tp", None),
        P("section", None),
    )
    out_specs = (
        P("section", None, "ctx", None),
        P("section", None, "ctx", None),
        P("section", None),
        P("section", None),
        P("section", None),
        P("section", None),
        P("section", None, "ctx", "tp"),
        P("section", None, "tp"),
        P("section", "tp", "ctx"),
        P("section", None),
        P("section", "ctx", "tp"),
        P("section", "tp"),
        P("section", "tp", "ctx"),
        P("section", None),
        P("section", None),
    )
    return jax.shard_map(
        on_device, mesh=mesh, in_specs=in_specs, out_specs=out_specs, check_vma=False
    )
```
